32 devices in a mesh: section: 2 (over x), dp: 8 (over z, y), expert: 2 (over core).
Axes of the slice: x: 2, y: 2, z: 4, core: 2. Of those that a mesh axis runs over, the one named last changes fastest.
Arguments:
- tokens: bfloat16 [2, 2048, 1152], P(None, ('dp', 'expert')), may hold values from -6 to 6
- cotangent: bfloat16 [2, 2048, 1152], P(None, ('dp', 'expert')), may hold values from -6 to 6
- routes: int32 [2, 2, 2048], P('section', None, ('dp', 'expert')), may hold values from 0 to 7, as said below
- slots: int32 [2, 2, 2048], P('section', None, ('dp', 'expert')), may hold values from 0 to 11, as said below
- drops: int32 [2, 2, 2048], P('section', None, ('dp', 'expert')), may hold values from 0 to 1, as said below
- norm_gain: float32 [2, 1152], P('section', 'dp'), may hold values from 0.5 to 1.5
- w_in: float32 [2, 1152, 2, 2304], P('section', None, None, ('dp', 'expert')), may hold values from -0.1875 to 0.1875
- conv_w: float32 [2, 4, 2304], P('section', None, ('dp', 'expert')), may hold values from -3 to 3
- conv_b: float32 [2, 2304], P('section', ('dp', 'expert')), may hold values from -3 to 3
- x_proj: float32 [2, 2304, 104], P('section', ('dp', 'expert')), may hold values from -0.125 to 0.125
- dt_proj: float32 [2, 72, 2304], P('section', None, ('dp', 'expert')), may hold values from -0.75 to 0.75
- dt_bias: float32 [2, 2304], P('section', ('dp', 'expert')), may hold values from -6 to -1
- a_log: float32 [2, 16, 2304], P('section', None, ('dp', 'expert')), may hold values from -5 to 1
- skip: float32 [2, 2304], P('section', ('dp', 'expert')), may hold values from 0.5 to 1.5
- w_out: float32 [2, 2304, 1152], P('section', ('dp', 'expert')), may hold values from -0.375 to 0.375
- moe_gain: float32 [2, 1152], P('section', 'dp'), may hold values from 0.5 to 1.5
- router: float32 [2, 1152, 8], P('section', 'dp'), may hold values from -0.09375 to 0.09375
- w_up: float32 [2, 8, 1152, 3072], P('section', 'expert', 'dp'), may hold values from -0.1875 to 0.1875
- w_down: float32 [2, 8, 3072, 1152], P('section', 'expert', 'dp'), may hold values from -0.875 to 0.875
Outputs:
- segment_outputs: bfloat16 [2, 2, 2048, 1152], P('section', None, ('dp', 'expert'))
- input_grads: bfloat16 [2, 2, 2048, 1152], P('section', None, ('dp', 'expert'))
- norm_gain_grad: float32 [2, 1152], P('section', 'dp')
- w_in_grad: float32 [2, 1152, 2, 2304], P('section', None, None, ('dp', 'expert'))
- conv_w_grad: float32 [2, 4, 2304], P('section', None, ('dp', 'expert'))
- conv_b_grad: float32 [2, 2304], P('section', ('dp', 'expert'))
- x_proj_grad: float32 [2, 2304, 104], P('section', ('dp', 'expert'))
- dt_proj_grad: float32 [2, 72, 2304], P('section', None, ('dp', 'expert'))
- dt_bias_grad: float32 [2, 2304], P('section', ('dp', 'expert'))
- a_log_grad: float32 [2, 16, 2304], P('section', None, ('dp', 'expert'))
- skip_grad: float32 [2, 2304], P('section', ('dp', 'expert'))
- w_out_grad: float32 [2, 2304, 1152], P('section', ('dp', 'expert'))
- moe_gain_grad: float32 [2, 1152], P('section', 'dp')
- router_grad: float32 [2, 1152, 8], P('section', 'dp')
- w_up_grad: float32 [2, 8, 1152, 3072], P('section', 'expert', 'dp')
- w_down_grad: float32 [2, 8, 3072, 1152], P('section', 'expert', 'dp')
The draws below stay inside these ranges and needn't reach their ends.
Inputs may be any that keep to these rules, and one draw needn't show every extreme that they name: `routes`: each token's one expert. Within each aligned block of 128 tokens, the tokens of one expert that are kept have the distinct slots 0, 1, 2 and so on in token order; dropped tokens have slot 0. `drops`: 1 exactly for the tokens of an aligned block of 128 tokens that come after the first 12 tokens of their expert in that block.
All inputs are finite; a program needn't handle non-finite values.
Results may differ from the reference program's by a relative error of at most 0.023.
The reference program's roundings to bfloat16 on the way count: a program that leaves them out, or rounds other values in their place, can miss the bound.
Values may be sent and summed in bfloat16 or wider, within the bound.
A program may use at most 448 MiB of HBM per device.

```python
import math
import jax
import jax.numpy as jnp
from jax import lax

D = 1152
INNER = 2304
STATE = 16
CONV = 4
DT_RANK = 72
EXPERTS = 8
FFN = 3072
BLOCK = 128
MICRO = 2
CAP = 12
SEQ = 2048
XW = 104
N_SECTION = 2


def route_draw(key):
    blocks = SEQ // BLOCK
    shape = (N_SECTION, MICRO, blocks, BLOCK)
    keys = jax.random.split(jax.random.fold_in(key, 101), N_SECTION * MICRO * blocks)
    order = jax.vmap(lambda single: jax.random.permutation(single, BLOCK))(keys).reshape(shape)
    favored = jax.random.randint(jax.random.fold_in(key, 102), (N_SECTION, MICRO, 1, 1), 0, EXPERTS)
    others = jax.random.randint(jax.random.fold_in(key, 103), shape, 0, EXPERTS - 1)
    others = others + (others >= favored).astype(jnp.int32)
    chosen = jnp.where(order < BLOCK // 2, favored, others).astype(jnp.int32)
    marks = (chosen[..., None] == jnp.arange(EXPERTS, dtype=jnp.int32)).astype(jnp.int32)
    ranks = jnp.sum((jnp.cumsum(marks, axis=3) - 1) * marks, axis=-1)
    dropped = (ranks >= CAP).astype(jnp.int32)
    placed = jnp.where(ranks >= CAP, 0, ranks).astype(jnp.int32)
    flat = (N_SECTION, MICRO, SEQ)
    return (chosen.reshape(flat), placed.reshape(flat), dropped.reshape(flat))


def draw_routes(key, part):
    chosen, placed, dropped = route_draw(key)
    return chosen


def draw_slots(key, part):
    chosen, placed, dropped = route_draw(key)
    return placed


def draw_drops(key, part):
    chosen, placed, dropped = route_draw(key)
    return dropped


def steps_of(rng, extent, cuts, smallest, high):
    factor_of, own = 1.0, jax.random.fold_in(rng, 6)
    for position, blocks in cuts:
        heights = jnp.exp(jax.random.uniform(jax.random.fold_in(own, position), (blocks,), jnp.float32, smallest / len(cuts), high / len(cuts)))
        factor_of = factor_of * jnp.repeat(heights, extent[position] // blocks).reshape([-1 if axis == position else 1 for axis in range(len(extent))])
    return factor_of


def gaussian(rng, extent, scale, limit, shards=(), held_as=jnp.bfloat16):
    values = scale * jax.random.normal(rng, extent, jnp.float32)
    if shards:
        values = values * steps_of(rng, extent, shards, -0.22, 0.18)
    return jnp.clip(values, -limit, limit).astype(held_as)


def setup_inputs(seed: int = 0) -> dict:
    key_of = jax.random.split(jax.random.key(seed), 20)
    tokens = gaussian(key_of[0], (MICRO, SEQ, D), 1.0, 6.0, ((1, 16),))
    cotangent = gaussian(key_of[1], (MICRO, SEQ, D), 1.0, 6.0, ((1, 16),))
    routes = draw_routes(jax.random.fold_in(key_of[19], 71), 0)
    slots = draw_slots(jax.random.fold_in(key_of[19], 71), 0)
    drops = draw_drops(jax.random.fold_in(key_of[19], 71), 0)
    norm_gain = jnp.clip(1.0 + 0.1 * jax.random.normal(key_of[5], (N_SECTION, D), jnp.float32), 0.5, 1.5)
    w_in = gaussian(key_of[6], (N_SECTION, D, 2, INNER), D ** -0.5, 0.1875, ((0, 2), (3, 16)), jnp.float32)
    conv_w = gaussian(key_of[7], (N_SECTION, CONV, INNER), CONV ** -0.5, 3.0, ((0, 2), (2, 16)), jnp.float32)
    conv_b = gaussian(key_of[8], (N_SECTION, INNER), 0.5, 3.0, ((0, 2), (1, 16)), jnp.float32)
    x_proj = gaussian(key_of[9], (N_SECTION, INNER, XW), INNER ** -0.5, 0.125, ((0, 2), (1, 16)), jnp.float32)
    dt_proj = gaussian(key_of[10], (N_SECTION, DT_RANK, INNER), DT_RANK ** -0.5, 0.75, ((0, 2), (2, 16)), jnp.float32)
    dt_bias = jnp.clip(-6.0 + 5.0 * jax.random.uniform(key_of[11], (N_SECTION, INNER), jnp.float32) ** steps_of(key_of[11], (N_SECTION, INNER), ((0, 2), (1, 16)), -0.2, 0.2), -6.0, -1.0)
    a_log = jnp.clip(-5.0 + 6.0 * jax.random.uniform(key_of[12], (N_SECTION, STATE, INNER), jnp.float32) ** steps_of(key_of[12], (N_SECTION, STATE, INNER), ((0, 2), (2, 16)), -0.2, 0.2), -5.0, 1.0)
    skip = jnp.clip(0.5 + 1.0 * jax.random.uniform(key_of[13], (N_SECTION, INNER), jnp.float32) ** steps_of(key_of[13], (N_SECTION, INNER), ((0, 2), (1, 16)), -0.2, 0.2), 0.5, 1.5)
    w_out = gaussian(key_of[14], (N_SECTION, INNER, D), (INNER // 8) ** -0.5, 0.375, ((0, 2), (1, 16)), jnp.float32)
    moe_gain = jnp.clip(1.0 + 0.1 * jax.random.normal(key_of[15], (N_SECTION, D), jnp.float32), 0.5, 1.5)
    router = gaussian(key_of[16], (N_SECTION, D, EXPERTS), (4 * D) ** -0.5, 0.09375, ((0, 2), (1, 8)), jnp.float32)
    w_up = gaussian(key_of[17], (N_SECTION, EXPERTS, D, FFN), D ** -0.5, 0.1875, ((0, 2), (1, 2), (2, 8)), jnp.float32)
    w_down = gaussian(key_of[18], (N_SECTION, EXPERTS, FFN, D), (FFN // 64) ** -0.5, 0.875, ((0, 2), (1, 2), (2, 8)), jnp.float32)
    return {"tokens": tokens, "cotangent": cotangent, "routes": routes, "slots": slots, "drops": drops, "norm_gain": norm_gain, "w_in": w_in, "conv_w": conv_w, "conv_b": conv_b, "x_proj": x_proj, "dt_proj": dt_proj, "dt_bias": dt_bias, "a_log": a_log, "skip": skip, "w_out": w_out, "moe_gain": moe_gain, "router": router, "w_up": w_up, "w_down": w_down}


@jax.custom_vjp
def low(v):
    return lax.optimization_barrier(v.astype(jnp.bfloat16)).astype(jnp.float32)

@jax.custom_vjp
def low_back(v):
    return v

def low_keep(v):
    return (low(v), None)

def low_pass(kept, grad):
    return (grad,)

def back_keep(v):
    return (v, None)

def back_low(kept, grad):
    return (low(grad),)
low.defvjp(low_keep, low_pass)
low_back.defvjp(back_keep, back_low)
epsilon = 1e-05
highest = lax.Precision.HIGHEST

def normalize(values, gain):
    return values * lax.rsqrt(lax.optimization_barrier(jnp.mean(values * values, axis=-1, keepdims=True)) + epsilon) * gain

def compose(early, late):
    return (early[0] * late[0], late[0] * early[1] + late[1])

def selective_scan(step_size, input_map, output_map, signal, rates):
    length, width = step_size.shape
    span = math.gcd(length, 128)
    count = length // span

    def blocked(values):
        return values.reshape((count, span) + values.shape[1:])

    def advance(state, pieces):
        step_blk, in_blk, out_blk, sig_blk = pieces
        decay = jnp.exp(step_blk[:, None, :] * rates[None])
        drive = (step_blk * sig_blk)[:, None, :] * in_blk[:, :, None]
        part_a, part_b = lax.associative_scan(compose, (decay, drive), axis=0)
        states = part_a * state[None] + part_b
        return (states[-1], jnp.einsum('tne,tn->te', states, out_blk, precision=highest))
    start = jnp.zeros((rates.shape[0], width), jnp.float32)
    unused, outputs = lax.scan(jax.checkpoint(advance), start, (blocked(step_size), blocked(input_map), blocked(output_map), blocked(signal)))
    return outputs.reshape(length, width)

def segment_layer(inputs, chosen, placed, dropped, gain_in, w_in, conv_w, conv_b, x_proj, dt_proj, dt_bias, a_log, skip, w_out, gain_moe, router, w_up, w_down):
    normed = low(normalize(inputs, gain_in))
    mixed = low_back(jnp.einsum('ld,dke->lke', normed, w_in, precision=highest))
    conv_in = mixed[:, 0]
    length = conv_in.shape[0]
    taps = conv_w.shape[0]
    padded = jnp.concatenate([jnp.zeros((taps - 1, conv_in.shape[1]), jnp.float32), conv_in], 0)
    summed = conv_b[None] + sum((conv_w[tap] * padded[tap:tap + length] for tap in range(taps)))
    signal = low(jax.nn.silu(summed))
    projected = low_back(jnp.dot(signal, x_proj, precision=highest))
    rank = dt_proj.shape[0]
    states = a_log.shape[0]
    dt_low = low(projected[:, :rank])
    input_map = projected[:, rank:rank + states]
    output_map = projected[:, rank + states:]
    step_size = jax.nn.softplus(low_back(jnp.dot(dt_low, dt_proj, precision=highest)) + dt_bias[None])
    rates = -jnp.exp(a_log)
    scanned = selective_scan(step_size, input_map, output_map, signal, rates)
    gated = low((scanned + skip[None] * signal) * jax.nn.silu(mixed[:, 1]))
    resid = inputs + low_back(jnp.dot(gated, w_out, precision=highest))
    normed_moe = normalize(resid, gain_moe)
    probs = jax.nn.softmax(jnp.dot(normed_moe, router, precision=highest), axis=-1)
    keep = (1 - dropped).astype(jnp.float32)
    pick = (chosen[:, None] == jnp.arange(EXPERTS)[None]).astype(jnp.float32)
    gate = lax.optimization_barrier(jnp.sum(probs * pick, -1)) * keep
    sent = low_back(low(normed_moe))
    flat = chosen * CAP + placed
    table = ((flat[:, None] == jnp.arange(EXPERTS * CAP)[None]) & (dropped[:, None] == 0)).astype(jnp.float32)
    blocks = length // BLOCK
    table = table.reshape(blocks, BLOCK, EXPERTS * CAP)
    buffer = jnp.einsum('bts,btd->sbd', table, sent.reshape(blocks, BLOCK, -1), precision=highest)
    buffer = buffer.reshape(EXPERTS, CAP * blocks, -1)
    hidden_pre = low_back(jnp.einsum('erd,edf->erf', buffer, w_up, precision=highest))
    hidden = low(jax.nn.gelu(hidden_pre))
    produced = low_back(low(jnp.einsum('erf,efd->erd', hidden, w_down, precision=highest)))
    back = jnp.einsum('bts,sbd->btd', table, produced.reshape(EXPERTS * CAP, blocks, -1), precision=highest)
    return resid + gate[:, None] * back.reshape(resid.shape)

def reference(tokens, cotangent, routes, slots, drops, norm_gain, w_in, conv_w, conv_b, x_proj, dt_proj, dt_bias, a_log, skip, w_out, moe_gain, router, w_up, w_down):
    masters = tuple((v.astype(jnp.float32) for v in (norm_gain, w_in, conv_w, conv_b, x_proj, dt_proj, dt_bias, a_log, skip, w_out, moe_gain, router, w_up, w_down)))
    start = tokens.astype(jnp.float32)
    nudges = jnp.zeros((N_SECTION,) + tokens.shape, jnp.float32)
    layer = jax.checkpoint(segment_layer)

    def forward(params, nudge):
        lowered = [low(v) for v in params]
        results = []
        for segment in range(N_SECTION):
            weights = [v[segment] for v in lowered]
            current = []
            for micro in range(MICRO):
                if segment == 0:
                    source = start[micro]
                else:
                    source = results[segment - 1][micro]
                inputs = low_back(source + nudge[segment, micro])
                result = layer(inputs, routes[segment, micro], slots[segment, micro], drops[segment, micro], *weights)
                current.append(low(result))
            results.append(current)
        return jnp.stack([jnp.stack(group) for group in results])
    stacked, pullback = jax.vjp(forward, masters, nudges)
    top_grads = jnp.zeros_like(stacked).at[N_SECTION - 1].set(cotangent.astype(jnp.float32))
    grads, d_nudge = pullback(top_grads)
    return (stacked.astype(jnp.bfloat16), d_nudge.astype(jnp.bfloat16), grads[0], grads[1], grads[2], grads[3], grads[4], grads[5], grads[6], grads[7], grads[8], grads[9], grads[10], grads[11], grads[12], grads[13])
```

```python
import functools

import jax
import jax.numpy as jnp
from jax import lax
from jax.experimental import pallas as pl
from jax.experimental.pallas import tpu as pltpu
from jax.sharding import PartitionSpec as P

EXPERTS = 8
CAP = 12
LANES = 128
CHUNK = 8
HALO = 16
LOG2E = 1.4426950408889634
MESH = pl.DeviceIdType.MESH
MIB = 2**20

epsilon = 1e-05
highest = lax.Precision.HIGHEST
f32 = jnp.float32
bf16 = jnp.bfloat16


def tiles_of(width):
    return [slice(i * LANES, (i + 1) * LANES) for i in range(width // LANES)]


def lanes_at(block, width):
    return pl.ds(pl.multiple_of(block * width, LANES), width)


def scan_final(step_ref, drive_ref, bb_ref, a_ref, state, total, width):
    states = a_ref.shape[0]
    tiles = tiles_of(width)
    each = state.shape[2] // width

    def block(b, unused):
        lanes = lanes_at(b, width)
        rates = [a_ref[:, lanes][:, t] for t in tiles]

        def body(i, carry):
            base = pl.multiple_of(i * CHUNK, CHUNK)
            step = step_ref[pl.ds(base, CHUNK), lanes]
            drive = drive_ref[pl.ds(base, CHUNK), lanes]
            carry, sums = list(carry[0]), carry[1]
            for k in range(CHUNK):
                in_map = bb_ref[base + k]
                for j, t in enumerate(tiles):
                    decay = jnp.exp2(step[k : k + 1, t] * rates[j])
                    carry[j] = decay * carry[j] + drive[k : k + 1, t] * in_map
            return tuple(carry), sums + step

        zeros = tuple(jnp.zeros((states, LANES), f32) for _ in tiles)
        final, sums = lax.fori_loop(
            0, step_ref.shape[0] // CHUNK, body, (zeros, jnp.zeros((CHUNK, width), f32))
        )
        side, at = lax.div(b, each), lanes_at(lax.rem(b, each), width)
        state[side, :, at] = jnp.concatenate(final, 1)
        total[side, :, at] = jnp.sum(sums, 0, keepdims=True)
        return unused

    lax.fori_loop(0, 2 * each, block, 0)


def scan_leak(step_ref, dy_ref, cb_ref, a_ref, state, total, width):
    states = a_ref.shape[0]
    tiles = tiles_of(width)
    each = state.shape[2] // width
    count = step_ref.shape[0] // CHUNK

    def block(b, unused):
        lanes = lanes_at(b, width)
        rates = [a_ref[:, lanes][:, t] for t in tiles]

        def body(i, carry):
            base = pl.multiple_of((count - 1 - i) * CHUNK, CHUNK)
            step = step_ref[pl.ds(base, CHUNK), lanes]
            dys = dy_ref[pl.ds(base, CHUNK), lanes]
            carry, sums = list(carry[0]), carry[1]
            for k in reversed(range(CHUNK)):
                out_map = cb_ref[base + k]
                for j, t in enumerate(tiles):
                    decay = jnp.exp2(step[k : k + 1, t] * rates[j])
                    carry[j] = decay * (carry[j] + dys[k : k + 1, t] * out_map)
            return tuple(carry), sums + step

        zeros = tuple(jnp.zeros((states, LANES), f32) for _ in tiles)
        final, sums = lax.fori_loop(0, count, body, (zeros, jnp.zeros((CHUNK, width), f32)))
        side, at = lax.div(b, each), lanes_at(lax.rem(b, each), width)
        state[side, :, at] = jnp.concatenate(final, 1)
        total[side, :, at] = jnp.sum(sums, 0, keepdims=True)
        return unused

    lax.fori_loop(0, 2 * each, block, 0)


def scan_outputs(step_ref, drive_ref, bb_ref, cb_ref, a_ref, entering, y_ref, starts_ref, width):
    tiles = tiles_of(width)
    each = entering.shape[2] // width

    def block(b, unused):
        lanes = lanes_at(b, width)
        rates = [a_ref[:, lanes][:, t] for t in tiles]

        def body(i, carry):
            base = pl.multiple_of(i * CHUNK, CHUNK)
            step = step_ref[pl.ds(base, CHUNK), lanes]
            drive = drive_ref[pl.ds(base, CHUNK), lanes]
            carry = list(carry)
            starts_ref[i, :, lanes] = jnp.concatenate(carry, 1)
            rows = [[] for _ in tiles]
            for k in range(CHUNK):
                in_map = bb_ref[base + k]
                out_map = cb_ref[base + k]
                for j, t in enumerate(tiles):
                    decay = jnp.exp2(step[k : k + 1, t] * rates[j])
                    carry[j] = decay * carry[j] + drive[k : k + 1, t] * in_map
                    rows[j].append(jnp.sum(carry[j] * out_map, 0, keepdims=True))
            y_ref[pl.ds(base, CHUNK), lanes] = jnp.concatenate(
                [jnp.concatenate(row, 0) for row in rows], 1
            )
            return tuple(carry)

        first = entering[lax.div(b, each), :, lanes_at(lax.rem(b, each), width)]
        lax.fori_loop(0, step_ref.shape[0] // CHUNK, body, tuple(first[:, t] for t in tiles))
        return unused

    lax.fori_loop(0, 2 * each, block, 0)


def scan_back(
    step_ref, drive_ref, dy_ref, bb_ref, cb_ref, a_ref, starts_ref, inflow, through_ref, flow_ref, db_ref,
    dc_ref, da_ref, width,
):
    tiles = tiles_of(width)
    each = inflow.shape[2] // width
    count = step_ref.shape[0] // CHUNK
    db_ref[...] = jnp.zeros_like(db_ref)
    dc_ref[...] = jnp.zeros_like(dc_ref)

    def block(b, unused):
        lanes = lanes_at(b, width)
        rates = [a_ref[:, lanes][:, t] for t in tiles]

        def body(i, carry):
            grads, d_rates = list(carry[0]), list(carry[1])
            chunk = count - 1 - i
            base = pl.multiple_of(chunk * CHUNK, CHUNK)
            step = step_ref[pl.ds(base, CHUNK), lanes]
            drive = drive_ref[pl.ds(base, CHUNK), lanes]
            dys = dy_ref[pl.ds(base, CHUNK), lanes]
            start = starts_ref[chunk, :, lanes]
            d_in, d_out = [None] * CHUNK, [None] * CHUNK
            all_through, all_flows = [], []
            for j, t in enumerate(tiles):
                current = start[:, t]
                decays, states = [], [current]
                for k in range(CHUNK):
                    decay = jnp.exp2(step[k : k + 1, t] * rates[j])
                    current = decay * current + drive[k : k + 1, t] * bb_ref[base + k]
                    decays.append(decay)
                    states.append(current)
                grad = grads[j]
                through, flows = [None] * CHUNK, [None] * CHUNK
                for k in reversed(range(CHUNK)):
                    dy = dys[k : k + 1, t]
                    grad = grad + dy * cb_ref[base + k]
                    through[k] = jnp.sum(grad * bb_ref[base + k], 0, keepdims=True)
                    piece = grad * drive[k : k + 1, t]
                    d_in[k] = piece if d_in[k] is None else d_in[k] + piece
                    piece = dy * states[k + 1]
                    d_out[k] = piece if d_out[k] is None else d_out[k] + piece
                    grad = decays[k] * grad
                    flow = grad * states[k]
                    flows[k] = jnp.sum(flow * rates[j], 0, keepdims=True)
                    d_rates[j] = d_rates[j] + flow * step[k : k + 1, t]
                grads[j] = grad
                all_through.append(jnp.concatenate(through, 0))
                all_flows.append(jnp.concatenate(flows, 0))
            through_ref[pl.ds(base, CHUNK), lanes] = jnp.concatenate(all_through, 1)
            flow_ref[pl.ds(base, CHUNK), lanes] = jnp.concatenate(all_flows, 1)
            for k in range(CHUNK):
                db_ref[base + k] += d_in[k]
                dc_ref[base + k] += d_out[k]
            return tuple(grads), tuple(d_rates)

        first = inflow[lax.div(b, each), :, lanes_at(lax.rem(b, each), width)]
        zeros = tuple(jnp.zeros((a_ref.shape[0], LANES), f32) for _ in tiles)
        d_rates = lax.fori_loop(0, count, body, (tuple(first[:, t] for t in tiles), zeros))[1]
        da_ref[:, lanes] = jnp.concatenate(d_rates, 1)
        return unused

    lax.fori_loop(0, 2 * each, block, 0)


def block_width(width, most):
    while width % most:
        most -= LANES
    return most


def shape_of(*shape, dtype=f32):
    return jax.ShapeDtypeStruct(shape, dtype)


def place_of(index, count):
    return jnp.where(
        lax.rem(index, 2) == 0, lax.div(index, 2), count - 1 - lax.div(index, 2)
    )


def index_at(place, count):
    place = lax.rem(place + 2 * count, count)
    return jnp.where(place < (count + 1) // 2, 2 * place, 2 * (count - 1 - place) + 1)


def greet(devices):
    barrier = pltpu.get_barrier_semaphore()
    for device in devices:
        pl.semaphore_signal(barrier, inc=1, device_id=device, device_id_type=MESH)
    pl.semaphore_wait(barrier, len(devices))


def remote(src, dst, send, recv, device):
    return pltpu.make_async_remote_copy(
        src_ref=src, dst_ref=dst, send_sem=send, recv_sem=recv, device_id=device,
        device_id_type=MESH,
    )


def here(count):
    section, dp, core = (lax.axis_index(name) for name in ("section", "dp", "expert"))
    place = place_of(dp, count)
    right = (section, index_at(place + 1, count), core)
    left = (section, index_at(place - 1, count), core)
    return dp, core, place, right, left, (section, dp, 1 - core)


def dp_peers(count):
    section, dp, core = (lax.axis_index(name) for name in ("section", "dp", "expert"))
    return [(section, lax.rem(dp + by, count), core) for by in range(1, count)]


def comm_params(identity, vmem=48):
    return pltpu.CompilerParams(
        collective_id=identity, has_side_effects=True, vmem_limit_bytes=vmem * MIB
    )


anywhere = pl.BlockSpec(memory_space=pl.ANY)
in_vmem = pl.BlockSpec(memory_space=pltpu.VMEM)
dma = pltpu.SemaphoreType.DMA


def gelu_parts(x):
    scale, cubic = 0.7978845608028654, 0.044715
    square = x * x
    t = jnp.tanh(scale * x * (1.0 + cubic * square))
    act = 0.5 * x * (1.0 + t)
    slope = 0.5 * (1.0 + t) + 0.5 * x * (1.0 - t * t) * scale * (1.0 + 3.0 * cubic * square)
    return act, slope


def own_expert(rows, each_rows, hidden):
    each = each_rows // CAP
    row = lax.broadcasted_iota(jnp.int32, (rows, 1), 0)
    for _ in range(rows // each_rows - 1):
        row = jnp.where(row >= each_rows, row - each_rows, row)
    column = lax.broadcasted_iota(jnp.int32, (1, hidden), 1)
    row_expert, column_expert = jnp.zeros_like(row), jnp.zeros_like(column)
    for e in range(1, each):
        row_expert = row_expert + (row >= e * CAP).astype(jnp.int32)
        column_expert = column_expert + (column >= e * (hidden // each)).astype(jnp.int32)
    return row_expert == column_expert


def mm(a, b, dims):
    return lax.dot_general(a, b, (dims, ((), ())), preferred_element_type=f32)


class Round:
    def __init__(self, count, own, held, work, part, out, scratch):
        self.own, self.held, self.work, self.part, self.out = own, held, work, part, out
        self.slots, (self.total, self.pair_in, self.pair_sems) = scratch[:4], scratch[4:7]
        self.sems, self.back_sems, self.local_sem = scratch[7:9], scratch[9:11], scratch[11]
        self.count, self.reach = count, count // 2
        self.dp, self.core, self.place, right, left, self.partner = here(count)
        self.towards = (right, left)

    def source(self, way, k):
        return index_at(self.place - k if way == 0 else self.place + k, self.count)

    def hop(self, way, k, half, src=None):
        sem = self.sems[way]
        slot = self.held.at[self.source(way, k), self.core if half == 0 else 1 - self.core]
        return remote(
            slot if src is None else src, slot, sem.at[0, k, half], sem.at[1, k, half],
            self.towards[way],
        )

    def first(self, half):
        return self.own.at[self.core] if half == 0 else None

    def swap(self):
        return remote(
            self.own.at[1 - self.core], self.held.at[self.dp, self.core], self.pair_sems.at[0, 0],
            self.pair_sems.at[1, 0], self.partner,
        )

    def keep(self):
        return pltpu.make_async_copy(
            self.own.at[self.core], self.held.at[self.dp, self.core], self.local_sem
        )

    def begin(self):
        self.swap().start()
        self.keep().start()
        for way in range(2):
            if self.reach > 1 or way == 0:
                self.hop(way, 0, 0, self.first(0)).start()

    def begin_other(self):
        self.swap().wait_recv()
        for way in range(2):
            if self.reach > 1 or way == 1:
                self.hop(way, 0, 1).start()
        self.keep().wait()

    def further(self, k):
        for half in range(2):
            for way in range(2):
                self.hop(way, k - 1, half).wait_recv()
                if half == way:
                    self.hop(way, k, half).start()
                else:

                    @pl.when(k < self.reach - 1)
                    def _(way=way, half=half):
                        self.hop(way, k, half).start()

    def arrive(self):
        for way in range(2):
            self.hop(way, self.reach - 1, way).wait_recv()

    def back(self, way, k, half):
        sem = self.back_sems[way]
        return remote(
            self.slots[way].at[k, half], self.slots[way + 2].at[k, half], sem.at[0, k, half],
            sem.at[1, k, half], self.towards[way],
        )

    def begin_back(self):
        for way in range(2):
            self.slots[way + 2][0, 1 - way] = jnp.zeros(self.slots[0].shape[2:], bf16)
            self.slots[way][0, way] = self.part[self.source(way, self.reach), way]
            self.back(way, 0, way).start()

    def nearer(self, k):
        for half in range(2):
            for way in range(2):
                owner = self.source(1 - way, self.reach - k)
                piece = self.part[owner, half].astype(f32)
                if half == way:
                    self.back(way, k - 1, half).wait_recv()
                else:

                    @pl.when(k > 1)
                    def _(way=way, half=half):
                        self.back(way, k - 1, half).wait_recv()

                before = self.slots[way + 2][k - 1, half].astype(f32)
                self.slots[way][k, half] = (piece + before).astype(bf16)
                self.back(way, k, half).start()

    def swap_back(self):
        return remote(
            self.total.at[1 - self.core], self.pair_in, self.pair_sems.at[0, 1], self.pair_sems.at[1, 1],
            self.partner,
        )

    def sum_up(self):
        for half in range(2):
            value = self.part[self.dp, half].astype(f32)
            for way in range(2):
                if self.reach > 1 or half == way:
                    self.back(way, self.reach - 1, half).wait_recv()
                    value = value + self.slots[way + 2][self.reach - 1, half].astype(f32)
            self.total[half] = value.astype(bf16)
        self.swap_back().start()

    def end(self):
        self.out[self.core] = self.total[self.core]
        self.swap_back().wait_recv()
        self.out[1 - self.core] = self.pair_in[...]
        self.swap().wait_send()
        self.swap_back().wait_send()

    def finish(self, k):
        for half in range(2):
            for way in range(2):
                if half == way:
                    self.hop(way, k, half, self.first(half)).wait_send()
                    self.back(way, k, half).wait_send()
                else:

                    @pl.when(k < self.reach - 1)
                    def _(way=way, half=half):
                        self.hop(way, k, half, self.first(half)).wait_send()

                    @pl.when(k > 0)
                    def _(way=way, half=half):
                        self.back(way, k, half).wait_send()


def go_round(rounds):
    reach = rounds[0].reach

    def steps(from_step, step):
        def body(k, unused):
            step(k)
            return unused

        lax.fori_loop(from_step, reach, body, 0)

    for one in rounds:
        one.begin()
    for one in rounds:
        one.begin_other()
    for one in rounds:
        one.work([one.dp])

    def further(k):
        for one in rounds:
            one.further(k)
        for one in rounds:
            one.work([one.source(0, k), one.source(1, k)])

    steps(1, further)
    for one in rounds:
        one.arrive()
        one.work([one.source(0, reach)])
        one.begin_back()

    def nearer(k):
        for one in rounds:
            one.nearer(k)

    steps(1, nearer)
    for one in rounds:
        one.sum_up()
    for one in rounds:
        one.end()

    def finish(k):
        for one in rounds:
            one.finish(k)

    steps(0, finish)


def rows_of(held, sources):
    pieces = [held[s].reshape(-1, held.shape[-1]) for s in sources]
    return pieces[0] if len(pieces) == 1 else jnp.concatenate(pieces, 0)


def put_rows(ref, sources, value):
    size = value.shape[0] // len(sources)
    for i, s in enumerate(sources):
        ref[s] = value[i * size : (i + 1) * size].reshape(ref.shape[1:]).astype(ref.dtype)


def block_at(section, index, count):
    index = lax.rem(index + 2 * count, 2 * count)
    return section, lax.div(index, 2), lax.rem(index, 2)


def experts_kernel(count, ahead, behind, cross, *refs):
    refs = list(refs)

    def take(number):
        taken = refs[:number]
        del refs[:number]
        return taken

    if ahead:
        own, resid, table, gate = take(4)
    if behind:
        below = take(1)[0] if cross else None
        above, table_back, gate_back, arrived_hbm = take(4)
    up_hbm, down_hbm = take(2)
    if ahead:
        out, result = take(2)
        next_rows, next_halo = take(2) if cross else (None, None)
        (arrived_out,) = take(1)
    if behind:
        upstream_out, out_back, given_out, hidden_out, slope_out = take(5)
    up, down, load_sems = take(3)
    section = lax.axis_index("section")
    dp, core, place, right, left, partner = here(count)
    block = 2 * dp + core
    across, before, after = (block_at(1 - section, block + by, count) for by in (0, -1, 1))
    greet([right, left, partner] + [across] * cross + [before] * (cross and ahead))
    loads = [
        pltpu.make_async_copy(up_hbm, up, load_sems.at[0]),
        pltpu.make_async_copy(down_hbm, down, load_sems.at[1]),
    ]
    rounds = []
    if ahead:
        held, part = take(2)
        landed, landed_halo, cross_sems = take(3) if cross else (None, None, None)
        scratch = take(12)
        (save_sem,) = take(1)

        def work(sources):
            pre = mm(rows_of(held, sources), up[...], ((1,), (0,)))
            mask = own_expert(pre.shape[0], held.shape[2], pre.shape[1])
            hidden = jnp.where(mask, gelu_parts(pre)[0], 0.0).astype(bf16)
            put_rows(part, sources, mm(hidden, down[...], ((1,), (0,))))

        rounds.append(Round(count, own, held, work, part, out, scratch))
    if behind:
        own_back, held_back, arrived, hidden_all, slope_all, part_back = take(6)
        landed_back, cross_back = take(2) if cross else (None, None)
        scratch_back = take(12)
        (back_sems,) = take(1)
        loads.append(pltpu.make_async_copy(arrived_hbm, arrived, back_sems.at[0]))

        def work_back(sources):
            pre = mm(rows_of(arrived, sources), up[...], ((1,), (0,)))
            mask = own_expert(pre.shape[0], held_back.shape[2], pre.shape[1])
            act, slope = gelu_parts(pre)
            put_rows(hidden_all, sources, jnp.where(mask, act, 0.0))
            d_hidden = mm(rows_of(held_back, sources), down[...], ((1,), (1,)))
            d_pre = jnp.where(mask, d_hidden * slope, 0.0).astype(bf16)
            put_rows(slope_all, sources, d_pre)
            put_rows(part_back, sources, mm(d_pre, up[...], ((1,), (1,))))

        rounds.append(Round(count, own_back, held_back, work_back, part_back, out_back, scratch_back))
    if behind:
        if cross:
            crossing = remote(below, landed_back, cross_back.at[0], cross_back.at[1], across)
            crossing.start()
    for load in loads:
        load.start()
    if behind:
        upstream = above[...].astype(f32)
        if cross:
            crossing.wait_recv()
            upstream = jnp.where(section == 1, upstream, landed_back[...].astype(f32))
        upstream_out[...] = upstream.astype(bf16)
        slots_grad = mm(table_back[...], (upstream * gate_back[...]).astype(bf16), ((1,), (0,)))
        own_back[...] = slots_grad.astype(bf16).reshape(own_back.shape)
    waiting = list(loads)
    for one in rounds:

        def work_first(sources, work=one.work):
            while waiting:
                waiting.pop().wait()
            work(sources)

        one.work = work_first
    go_round(rounds)
    saves = []
    if ahead:
        saves.append(pltpu.make_async_copy(held, arrived_out, save_sem))
    if behind:
        for n, (src, dst) in enumerate(
            ((held_back, given_out), (hidden_all, hidden_out), (slope_all, slope_out))
        ):
            saves.append(pltpu.make_async_copy(src, dst, back_sems.at[1 + n]))
    for save in saves:
        save.start()
    if ahead:
        returned = out[...].reshape(-1, out.shape[2])
        combined = mm(table[...], returned, ((1,), (0,))) * gate[...]
        result[...] = (resid[...] + combined).astype(bf16)
    if ahead and cross:
        length, halo = result.shape[0], next_halo.shape[0]
        copies = [
            remote(result, landed, cross_sems.at[0, 0], cross_sems.at[1, 0], across),
            remote(
                result.at[length - halo : length], landed_halo, cross_sems.at[0, 1], cross_sems.at[1, 1], after
            ),
        ]
        for copy in copies:
            copy.start()
        for copy in copies:
            copy.wait_recv()
        next_rows[...] = landed[...]
        next_halo[...] = jnp.where(block > 0, landed_halo[...].astype(f32), 0.0).astype(bf16)
        for copy in copies:
            copy.wait_send()
    if behind and cross:
        crossing.wait_send()
    for save in saves:
        save.wait()


def experts(up, down, ahead, behind, cross):
    count = lax.axis_size("dp")
    reach = count // 2
    width = (ahead[1] if ahead else behind[-4]).shape[1]
    length = (ahead[1] if ahead else behind[-4]).shape[0]
    rows = (2, EXPERTS * CAP // 2, width)
    gathered = (count,) + rows
    units = (count, 2 * rows[1], up.shape[1])
    around = (
        [pltpu.VMEM((reach,) + rows, bf16)] * 4
        + [pltpu.VMEM(rows, bf16), pltpu.VMEM(rows[1:], bf16), dma((2, 2))]
        + [dma((2, reach, 2))] * 4
        + [dma(())]
    )
    in_specs, out_specs, shapes, scratch = [], [], [], []
    if ahead:
        landing = [(length, width), (HALO, width)] if cross else []
        in_specs += [in_vmem] * 4
        out_specs += [in_vmem] * (2 + len(landing)) + [anywhere]
        shapes += [rows, (length, width)] + landing + [gathered]
        scratch += [pltpu.VMEM(gathered, bf16)] * 2 + [pltpu.VMEM(shape, bf16) for shape in landing]
        scratch += [dma((2, 2))] * cross + around + [dma(())]
    if behind:
        in_specs += [in_vmem] * (len(behind) - 1) + [anywhere]
        out_specs += [in_vmem] * 2 + [anywhere] * 3
        shapes += [(length, width), rows, gathered, units, units]
        scratch += [pltpu.VMEM(rows, bf16)] + [pltpu.VMEM(gathered, bf16)] * 2
        scratch += [pltpu.VMEM(units, bf16)] * 2 + [pltpu.VMEM(gathered, bf16)]
        scratch += [pltpu.VMEM((length, width), bf16), dma((2,))] if cross else []
        scratch += around + [dma((4,))]
    number = 7 if ahead and behind else 1 if ahead else 2
    number += 0 if cross or number == 7 else 7
    return pl.pallas_call(
        functools.partial(experts_kernel, count, bool(ahead), bool(behind), cross),
        in_specs=in_specs + [anywhere] * 2,
        out_specs=out_specs,
        out_shape=[shape_of(*shape, dtype=bf16) for shape in shapes],
        scratch_shapes=[pltpu.VMEM(up.shape, bf16), pltpu.VMEM(down.shape, bf16), dma((2,))] + scratch,
        compiler_params=comm_params(number, 60),
        name="experts_both" if number == 7 else "experts_forward" if ahead else "experts_backward",
    )(*(ahead or ()), *(behind or ()), up, down)


def grid_here(count):
    section, dp, core = (lax.axis_index(name) for name in ("section", "dp", "expert"))
    a, b = lax.div(dp, 2), lax.rem(dp, 2)
    line = count // 2

    def at(place):
        return section, 2 * lax.rem(place + line, line) + b, core

    return a, b, core, at(a + 1), at(a - 1), (section, 2 * a + 1 - b, core), (section, dp, 1 - core)


def greet_lines(count):
    greet_all(count)


def weights_gather_kernel(count, parts, wide_up, wide_down, *refs):
    own, refs = refs[:parts], refs[parts:]
    (up_out, low_down), out, refs = refs[:2], refs[2 : parts + 2], refs[parts + 2 :]
    buffer_up, buffer_down, rounded_up, rounded_down, load_sems, up_sems = refs[:6]
    after_sems, before_sems, side_sems, pair_sems, local_sems = refs[6:]
    a, b, core, after, before, beside, partner = grid_here(count)
    line = count // 2
    greet_lines(count)

    def slot(p, place, which):
        return out[p].at[core, 2 * place + which]

    def source(p, place, k):
        return own[p] if isinstance(k, int) and k == 0 else slot(p, place, b)

    def along(way, k, p):
        place = a - k if way == 0 else a + k
        sems = after_sems if way == 0 else before_sems
        return remote(
            source(p, place, k), slot(p, place, b), sems.at[0, k, p], sems.at[1, k, p],
            after if way == 0 else before,
        )

    def aside(place, k, p):
        return remote(
            source(p, place, k), slot(p, place, b), side_sems.at[0, place, p], side_sems.at[1, place, p],
            beside,
        )

    def across(place, which, k, p):
        src = source(p, place, k) if which is b else slot(p, place, which)
        number = 2 * place + which
        return remote(
            src, slot(p, place, which), pair_sems.at[0, number, p], pair_sems.at[1, number, p], partner
        )

    def has(way, k):
        return a - k >= 0 if way == 0 else a + k < line

    def goes(way):
        return a + 1 < line if way == 0 else a >= 1

    for p in range(parts):
        aside(a, 0, p).start()
        for way in range(2):

            @pl.when(goes(way))
            def _(way=way, p=p):
                along(way, 0, p).start()

    keeps = [
        pltpu.make_async_copy(own[p], slot(p, a, b), local_sems.at[p]) for p in range(parts)
    ]
    for p in range(parts):
        across(a, b, 0, p).start()
        keeps[p].start()
    loads = [
        pltpu.make_async_copy(wide_up, buffer_up, load_sems.at[0]),
        pltpu.make_async_copy(wide_down, buffer_down, load_sems.at[1]),
    ]
    save = pltpu.make_async_copy(rounded_down, low_down, load_sems.at[2])
    for load in loads:
        load.start()
    loads[0].wait()
    each, depth, hidden = wide_up.shape
    cut = hidden // count
    for piece in range(count):
        for e in range(each):
            rounded_up[piece, :, e * cut : (e + 1) * cut] = buffer_up[
                e, :, piece * cut : (piece + 1) * cut
            ].astype(bf16)
    end = exchange(count, rounded_up, up_out, up_sems, load_sems.at[3])
    loads[1].wait()

    def rounding(e, unused):
        rounded_down[e] = buffer_down[e].astype(bf16)
        return unused

    lax.fori_loop(0, each, rounding, 0)
    save.start()

    def came_aside(place, p):
        aside(place, None, p).wait_recv()
        across(place, 1 - b, None, p).start()

    def arrivals(k, unused):
        for p in range(parts):
            for way in range(2):

                @pl.when(has(way, k))
                def _(way=way, p=p):
                    place = a - k if way == 0 else a + k
                    along(way, k - 1, p).wait_recv()

                    @pl.when(goes(way))
                    def _():
                        along(way, k, p).start()

                    aside(place, None, p).start()
                    across(place, b, None, p).start()

        for p in range(parts):

            @pl.when(k == 1)
            def _(p=p):
                came_aside(a, p)

            for way in range(2):

                @pl.when((k > 1) & has(way, k - 1))
                def _(way=way, p=p):
                    came_aside(a - k + 1 if way == 0 else a + k - 1, p)

        return unused

    lax.fori_loop(1, line, arrivals, 0)
    for p in range(parts):
        if line == 1:
            came_aside(a, p)
        for way in range(2):

            @pl.when((line > 1) & has(way, line - 1))
            def _(way=way, p=p):
                came_aside(a - line + 1 if way == 0 else a + line - 1, p)

    for p in range(parts):
        keeps[p].wait()

    def finish(place, unused):
        for p in range(parts):
            for which in range(2):
                copy = across(place, which, None, p)
                copy.wait_recv()
                copy.wait_send()
            aside(place, None, p).wait_send()
        return unused

    lax.fori_loop(0, line, finish, 0)

    def sent(k, unused):
        for p in range(parts):
            for way in range(2):

                @pl.when(has(way, k) & goes(way))
                def _(way=way, p=p):
                    along(way, k, p).wait_send()

        return unused

    lax.fori_loop(0, line, sent, 0)
    save.wait()
    end()


def weights_gather(up, down, own):
    count = lax.axis_size("dp")
    reach = count // 2
    parts = len(own)
    pieces = (count, up.shape[1], up.shape[0] * up.shape[2] // count)
    return pl.pallas_call(
        functools.partial(weights_gather_kernel, count, parts),
        in_specs=[anywhere] * (parts + 2),
        out_specs=[anywhere] * (parts + 2),
        out_shape=[shape_of(*pieces, dtype=bf16), shape_of(*down.shape, dtype=bf16)]
        + [shape_of(2, count, *part.shape, dtype=part.dtype) for part in own],
        scratch_shapes=[
            pltpu.VMEM(up.shape, f32),
            pltpu.VMEM(down.shape, f32),
            pltpu.VMEM(pieces, bf16),
            pltpu.VMEM(down.shape, bf16),
            dma((4,)),
            dma((2, count - 1)),
            dma((2, reach, parts)),
            dma((2, reach, parts)),
            dma((2, reach, parts)),
            dma((2, count, parts)),
            dma((parts,)),
        ],
        compiler_params=comm_params(3),
        name="weights_gather",
    )(up, down, *own)


def grads_reduce_kernel(count, parts, pieces, *refs):
    part, pieces_out, refs = refs[:parts], refs[parts], refs[parts + 1 :]
    out, refs = refs[:parts], refs[parts:]
    sides, refs = refs[:parts], refs[parts:]
    outs = (refs[:parts], refs[parts : 2 * parts])
    ins = (refs[2 * parts : 3 * parts], refs[3 * parts : 4 * parts])
    after_sems, before_sems, side_sems, piece_sems, local_sem = refs[4 * parts :]
    a, b, core, after, before, beside, partner = grid_here(count)
    line = count // 2
    greet(dp_peers(count))

    def aside(place, p):
        return remote(
            part[p].at[2 * place + 1 - b], sides[p].at[place], side_sems.at[0, place, p],
            side_sems.at[1, place, p], beside,
        )

    def along(way, place, p):
        sems = after_sems if way == 0 else before_sems
        return remote(
            outs[way][p].at[place], ins[way][p].at[place], sems.at[0, place, p], sems.at[1, place, p],
            after if way == 0 else before,
        )

    def far(way, k):
        return line - 1 - k if way == 0 else k

    def starts(k, unused):
        for p in range(parts):
            for way in range(2):

                @pl.when((way == 0) | (far(0, k) != far(1, k)))
                def _(way=way, p=p):
                    aside(far(way, k), p).start()

        return unused

    lax.fori_loop(0, (line + 1) // 2, starts, 0)
    end = exchange(count, pieces, pieces_out, piece_sems, local_sem)

    def both_lines(place, p):
        aside(place, p).wait_recv()
        return part[p][2 * place + b].astype(f32) + sides[p][place].astype(f32)

    def passing(k, unused):
        for p in range(parts):
            for way in range(2):
                place = far(way, k)

                @pl.when(place > a if way == 0 else place < a)
                def _(way=way, place=place, p=p):
                    value = both_lines(place, p)
                    outs[way][p][place] = value.astype(bf16)

                    @pl.when(a > 0 if way == 0 else a < line - 1)
                    def _():
                        along(way, place, p).wait_recv()
                        value = outs[way][p][place].astype(f32) + ins[way][p][place].astype(f32)
                        outs[way][p][place] = value.astype(bf16)

                    along(way, place, p).start()

        return unused

    lax.fori_loop(0, line - 1, passing, 0)
    for p in range(parts):
        out[p][...] = both_lines(a, p)
        for way in range(2):

            @pl.when(a > 0 if way == 0 else a < line - 1)
            def _(way=way, p=p):
                along(way, a, p).wait_recv()
                out[p][...] = out[p][...] + ins[way][p][a].astype(f32)

    def finish(place, unused):
        for p in range(parts):
            aside(place, p).wait_send()
            for way in range(2):

                @pl.when(place > a if way == 0 else place < a)
                def _(way=way, p=p):
                    along(way, place, p).wait_send()

        return unused

    lax.fori_loop(0, line, finish, 0)
    end()


def grads_reduce(pieces, parts):
    count = lax.axis_size("dp")
    reach = count // 2
    number = len(parts)
    slots = [pltpu.VMEM((reach,) + part.shape[1:], bf16) for part in parts]
    return pl.pallas_call(
        functools.partial(grads_reduce_kernel, count, number),
        in_specs=[anywhere] + [in_vmem] * number,
        out_specs=[anywhere] + [in_vmem] * number,
        out_shape=[shape_of(*pieces.shape, dtype=bf16)]
        + [shape_of(*part.shape[1:]) for part in parts],
        scratch_shapes=slots * 5
        + [dma((2, reach, number))] * 3
        + [dma((2, count - 1)), dma(())],
        compiler_params=comm_params(4, 60),
        name="grads_reduce",
    )(pieces, *parts)


def join(
    count, forward, state_ref, total_ref, rates, out_ref, other_state, other_total, mine, mine_total, states,
    totals, back, back_in, pair_sems, sems,
):
    section, dp, core = (lax.axis_index(name) for name in ("section", "dp", "expert"))
    partner = (section, dp, 1 - core)
    swap = [
        remote(state_ref.at[1 - core], other_state, pair_sems.at[0, 0], pair_sems.at[1, 0], partner),
        remote(total_ref.at[1 - core], other_total, pair_sems.at[0, 1], pair_sems.at[1, 1], partner),
    ]
    for copy in swap:
        copy.start()
    own_state, own_total = state_ref[core], total_ref[core]
    for copy in swap:
        copy.wait_recv()
    leads = core == (0 if forward else 1)
    first_state = jnp.where(leads, own_state, other_state[...])
    first_total = jnp.where(leads, own_total, other_total[...])
    second_state = jnp.where(leads, other_state[...], own_state)
    second_total = jnp.where(leads, other_total[...], own_total)
    mine[...] = (jnp.exp2(rates * second_total) * first_state + second_state).astype(bf16)
    mine_total[...] = first_total + second_total
    copies = []
    for d, peer in enumerate(dp_peers(count)):
        for n, (src, dst) in enumerate(((mine, states), (mine_total, totals))):
            copy = remote(src, dst.at[dp], sems.at[0, d, n], sems.at[1, d, n], peer)
            copy.start()
            copies.append(copy)
    states[dp] = mine[...]
    totals[dp] = mine_total[...]
    for copy in copies:
        copy.wait_recv()

    entering = jnp.zeros_like(own_state)
    for k in range(count):
        source = k if forward else count - 1 - k
        reached = (source < dp) if forward else (source > dp)
        fresh = jnp.exp2(rates * totals[source]) * entering + states[source].astype(f32)
        entering = jnp.where(reached, fresh, entering)
    after = jnp.exp2(rates * first_total) * entering + first_state
    back[...] = jnp.where(leads, after, entering)
    swap_back = remote(back, back_in, pair_sems.at[0, 2], pair_sems.at[1, 2], partner)
    swap_back.start()
    out_ref[core] = jnp.where(leads, entering, after)
    swap_back.wait_recv()
    out_ref[1 - core] = back_in[...]
    for copy in swap + copies + [swap_back]:
        copy.wait_send()


def join_scratch(count, states, half):
    one, sums = pltpu.VMEM((states, half), f32), pltpu.VMEM((1, half), f32)
    return [
        pltpu.VMEM((2, states, half), f32),
        pltpu.VMEM((2, 1, half), f32),
        pltpu.VMEM((2, states, half), f32),
        one,
        sums,
        pltpu.VMEM((states, half), bf16),
        sums,
        pltpu.VMEM((count, states, half), bf16),
        pltpu.VMEM((count, 1, half), f32),
        one,
        one,
        dma((2, 3)),
        dma((2, count - 1, 2)),
    ]


def own_lanes(a_ref, half):
    return a_ref[:, lanes_at(lax.axis_index("expert"), half)]


def greet_all(count):
    section, dp, core = (lax.axis_index(name) for name in ("section", "dp", "expert"))
    greet(dp_peers(count) + [(section, dp, 1 - core)])


def exchange(count, pieces_ref, out_ref, sems, local_sem):
    dp = lax.axis_index("dp")
    keep = pltpu.make_async_copy(pieces_ref.at[dp], out_ref.at[dp], local_sem)
    keep.start()
    copies = []
    for by, peer in enumerate(dp_peers(count)):
        copy = remote(pieces_ref.at[peer[1]], out_ref.at[dp], sems.at[0, by], sems.at[1, by], peer)
        copy.start()
        copies.append(copy)

    def end():
        keep.wait()
        for copy in copies:
            copy.wait()

    return end


def mixer_forward_kernel(
    count, step_ref, drive_ref, bb_ref, cb_ref, a_ref, y_ref, starts_ref, state, total, entering, *rest
):
    half = state.shape[2]
    width = block_width(half, 384)
    scan_final(step_ref, drive_ref, bb_ref, a_ref, state, total, width)
    greet_all(count)
    join(count, True, state, total, own_lanes(a_ref, half), entering, *rest)
    scan_outputs(step_ref, drive_ref, bb_ref, cb_ref, a_ref, entering, y_ref, starts_ref, width)


def mixer_forward(step, drive, in_map, out_map, rates):
    count = lax.axis_size("dp")
    (length, width), states = step.shape, rates.shape[0]
    return pl.pallas_call(
        functools.partial(mixer_forward_kernel, count),
        in_specs=[in_vmem] * 5,
        out_specs=[in_vmem] * 2,
        out_shape=[shape_of(length, width), shape_of(length // CHUNK, states, width)],
        scratch_shapes=join_scratch(count, states, width // 2),
        compiler_params=comm_params(5),
        name="mixer_forward",
    )(step, drive, in_map, out_map, rates)


def mixer_backward_kernel(
    count, step_ref, drive_ref, dy_ref, bb_ref, cb_ref, a_ref, starts_ref, through_ref, flow_ref, db_ref, dc_ref,
    da_ref, state, total, inflow, *rest,
):
    half = state.shape[2]
    width = block_width(half, 384)
    scan_leak(step_ref, dy_ref, cb_ref, a_ref, state, total, width)
    greet_all(count)
    join(count, False, state, total, own_lanes(a_ref, half), inflow, *rest)
    scan_back(
        step_ref, drive_ref, dy_ref, bb_ref, cb_ref, a_ref, starts_ref, inflow, through_ref, flow_ref, db_ref,
        dc_ref, da_ref, width,
    )


def mixer_backward(step, drive, dy, in_map, out_map, rates, starts):
    count = lax.axis_size("dp")
    (length, width), states = step.shape, rates.shape[0]
    wide, maps = shape_of(length, width), shape_of(*in_map.shape)
    return pl.pallas_call(
        functools.partial(mixer_backward_kernel, count),
        in_specs=[in_vmem] * 7,
        out_specs=[in_vmem] * 5,
        out_shape=[wide, wide, maps, maps, shape_of(states, width)],
        scratch_shapes=join_scratch(count, states, width // 2),
        compiler_params=comm_params(6),
        name="mixer_backward",
    )(step, drive, dy, in_map, out_map, rates, starts)


def dot(a, b, dims, dtype=f32):
    return lax.dot_general(a, b, (dims, ((), ())), preferred_element_type=f32).astype(dtype)


def nn(a, b, dtype=f32):
    return dot(a, b, ((1,), (0,)), dtype)


def nt(a, b, dtype=f32):
    return dot(a, b, ((1,), (1,)), dtype)


def tn(a, b, dtype=f32):
    return dot(a, b, ((0,), (0,)), dtype)


def normalize(values, gain):
    return values * lax.rsqrt(jnp.mean(values * values, axis=-1, keepdims=True) + epsilon) * gain


def sums(value):
    return jnp.sum(value, 0)


def normalize_back(values, gain, upstream):
    scale = lax.rsqrt(jnp.mean(values * values, axis=-1, keepdims=True) + epsilon)
    unit = values * scale
    inner = upstream * gain
    d_values = scale * (inner - unit * jnp.mean(inner * unit, axis=-1, keepdims=True))
    return d_values, sums(upstream * unit)


def from_behind(shard, axis, by):
    count = 1
    for name in (axis,) if isinstance(axis, str) else axis:
        count *= lax.axis_size(name)
    pairs = [(i, i + by) for i in range(count) if 0 <= i + by < count]
    return lax.ppermute(shard, axis, pairs)


def swap_pair(value):
    return lax.ppermute(value, "expert", [(0, 1), (1, 0)])


def spread(values):
    return jnp.broadcast_to(values[:, :, None], values.shape + (LANES,))


def routing(resid, moe_gain, router, chosen, placed, dropped):
    normed = normalize(resid, moe_gain)
    probs = jax.nn.softmax(jnp.dot(normed, router, precision=highest), axis=-1)
    keep = (1 - dropped).astype(f32)
    pick = (chosen[:, None] == jnp.arange(EXPERTS)[None]).astype(f32)
    gate = jnp.sum(probs * pick, -1) * keep
    flat = chosen * CAP + placed
    table = ((flat[:, None] == jnp.arange(EXPERTS * CAP)[None]) & (dropped[:, None] == 0)).astype(
        bf16
    )
    return normed, probs, pick, keep, gate, table


def by_core(buffer):
    return buffer.reshape(2, -1, buffer.shape[1])


def mixed(xz, weights):
    width = weights["w_out"].shape[0]
    taps = weights["conv_w"].shape[0]
    length = xz.shape[0] - HALO
    padded = xz[HALO - taps + 1 :, :width]
    summed = weights["conv_b"]
    for tap in range(taps):
        summed = summed + weights["conv_w"][tap : tap + 1] * padded[tap : tap + length]
    return padded, summed, xz[HALO:, width:]


def selective(projected, weights):
    rank = weights["dt_proj"].shape[0]
    states = weights["rates"].shape[0]
    dt_low = projected[:, :rank].astype(bf16)
    dt_raw = nn(dt_low, weights["dt_proj"]) + weights["dt_bias"]
    in_map = projected[:, rank : rank + states]
    out_map = projected[:, rank + states : rank + 2 * states]
    return dt_low, dt_raw, jax.nn.softplus(dt_raw), spread(in_map), spread(out_map)


def forward(rows, halo, chosen, placed, dropped, weights):
    inputs = jnp.concatenate([halo, rows], 0).astype(f32)
    normed = normalize(inputs, weights["norm_gain"]).astype(bf16)
    xz = nt(normed, weights["w_in"])
    padded, summed, gate_in = mixed(xz, weights)
    signal = jax.nn.silu(summed).astype(bf16)
    projected = nn(signal, weights["x_proj"])
    dt_low, dt_raw, step, in_map, out_map = selective(projected, weights)
    wide = signal.astype(f32)
    drive = step * wide
    rates = weights["rates"] * LOG2E
    scanned, starts = mixer_forward(step, drive, in_map, out_map, rates)
    gated = ((scanned + weights["skip"] * wide) * jax.nn.silu(gate_in)).astype(bf16)
    resid = rows.astype(f32) + nn(gated, weights["w_out"])
    normed_moe, probs, pick, keep, gate, table = routing(
        resid, weights["moe_gain"], weights["router"], chosen, placed, dropped
    )
    buffer = tn(table, normed_moe.astype(bf16), bf16)
    ahead = (by_core(buffer), resid, table, gate[:, None])
    kept = dict(
        rows=rows, halo=halo, xz=xz, projected=projected, scanned=scanned, starts=starts, resid=resid,
    )
    return ahead, kept


def backward_routing(kept, chosen, placed, dropped, weights):
    return routing(
        kept["resid"], weights["moe_gain"], weights["router"], chosen, placed, dropped
    )


def backward_experts(routed, returned, upstream, d_sent, weights):
    normed_moe, probs, pick, keep, gate, table = routed
    d_sent = d_sent.reshape(-1, d_sent.shape[2])
    returned = returned.reshape(d_sent.shape)
    upstream = upstream.astype(f32)
    d_gate = jnp.sum(upstream * nn(table, returned), -1)
    d_choice = d_gate[:, None] * pick * keep[:, None]
    d_logits = probs * (d_choice - jnp.sum(probs * d_choice, -1, keepdims=True))
    d_normed = nn(table, d_sent) + jnp.dot(d_logits, weights["router"].T, precision=highest)
    return upstream, d_normed, d_logits


def backward_mixer(upstream, kept, d_normed, d_logits, weights):
    resid = kept["resid"]
    normed_moe = normalize(resid, weights["moe_gain"])
    grad_router = lax.dot_general(
        normed_moe, d_logits, (((0,), (0,)), ((), ())), precision=highest
    )
    d_norm, grad_moe = normalize_back(resid, weights["moe_gain"], d_normed)
    d_resid = upstream + d_norm

    inputs = kept["rows"].astype(f32)
    normed = normalize(inputs, weights["norm_gain"]).astype(bf16)
    xz = kept["xz"]
    padded, summed, gate_in = mixed(xz, weights)
    signal_act, signal_back = jax.vjp(jax.nn.silu, summed)
    signal = signal_act.astype(bf16)
    wide = signal.astype(f32)
    dt_low, dt_raw, step, in_map, out_map = selective(kept["projected"], weights)
    drive = step * wide
    rates = weights["rates"] * LOG2E
    skip = weights["skip"]
    total_out = kept["scanned"] + skip * wide
    gate_act, gate_back = jax.vjp(jax.nn.silu, gate_in)
    gated = (total_out * gate_act).astype(bf16)
    d_mixer = d_resid.astype(bf16)
    d_gated = nt(d_mixer, weights["w_out"])
    d_total = d_gated * gate_act
    d_gate_in = gate_back(d_gated * total_out)[0]
    grad_skip = sums(d_total * wide)
    through, flow, d_in_map, d_out_map, d_rates = mixer_backward(
        step, drive, d_total, in_map, out_map, rates, kept["starts"]
    )
    d_step = flow / LOG2E + through * wide
    d_signal = step * through + d_total * skip
    d_raw = d_step * jax.nn.sigmoid(dt_raw)
    grad_dt_bias = sums(d_raw)
    d_raw_low = d_raw.astype(bf16)
    d_low = nt(d_raw_low, weights["dt_proj"])
    d_projected = jnp.concatenate(
        [d_low, jnp.sum(d_in_map, -1), jnp.sum(d_out_map, -1)], 1
    ).astype(bf16)
    d_signal = d_signal + nt(d_projected, weights["x_proj"])
    d_summed = signal_back(d_signal)[0]
    taps = weights["conv_w"].shape[0]
    length = d_summed.shape[0]
    ahead = from_behind(d_summed[:8], ("dp", "expert"), -1)
    extended = jnp.concatenate([d_summed, ahead], 0)
    d_conv_in = jnp.zeros_like(d_summed)
    for tap in range(taps):
        begin = taps - 1 - tap
        d_conv_in = d_conv_in + weights["conv_w"][tap : tap + 1] * extended[begin : begin + length]
    grad_conv = [
        sums(d_summed * padded[tap : tap + length]) for tap in range(taps)
    ]
    d_xz = jnp.concatenate([d_conv_in, d_gate_in], 1).astype(bf16)
    d_normed_in = nn(d_xz, weights["w_in"])
    d_inputs, grad_norm = normalize_back(inputs, weights["norm_gain"], d_normed_in)
    result = (d_resid + d_inputs).astype(bf16)
    half = signal.shape[1] // 2

    def sides(value):
        return value[:, :half], value[:, half:]

    lanes = (-(d_projected.shape[1] + dt_low.shape[1])) % LANES
    common = jnp.concatenate(
        [normed, d_mixer, d_projected, dt_low, jnp.zeros((length, lanes), bf16)], 1
    )
    width = signal.shape[1]
    cut = [sides(v) for v in (d_xz[:, :width], d_xz[:, width:], gated, signal, d_raw_low)]
    core = lax.axis_index("expert")
    own, theirs = (
        jnp.concatenate([jnp.where(core == side, a, b) for a, b in cut], 1) for side in (0, 1)
    )
    got_common, got = swap_pair(common), swap_pair(theirs)
    activations = (
        jnp.concatenate([common, got_common], 0), jnp.concatenate([own, got], 0),
    )
    vectors = (
        grad_conv + [sums(d_summed), grad_dt_bias, grad_skip], d_rates * weights["rates"],
        [grad_norm, grad_moe], grad_router,
    )
    return result, activations, vectors


def gather_weights(
    norm_gain, w_in, conv_w, conv_b, x_proj, dt_proj, dt_bias, a_log, skip, w_out, moe_gain, router,
    w_up, w_down,
):
    count = lax.axis_size("dp")
    share = x_proj.shape[1]
    model = w_out.shape[2]
    low_in = jnp.transpose(w_in[0].astype(bf16), (1, 2, 0))
    pieces = [
        x_proj[0], dt_proj[0].T, conv_w[0].T, conv_b[0][:, None], dt_bias[0][:, None],
        skip[0][:, None], a_log[0].T, norm_gain[0][:, None], moe_gain[0][:, None], router[0],
    ]
    sizes = [piece.shape[1] for piece in pieces]
    pad = (-sum(sizes)) % LANES
    small = jnp.concatenate(pieces + [jnp.zeros((share, pad), f32)], 1).astype(bf16)
    up, low_down, in_x, in_z, out, small = weights_gather(
        w_up[0], w_down[0], [low_in[0], low_in[1], w_out[0].astype(bf16), small]
    )
    width = 2 * count * share
    w_in_all = jnp.concatenate([in_x.reshape(width, model), in_z.reshape(width, model)], 0)
    table = small.reshape(width, -1)
    rows = table.astype(f32).T
    at = 0
    found = []
    for size in sizes:
        found.append(rows[at : at + size])
        at += size
    unused, dt_proj, conv_w, conv_b, dt_bias, a_skip, a_log, norm_gain, moe_gain, router = found
    weights = dict(
        w_in=w_in_all,
        w_out=out.reshape(width, model),
        x_proj=table[:, : sizes[0]],
        dt_proj=dt_proj.astype(bf16),
        conv_w=conv_w,
        conv_b=conv_b,
        dt_bias=dt_bias,
        skip=a_skip,
        rates=-jnp.exp(a_log),
        norm_gain=norm_gain[:, :model],
        moe_gain=moe_gain[:, :model],
        router=router[:, :model].T,
        w_up=up.reshape(-1, up.shape[2]),
        w_down=low_down.reshape(-1, model),
    )
    return weights, sizes


def mixer_grads(activations, vectors, sizes, up, count):
    common, own = activations
    channel, d_rates, feature, grad_router = vectors

    def added(pieces):
        return [piece[None] for piece in pieces]

    channel = jnp.concatenate(added(channel) + [d_rates], 0)
    feature = jnp.concatenate(added(feature) + [grad_router.T], 0)
    half = own.shape[1] // 5
    share = half // count
    model = feature.shape[1]
    core = lax.axis_index("expert")
    normed, d_mixer = common[:, :model], common[:, model : 2 * model]
    d_projected = common[:, 2 * model : 2 * model + sizes[0]]
    dt_low = common[:, 2 * model + sizes[0] : 2 * model + sizes[0] + sizes[1]]
    d_x, d_z, gated, signal, d_raw = (own[:, i * half : (i + 1) * half] for i in range(5))
    grad_x = tn(d_x, normed, bf16).reshape(count, share, model)
    grad_z = tn(d_z, normed, bf16).reshape(count, share, model)
    grad_out = tn(gated, d_mixer, bf16).reshape(count, share, model)
    grad_proj = tn(signal, d_projected)
    grad_dt = tn(d_raw, dt_low)
    sides = (channel[:, :half], channel[:, half:])

    def packed(which):
        return jnp.concatenate([which, feature], 0)

    own_vectors = packed(jnp.where(core == 0, sides[0], sides[1]))
    got = swap_pair(packed(jnp.where(core == 0, sides[1], sides[0])))
    total = (own_vectors + got).T
    pad = (-sum(sizes)) % LANES
    small = jnp.concatenate([grad_proj, grad_dt, total, jnp.zeros((half, pad), f32)], 1)
    small = small.astype(bf16).reshape(count, share, -1)
    up, grad_x, grad_z, grad_out, small = grads_reduce(up, [grad_x, grad_z, grad_out, small])
    at = 0
    found = []
    for size in sizes:
        found.append(small[:, at : at + size])
        at += size
    x_proj, dt_proj, conv_w, conv_b, dt_bias, skip, a_log, norm_gain, moe_gain, router = found
    return (
        norm_gain[:, 0],
        jnp.transpose(jnp.stack([grad_x, grad_z], 0), (2, 0, 1)),
        conv_w.T,
        conv_b[:, 0],
        x_proj,
        dt_proj.T,
        dt_bias[:, 0],
        a_log.T,
        skip[:, 0],
        grad_out,
        moe_gain[:, 0],
        router,
        up_grad(up),
    )


def rows_flat(value):
    return value.reshape(-1, value.shape[-1])


def down_grad(first, second):
    hidden, d_produced = (
        jnp.concatenate([rows_flat(a), rows_flat(b)], 0)
        for a, b in zip(first, second, strict=True)
    )
    return tn(hidden, d_produced).reshape(EXPERTS // 2, -1, d_produced.shape[1])


def up_pieces(first, second, count):
    arrived, d_pre = (
        jnp.concatenate([rows_flat(a), rows_flat(b)], 0)
        for a, b in zip(first, second, strict=True)
    )
    return tn(arrived, d_pre, bf16).reshape(count, arrived.shape[1] // count, -1)


def up_grad(up):
    each = EXPERTS // 2
    count = up.shape[0]
    cut = up.shape[2] // each
    return jnp.stack(
        [
            jnp.concatenate([up[k, :, e * cut : (e + 1) * cut] for k in range(count)], 1)
            for e in range(each)
        ],
        0,
    ).astype(f32)


def shards(
    tokens, cotangent, routes, slots, drops, norm_gain, w_in, conv_w, conv_b, x_proj, dt_proj, dt_bias,
    a_log, skip, w_out, moe_gain, router, w_up, w_down,
):
    count = lax.axis_size("dp")
    section = lax.axis_index("section")
    top = section == 1
    weights, sizes = gather_weights(
        norm_gain, w_in, conv_w, conv_b, x_proj, dt_proj, dt_bias, a_log, skip, w_out, moe_gain,
        router, w_up, w_down,
    )
    micro = tokens.shape[0]
    blocks = ("dp", "expert")
    steps = micro + 1

    def pick(which):
        return [lax.dynamic_index_in_dim(v[0], which, 0, False) for v in (routes, slots, drops)]

    halos = jnp.stack(
        [from_behind(tokens[m, -HALO:], blocks, 1) for m in range(micro)], 0
    )
    incoming, incoming_halo = jnp.zeros_like(tokens[0]), jnp.zeros_like(halos[0])
    results, bank, grads, found, last = [], [], [], [], []
    below = None

    def micro_of(step, first):
        return jnp.clip(step - first, 0, micro - 1)

    def back_parts(step):
        if step == 1:
            kept = jax.tree.map(lambda a, b: jnp.where(top, a, b), bank[2], bank[0])
        else:
            kept = bank[1]
        routed = backward_routing(kept, *pick(micro_of(step, 1 - section)), weights)
        above = cotangent[step] if step < micro else jnp.zeros_like(cotangent[0])
        above = jnp.where(top, above, jnp.zeros_like(above))
        crossing = () if below is None else (below,)
        return kept, routed, crossing + (above, routed[5].T, routed[4][:, None], kept["arrived"])

    for step in range(2 * steps - 1):
        ahead = behind = None
        if step < steps:
            fresh = min(step, micro - 1)
            rows = jnp.where(top, incoming, tokens[fresh])
            halo = jnp.where(top, incoming_halo, halos[fresh])
            ahead, fresh_kept = forward(rows, halo, *pick(micro_of(step, section)), weights)
        if step >= steps - 1:
            kept, routed, behind = back_parts(step - steps + 1)
        cross = (ahead is None) != (behind is None)
        if cross or count <= 8:
            done = experts(weights["w_up"], weights["w_down"], ahead, behind, cross)
        else:
            done = experts(weights["w_up"], weights["w_down"], ahead, None, False)
            done = [*done, *experts(weights["w_up"], weights["w_down"], None, behind, False)]
        if ahead is not None:
            fresh_kept["returned"], result = done[:2]
            if cross:
                incoming, incoming_halo = done[2:4]
            number = 5 if cross else 3
            fresh_kept["arrived"] = done[number - 1]
            results.append(result)
            bank.append(fresh_kept)
            done = done[number:]
        if behind is not None:
            upstream, d_sent, d_produced, hidden, d_pre = done
            last.append((hidden, d_produced, kept["arrived"], d_pre))
            upstream, d_normed, d_logits = backward_experts(
                routed, kept["returned"], upstream, d_sent, weights
            )
            if len(last) == steps:
                one = jax.tree.map(lambda a, b: jnp.where(top, a, b), last[0], last[2])
                moving = up_pieces(one[2:], last[1][2:], count)
            below, *pieces = backward_mixer(upstream, kept, d_normed, d_logits, weights)
            grads.append(below)
            found.append(pieces)
    outputs = jnp.stack(
        [jnp.where(top, results[m + 1], results[m]) for m in range(micro)], 0
    )
    backs = jnp.stack([jnp.where(top, grads[m], grads[m + 1]) for m in range(micro)], 0)

    def valid_one(place):
        return jax.tree.map(lambda a, b: jnp.where(top, a, b), found[0][place], found[2][place])

    activations = jax.tree.map(
        lambda a, b: jnp.concatenate([a, b], 0), valid_one(0), found[1][0]
    )
    vectors = jax.tree.map(lambda a, b: a + b, valid_one(1), found[1][1])
    mixer = mixer_grads(activations, vectors, sizes, moving, count)
    down = down_grad(one[:2], last[1][:2])
    return (outputs[None], backs[None]) + tuple(v[None] for v in mixer) + (down[None],)


def solution(mesh):
    both = ("dp", "expert")
    weights = (
        P("section", "dp"),
        P("section", None, None, both),
        P("section", None, both),
        P("section", both),
        P("section", both, None),
        P("section", None, both),
        P("section", both),
        P("section", None, both),
        P("section", both),
        P("section", both, None),
        P("section", "dp"),
        P("section", "dp", None),
        P("section", "expert", "dp", None),
        P("section", "expert", "dp", None),
    )
    return jax.shard_map(
        shards,
        mesh=mesh,
        in_specs=(P(None, both, None),) * 2 + (P("section", None, both),) * 3 + weights,
        out_specs=(P("section", None, both, None),) * 2 + weights,
        check_vma=False,
    )
```

```python
import functools

import jax
import jax.numpy as jnp
from jax import lax
from jax.experimental import pallas as pl
from jax.experimental.pallas import tpu as pltpu
from jax.sharding import PartitionSpec as P

EXPERTS = 8
CAP = 12
LANES = 128
CHUNK = 8
HALO = 16
LOG2E = 1.4426950408889634
MESH = pl.DeviceIdType.MESH
MIB = 2**20

epsilon = 1e-05
highest = lax.Precision.HIGHEST
f32 = jnp.float32
bf16 = jnp.bfloat16


def tiles_of(width):
    return [slice(i * LANES, (i + 1) * LANES) for i in range(width // LANES)]


def lanes_at(block, width):
    return pl.ds(pl.multiple_of(block * width, LANES), width)


def scan_final(step_ref, drive_ref, bb_ref, a_ref, state, total, width):
    states = a_ref.shape[0]
    tiles = tiles_of(width)
    each = state.shape[2] // width

    def block(b, unused):
        lanes = lanes_at(b, width)
        rates = [a_ref[:, lanes][:, t] for t in tiles]

        def body(i, carry):
            base = pl.multiple_of(i * CHUNK, CHUNK)
            step = step_ref[pl.ds(base, CHUNK), lanes]
            drive = drive_ref[pl.ds(base, CHUNK), lanes]
            carry, sums = list(carry[0]), carry[1]
            for k in range(CHUNK):
                in_map = bb_ref[base + k]
                for j, t in enumerate(tiles):
                    decay = jnp.exp2(step[k : k + 1, t] * rates[j])
                    carry[j] = decay * carry[j] + drive[k : k + 1, t] * in_map
            return tuple(carry), sums + step

        zeros = tuple(jnp.zeros((states, LANES), f32) for _ in tiles)
        final, sums = lax.fori_loop(
            0, step_ref.shape[0] // CHUNK, body, (zeros, jnp.zeros((CHUNK, width), f32))
        )
        side, at = lax.div(b, each), lanes_at(lax.rem(b, each), width)
        state[side, :, at] = jnp.concatenate(final, 1)
        total[side, :, at] = jnp.sum(sums, 0, keepdims=True)
        return unused

    lax.fori_loop(0, 2 * each, block, 0)


def scan_leak(step_ref, dy_ref, cb_ref, a_ref, state, total, width):
    states = a_ref.shape[0]
    tiles = tiles_of(width)
    each = state.shape[2] // width
    count = step_ref.shape[0] // CHUNK

    def block(b, unused):
        lanes = lanes_at(b, width)
        rates = [a_ref[:, lanes][:, t] for t in tiles]

        def body(i, carry):
            base = pl.multiple_of((count - 1 - i) * CHUNK, CHUNK)
            step = step_ref[pl.ds(base, CHUNK), lanes]
            dys = dy_ref[pl.ds(base, CHUNK), lanes]
            carry, sums = list(carry[0]), carry[1]
            for k in reversed(range(CHUNK)):
                out_map = cb_ref[base + k]
                for j, t in enumerate(tiles):
                    decay = jnp.exp2(step[k : k + 1, t] * rates[j])
                    carry[j] = decay * (carry[j] + dys[k : k + 1, t] * out_map)
            return tuple(carry), sums + step

        zeros = tuple(jnp.zeros((states, LANES), f32) for _ in tiles)
        final, sums = lax.fori_loop(0, count, body, (zeros, jnp.zeros((CHUNK, width), f32)))
        side, at = lax.div(b, each), lanes_at(lax.rem(b, each), width)
        state[side, :, at] = jnp.concatenate(final, 1)
        total[side, :, at] = jnp.sum(sums, 0, keepdims=True)
        return unused

    lax.fori_loop(0, 2 * each, block, 0)


def scan_outputs(step_ref, drive_ref, bb_ref, cb_ref, a_ref, entering, y_ref, starts_ref, width):
    tiles = tiles_of(width)
    each = entering.shape[2] // width

    def block(b, unused):
        lanes = lanes_at(b, width)
        rates = [a_ref[:, lanes][:, t] for t in tiles]

        def body(i, carry):
            base = pl.multiple_of(i * CHUNK, CHUNK)
            step = step_ref[pl.ds(base, CHUNK), lanes]
            drive = drive_ref[pl.ds(base, CHUNK), lanes]
            carry = list(carry)
            starts_ref[i, :, lanes] = jnp.concatenate(carry, 1)
            rows = [[] for _ in tiles]
            for k in range(CHUNK):
                in_map = bb_ref[base + k]
                out_map = cb_ref[base + k]
                for j, t in enumerate(tiles):
                    decay = jnp.exp2(step[k : k + 1, t] * rates[j])
                    carry[j] = decay * carry[j] + drive[k : k + 1, t] * in_map
                    rows[j].append(jnp.sum(carry[j] * out_map, 0, keepdims=True))
            y_ref[pl.ds(base, CHUNK), lanes] = jnp.concatenate(
                [jnp.concatenate(row, 0) for row in rows], 1
            )
            return tuple(carry)

        first = entering[lax.div(b, each), :, lanes_at(lax.rem(b, each), width)]
        lax.fori_loop(0, step_ref.shape[0] // CHUNK, body, tuple(first[:, t] for t in tiles))
        return unused

    lax.fori_loop(0, 2 * each, block, 0)


def scan_back(
    step_ref, drive_ref, dy_ref, bb_ref, cb_ref, a_ref, starts_ref, inflow, through_ref, flow_ref, db_ref,
    dc_ref, da_ref, width,
):
    tiles = tiles_of(width)
    each = inflow.shape[2] // width
    count = step_ref.shape[0] // CHUNK
    db_ref[...] = jnp.zeros_like(db_ref)
    dc_ref[...] = jnp.zeros_like(dc_ref)

    def block(b, unused):
        lanes = lanes_at(b, width)
        rates = [a_ref[:, lanes][:, t] for t in tiles]

        def body(i, carry):
            grads, d_rates = list(carry[0]), list(carry[1])
            chunk = count - 1 - i
            base = pl.multiple_of(chunk * CHUNK, CHUNK)
            step = step_ref[pl.ds(base, CHUNK), lanes]
            drive = drive_ref[pl.ds(base, CHUNK), lanes]
            dys = dy_ref[pl.ds(base, CHUNK), lanes]
            start = starts_ref[chunk, :, lanes]
            d_in, d_out = [None] * CHUNK, [None] * CHUNK
            all_through, all_flows = [], []
            for j, t in enumerate(tiles):
                current = start[:, t]
                decays, states = [], [current]
                for k in range(CHUNK):
                    decay = jnp.exp2(step[k : k + 1, t] * rates[j])
                    current = decay * current + drive[k : k + 1, t] * bb_ref[base + k]
                    decays.append(decay)
                    states.append(current)
                grad = grads[j]
                through, flows = [None] * CHUNK, [None] * CHUNK
                for k in reversed(range(CHUNK)):
                    dy = dys[k : k + 1, t]
                    grad = grad + dy * cb_ref[base + k]
                    through[k] = jnp.sum(grad * bb_ref[base + k], 0, keepdims=True)
                    piece = grad * drive[k : k + 1, t]
                    d_in[k] = piece if d_in[k] is None else d_in[k] + piece
                    piece = dy * states[k + 1]
                    d_out[k] = piece if d_out[k] is None else d_out[k] + piece
                    grad = decays[k] * grad
                    flow = grad * states[k]
                    flows[k] = jnp.sum(flow * rates[j], 0, keepdims=True)
                    d_rates[j] = d_rates[j] + flow * step[k : k + 1, t]
                grads[j] = grad
                all_through.append(jnp.concatenate(through, 0))
                all_flows.append(jnp.concatenate(flows, 0))
            through_ref[pl.ds(base, CHUNK), lanes] = jnp.concatenate(all_through, 1)
            flow_ref[pl.ds(base, CHUNK), lanes] = jnp.concatenate(all_flows, 1)
            for k in range(CHUNK):
                db_ref[base + k] += d_in[k]
                dc_ref[base + k] += d_out[k]
            return tuple(grads), tuple(d_rates)

        first = inflow[lax.div(b, each), :, lanes_at(lax.rem(b, each), width)]
        zeros = tuple(jnp.zeros((a_ref.shape[0], LANES), f32) for _ in tiles)
        d_rates = lax.fori_loop(0, count, body, (tuple(first[:, t] for t in tiles), zeros))[1]
        da_ref[:, lanes] = jnp.concatenate(d_rates, 1)
        return unused

    lax.fori_loop(0, 2 * each, block, 0)


def block_width(width, most):
    while width % most:
        most -= LANES
    return most


def shape_of(*shape, dtype=f32):
    return jax.ShapeDtypeStruct(shape, dtype)


def place_of(index, count):
    return jnp.where(
        lax.rem(index, 2) == 0, lax.div(index, 2), count - 1 - lax.div(index, 2)
    )


def index_at(place, count):
    place = lax.rem(place + 2 * count, count)
    return jnp.where(place < (count + 1) // 2, 2 * place, 2 * (count - 1 - place) + 1)


def greet(devices):
    barrier = pltpu.get_barrier_semaphore()
    for device in devices:
        pl.semaphore_signal(barrier, inc=1, device_id=device, device_id_type=MESH)
    pl.semaphore_wait(barrier, len(devices))


def remote(src, dst, send, recv, device):
    return pltpu.make_async_remote_copy(
        src_ref=src, dst_ref=dst, send_sem=send, recv_sem=recv, device_id=device,
        device_id_type=MESH,
    )


def here(count):
    section, dp, core = (lax.axis_index(name) for name in ("section", "dp", "expert"))
    place = place_of(dp, count)
    right = (section, index_at(place + 1, count), core)
    left = (section, index_at(place - 1, count), core)
    return dp, core, place, right, left, (section, dp, 1 - core)


def dp_peers(count):
    section, dp, core = (lax.axis_index(name) for name in ("section", "dp", "expert"))
    return [(section, lax.rem(dp + by, count), core) for by in range(1, count)]


def comm_params(identity, vmem=48):
    return pltpu.CompilerParams(
        collective_id=identity, has_side_effects=True, vmem_limit_bytes=vmem * MIB
    )


anywhere = pl.BlockSpec(memory_space=pl.ANY)
in_vmem = pl.BlockSpec(memory_space=pltpu.VMEM)
dma = pltpu.SemaphoreType.DMA


def gelu_parts(x):
    scale, cubic = 0.7978845608028654, 0.044715
    square = x * x
    t = jnp.tanh(scale * x * (1.0 + cubic * square))
    act = 0.5 * x * (1.0 + t)
    slope = 0.5 * (1.0 + t) + 0.5 * x * (1.0 - t * t) * scale * (1.0 + 3.0 * cubic * square)
    return act, slope


def own_expert(rows, each_rows, hidden):
    each = each_rows // CAP
    row = lax.broadcasted_iota(jnp.int32, (rows, 1), 0)
    for _ in range(rows // each_rows - 1):
        row = jnp.where(row >= each_rows, row - each_rows, row)
    column = lax.broadcasted_iota(jnp.int32, (1, hidden), 1)
    row_expert, column_expert = jnp.zeros_like(row), jnp.zeros_like(column)
    for e in range(1, each):
        row_expert = row_expert + (row >= e * CAP).astype(jnp.int32)
        column_expert = column_expert + (column >= e * (hidden // each)).astype(jnp.int32)
    return row_expert == column_expert


def mm(a, b, dims):
    return lax.dot_general(a, b, (dims, ((), ())), preferred_element_type=f32)


class Round:
    def __init__(self, count, own, held, work, part, out, scratch):
        self.own, self.held, self.work, self.part, self.out = own, held, work, part, out
        self.slots, (self.total, self.pair_in, self.pair_sems) = scratch[:4], scratch[4:7]
        self.sems, self.back_sems, self.local_sem = scratch[7:9], scratch[9:11], scratch[11]
        self.count, self.reach = count, count // 2
        self.dp, self.core, self.place, right, left, self.partner = here(count)
        self.towards = (right, left)

    def source(self, way, k):
        return index_at(self.place - k if way == 0 else self.place + k, self.count)

    def hop(self, way, k, half, src=None):
        sem = self.sems[way]
        slot = self.held.at[self.source(way, k), self.core if half == 0 else 1 - self.core]
        return remote(
            slot if src is None else src, slot, sem.at[0, k, half], sem.at[1, k, half],
            self.towards[way],
        )

    def first(self, half):
        return self.own.at[self.core] if half == 0 else None

    def swap(self):
        return remote(
            self.own.at[1 - self.core], self.held.at[self.dp, self.core], self.pair_sems.at[0, 0],
            self.pair_sems.at[1, 0], self.partner,
        )

    def keep(self):
        return pltpu.make_async_copy(
            self.own.at[self.core], self.held.at[self.dp, self.core], self.local_sem
        )

    def begin(self):
        self.swap().start()
        self.keep().start()
        for way in range(2):
            if self.reach > 1 or way == 0:
                self.hop(way, 0, 0, self.first(0)).start()

    def begin_other(self):
        self.swap().wait_recv()
        for way in range(2):
            if self.reach > 1 or way == 1:
                self.hop(way, 0, 1).start()
        self.keep().wait()

    def further(self, k):
        for half in range(2):
            for way in range(2):
                self.hop(way, k - 1, half).wait_recv()
                if half == way:
                    self.hop(way, k, half).start()
                else:

                    @pl.when(k < self.reach - 1)
                    def _(way=way, half=half):
                        self.hop(way, k, half).start()

    def arrive(self):
        for way in range(2):
            self.hop(way, self.reach - 1, way).wait_recv()

    def back(self, way, k, half):
        sem = self.back_sems[way]
        return remote(
            self.slots[way].at[k, half], self.slots[way + 2].at[k, half], sem.at[0, k, half],
            sem.at[1, k, half], self.towards[way],
        )

    def begin_back(self):
        for way in range(2):
            self.slots[way + 2][0, 1 - way] = jnp.zeros(self.slots[0].shape[2:], bf16)
            self.slots[way][0, way] = self.part[self.source(way, self.reach), way]
            self.back(way, 0, way).start()

    def nearer(self, k):
        for half in range(2):
            for way in range(2):
                owner = self.source(1 - way, self.reach - k)
                piece = self.part[owner, half].astype(f32)
                if half == way:
                    self.back(way, k - 1, half).wait_recv()
                else:

                    @pl.when(k > 1)
                    def _(way=way, half=half):
                        self.back(way, k - 1, half).wait_recv()

                before = self.slots[way + 2][k - 1, half].astype(f32)
                self.slots[way][k, half] = (piece + before).astype(bf16)
                self.back(way, k, half).start()

    def swap_back(self):
        return remote(
            self.total.at[1 - self.core], self.pair_in, self.pair_sems.at[0, 1], self.pair_sems.at[1, 1],
            self.partner,
        )

    def sum_up(self):
        for half in range(2):
            value = self.part[self.dp, half].astype(f32)
            for way in range(2):
                if self.reach > 1 or half == way:
                    self.back(way, self.reach - 1, half).wait_recv()
                    value = value + self.slots[way + 2][self.reach - 1, half].astype(f32)
            self.total[half] = value.astype(bf16)
        self.swap_back().start()

    def end(self):
        self.out[self.core] = self.total[self.core]
        self.swap_back().wait_recv()
        self.out[1 - self.core] = self.pair_in[...]
        self.swap().wait_send()
        self.swap_back().wait_send()

    def finish(self, k):
        for half in range(2):
            for way in range(2):
                if half == way:
                    self.hop(way, k, half, self.first(half)).wait_send()
                    self.back(way, k, half).wait_send()
                else:

                    @pl.when(k < self.reach - 1)
                    def _(way=way, half=half):
                        self.hop(way, k, half, self.first(half)).wait_send()

                    @pl.when(k > 0)
                    def _(way=way, half=half):
                        self.back(way, k, half).wait_send()


def go_round(rounds):
    reach = rounds[0].reach

    def steps(from_step, step):
        def body(k, unused):
            step(k)
            return unused

        lax.fori_loop(from_step, reach, body, 0)

    for one in rounds:
        one.begin()
    for one in rounds:
        one.begin_other()
    for one in rounds:
        one.work([one.dp])

    def further(k):
        for one in rounds:
            one.further(k)
        for one in rounds:
            one.work([one.source(0, k), one.source(1, k)])

    steps(1, further)
    for one in rounds:
        one.arrive()
        one.work([one.source(0, reach)])
        one.begin_back()

    def nearer(k):
        for one in rounds:
            one.nearer(k)

    steps(1, nearer)
    for one in rounds:
        one.sum_up()
    for one in rounds:
        one.end()

    def finish(k):
        for one in rounds:
            one.finish(k)

    steps(0, finish)


def rows_of(held, sources):
    pieces = [held[s].reshape(-1, held.shape[-1]) for s in sources]
    return pieces[0] if len(pieces) == 1 else jnp.concatenate(pieces, 0)


def put_rows(ref, sources, value):
    size = value.shape[0] // len(sources)
    for i, s in enumerate(sources):
        ref[s] = value[i * size : (i + 1) * size].reshape(ref.shape[1:]).astype(ref.dtype)


def block_at(section, index, count):
    index = lax.rem(index + 2 * count, 2 * count)
    return section, lax.div(index, 2), lax.rem(index, 2)


def experts_kernel(count, ahead, behind, cross, *refs):
    refs = list(refs)

    def take(number):
        taken = refs[:number]
        del refs[:number]
        return taken

    if ahead:
        own, resid, table, gate = take(4)
    if behind:
        below = take(1)[0] if cross else None
        above, table_back, gate_back, arrived_hbm = take(4)
    up_hbm, down_hbm = take(2)
    if ahead:
        out, result = take(2)
        next_rows, next_halo = take(2) if cross else (None, None)
        (arrived_out,) = take(1)
    if behind:
        upstream_out, out_back, given_out, hidden_out, slope_out = take(5)
    up, down, load_sems = take(3)
    section = lax.axis_index("section")
    dp, core, place, right, left, partner = here(count)
    block = 2 * dp + core
    across, before, after = (block_at(1 - section, block + by, count) for by in (0, -1, 1))
    greet([right, left, partner] + [across] * cross + [before] * (cross and ahead))
    loads = [
        pltpu.make_async_copy(up_hbm, up, load_sems.at[0]),
        pltpu.make_async_copy(down_hbm, down, load_sems.at[1]),
    ]
    rounds = []
    if ahead:
        held, part = take(2)
        landed, landed_halo, cross_sems = take(3) if cross else (None, None, None)
        scratch = take(12)
        (save_sem,) = take(1)

        def work(sources):
            pre = mm(rows_of(held, sources), up[...], ((1,), (0,)))
            mask = own_expert(pre.shape[0], held.shape[2], pre.shape[1])
            hidden = jnp.where(mask, gelu_parts(pre)[0], 0.0).astype(bf16)
            put_rows(part, sources, mm(hidden, down[...], ((1,), (0,))))

        rounds.append(Round(count, own, held, work, part, out, scratch))
    if behind:
        own_back, held_back, arrived, hidden_all, slope_all, part_back = take(6)
        landed_back, cross_back = take(2) if cross else (None, None)
        scratch_back = take(12)
        (back_sems,) = take(1)
        loads.append(pltpu.make_async_copy(arrived_hbm, arrived, back_sems.at[0]))

        def work_back(sources):
            pre = mm(rows_of(arrived, sources), up[...], ((1,), (0,)))
            mask = own_expert(pre.shape[0], held_back.shape[2], pre.shape[1])
            act, slope = gelu_parts(pre)
            put_rows(hidden_all, sources, jnp.where(mask, act, 0.0))
            d_hidden = mm(rows_of(held_back, sources), down[...], ((1,), (1,)))
            d_pre = jnp.where(mask, d_hidden * slope, 0.0).astype(bf16)
            put_rows(slope_all, sources, d_pre)
            put_rows(part_back, sources, mm(d_pre, up[...], ((1,), (1,))))

        rounds.append(Round(count, own_back, held_back, work_back, part_back, out_back, scratch_back))
    if behind:
        if cross:
            crossing = remote(below, landed_back, cross_back.at[0], cross_back.at[1], across)
            crossing.start()
    for load in loads:
        load.start()
    if behind:
        upstream = above[...].astype(f32)
        if cross:
            crossing.wait_recv()
            upstream = jnp.where(section == 1, upstream, landed_back[...].astype(f32))
        upstream_out[...] = upstream.astype(bf16)
        slots_grad = mm(table_back[...], (upstream * gate_back[...]).astype(bf16), ((1,), (0,)))
        own_back[...] = slots_grad.astype(bf16).reshape(own_back.shape)
    waiting = list(loads)
    for one in rounds:

        def work_first(sources, work=one.work):
            while waiting:
                waiting.pop().wait()
            work(sources)

        one.work = work_first
    go_round(rounds)
    saves = []
    if ahead:
        saves.append(pltpu.make_async_copy(held, arrived_out, save_sem))
    if behind:
        for n, (src, dst) in enumerate(
            ((held_back, given_out), (hidden_all, hidden_out), (slope_all, slope_out))
        ):
            saves.append(pltpu.make_async_copy(src, dst, back_sems.at[1 + n]))
    for save in saves:
        save.start()
    if ahead:
        returned = out[...].reshape(-1, out.shape[2])
        combined = mm(table[...], returned, ((1,), (0,))) * gate[...]
        result[...] = (resid[...] + combined).astype(bf16)
    if ahead and cross:
        length, halo = result.shape[0], next_halo.shape[0]
        copies = [
            remote(result, landed, cross_sems.at[0, 0], cross_sems.at[1, 0], across),
            remote(
                result.at[length - halo : length], landed_halo, cross_sems.at[0, 1], cross_sems.at[1, 1], after
            ),
        ]
        for copy in copies:
            copy.start()
        for copy in copies:
            copy.wait_recv()
        next_rows[...] = landed[...]
        next_halo[...] = jnp.where(block > 0, landed_halo[...].astype(f32), 0.0).astype(bf16)
        for copy in copies:
            copy.wait_send()
    if behind and cross:
        crossing.wait_send()
    for save in saves:
        save.wait()


def experts(up, down, ahead, behind, cross):
    count = lax.axis_size("dp")
    reach = count // 2
    width = (ahead[1] if ahead else behind[-4]).shape[1]
    length = (ahead[1] if ahead else behind[-4]).shape[0]
    rows = (2, EXPERTS * CAP // 2, width)
    gathered = (count,) + rows
    units = (count, 2 * rows[1], up.shape[1])
    around = (
        [pltpu.VMEM((reach,) + rows, bf16)] * 4
        + [pltpu.VMEM(rows, bf16), pltpu.VMEM(rows[1:], bf16), dma((2, 2))]
        + [dma((2, reach, 2))] * 4
        + [dma(())]
    )
    in_specs, out_specs, shapes, scratch = [], [], [], []
    if ahead:
        landing = [(length, width), (HALO, width)] if cross else []
        in_specs += [in_vmem] * 4
        out_specs += [in_vmem] * (2 + len(landing)) + [anywhere]
        shapes += [rows, (length, width)] + landing + [gathered]
        scratch += [pltpu.VMEM(gathered, bf16)] * 2 + [pltpu.VMEM(shape, bf16) for shape in landing]
        scratch += [dma((2, 2))] * cross + around + [dma(())]
    if behind:
        in_specs += [in_vmem] * (len(behind) - 1) + [anywhere]
        out_specs += [in_vmem] * 2 + [anywhere] * 3
        shapes += [(length, width), rows, gathered, units, units]
        scratch += [pltpu.VMEM(rows, bf16)] + [pltpu.VMEM(gathered, bf16)] * 2
        scratch += [pltpu.VMEM(units, bf16)] * 2 + [pltpu.VMEM(gathered, bf16)]
        scratch += [pltpu.VMEM((length, width), bf16), dma((2,))] if cross else []
        scratch += around + [dma((4,))]
    number = 7 if ahead and behind else 1 if ahead else 2
    number += 0 if cross or number == 7 else 7
    return pl.pallas_call(
        functools.partial(experts_kernel, count, bool(ahead), bool(behind), cross),
        in_specs=in_specs + [anywhere] * 2,
        out_specs=out_specs,
        out_shape=[shape_of(*shape, dtype=bf16) for shape in shapes],
        scratch_shapes=[pltpu.VMEM(up.shape, bf16), pltpu.VMEM(down.shape, bf16), dma((2,))] + scratch,
        compiler_params=comm_params(number, 60),
        name="experts_both" if number == 7 else "experts_forward" if ahead else "experts_backward",
    )(*(ahead or ()), *(behind or ()), up, down)


def grid_here(count):
    section, dp, core = (lax.axis_index(name) for name in ("section", "dp", "expert"))
    a, b = lax.div(dp, 2), lax.rem(dp, 2)
    line = count // 2

    def at(place):
        return section, 2 * lax.rem(place + line, line) + b, core

    return a, b, core, at(a + 1), at(a - 1), (section, 2 * a + 1 - b, core), (section, dp, 1 - core)


def weights_gather_kernel(count, parts, tokens, wide_up, wide_down, *refs):
    own, refs = refs[:parts], refs[parts:]
    (halos, up_out, low_down), out, refs = refs[:3], refs[3 : parts + 3], refs[parts + 3 :]
    buffer_up, buffer_down, rounded_up, rounded_down, load_sems, up_sems = refs[:6]
    after_sems, before_sems, side_sems, pair_sems, local_sems, halo_sems = refs[6:]
    a, b, core, after, before, beside, partner = grid_here(count)
    line = count // 2
    section, block = lax.axis_index("section"), 2 * (2 * a + b) + core
    greet(dp_peers(count) + [partner, block_at(section, block - 1, count)])
    micro, length = tokens.shape[:2]
    ends = [
        remote(
            tokens.at[m, length - HALO : length], halos.at[m], halo_sems.at[0, m], halo_sems.at[1, m],
            block_at(section, block + 1, count),
        )
        for m in range(micro)
    ]
    for copy in ends:
        copy.start()

    def slot(p, place, which):
        return out[p].at[core, 2 * place + which]

    def source(p, place, k):
        return own[p] if isinstance(k, int) and k == 0 else slot(p, place, b)

    def along(way, k, p):
        place = a - k if way == 0 else a + k
        sems = after_sems if way == 0 else before_sems
        return remote(
            source(p, place, k), slot(p, place, b), sems.at[0, k, p], sems.at[1, k, p],
            after if way == 0 else before,
        )

    def aside(place, k, p):
        return remote(
            source(p, place, k), slot(p, place, b), side_sems.at[0, place, p], side_sems.at[1, place, p],
            beside,
        )

    def across(place, which, k, p):
        src = source(p, place, k) if which is b else slot(p, place, which)
        number = 2 * place + which
        return remote(
            src, slot(p, place, which), pair_sems.at[0, number, p], pair_sems.at[1, number, p], partner
        )

    def has(way, k):
        return a - k >= 0 if way == 0 else a + k < line

    def goes(way):
        return a + 1 < line if way == 0 else a >= 1

    for p in range(parts):
        aside(a, 0, p).start()
        for way in range(2):

            @pl.when(goes(way))
            def _(way=way, p=p):
                along(way, 0, p).start()

    keeps = [
        pltpu.make_async_copy(own[p], slot(p, a, b), local_sems.at[p]) for p in range(parts)
    ]
    for p in range(parts):
        across(a, b, 0, p).start()
        keeps[p].start()
    loads = [
        pltpu.make_async_copy(wide_up, buffer_up, load_sems.at[0]),
        pltpu.make_async_copy(wide_down, buffer_down, load_sems.at[1]),
    ]
    save = pltpu.make_async_copy(rounded_down, low_down, load_sems.at[2])
    for load in loads:
        load.start()
    loads[0].wait()
    each, depth, hidden = wide_up.shape
    cut = hidden // count
    for piece in range(count):
        for e in range(each):
            rounded_up[piece, :, e * cut : (e + 1) * cut] = buffer_up[
                e, :, piece * cut : (piece + 1) * cut
            ].astype(bf16)
    start, end = exchange(count, rounded_up, up_out, up_sems, load_sems.at[3])
    start(0)
    start(1)
    loads[1].wait()

    def rounding(e, unused):
        rounded_down[e] = buffer_down[e].astype(bf16)
        return unused

    lax.fori_loop(0, each, rounding, 0)
    save.start()

    def came_aside(place, p):
        aside(place, None, p).wait_recv()
        across(place, 1 - b, None, p).start()

    def arrivals(k, unused):
        for p in range(parts):
            for way in range(2):

                @pl.when(has(way, k))
                def _(way=way, p=p):
                    place = a - k if way == 0 else a + k
                    along(way, k - 1, p).wait_recv()

                    @pl.when(goes(way))
                    def _():
                        along(way, k, p).start()

                    aside(place, None, p).start()
                    across(place, b, None, p).start()

        for p in range(parts):

            @pl.when(k == 1)
            def _(p=p):
                came_aside(a, p)

            for way in range(2):

                @pl.when((k > 1) & has(way, k - 1))
                def _(way=way, p=p):
                    came_aside(a - k + 1 if way == 0 else a + k - 1, p)

        return unused

    lax.fori_loop(1, line, arrivals, 0)
    for p in range(parts):
        if line == 1:
            came_aside(a, p)
        for way in range(2):

            @pl.when((line > 1) & has(way, line - 1))
            def _(way=way, p=p):
                came_aside(a - line + 1 if way == 0 else a + line - 1, p)

    for p in range(parts):
        keeps[p].wait()

    def finish(place, unused):
        for p in range(parts):
            for which in range(2):
                copy = across(place, which, None, p)
                copy.wait_recv()
                copy.wait_send()
            aside(place, None, p).wait_send()
        return unused

    lax.fori_loop(0, line, finish, 0)

    def sent(k, unused):
        for p in range(parts):
            for way in range(2):

                @pl.when(has(way, k) & goes(way))
                def _(way=way, p=p):
                    along(way, k, p).wait_send()

        return unused

    lax.fori_loop(0, line, sent, 0)
    save.wait()
    end()
    for copy in ends:
        copy.wait()


def weights_gather(tokens, up, down, own):
    count = lax.axis_size("dp")
    reach = count // 2
    parts = len(own)
    pieces = (count, up.shape[1], up.shape[0] * up.shape[2] // count)
    return pl.pallas_call(
        functools.partial(weights_gather_kernel, count, parts),
        in_specs=[anywhere] * (parts + 3),
        out_specs=[anywhere] * (parts + 3),
        out_shape=[shape_of(tokens.shape[0], HALO, tokens.shape[2], dtype=bf16)]
        + [shape_of(*pieces, dtype=bf16), shape_of(*down.shape, dtype=bf16)]
        + [shape_of(2, count, *part.shape, dtype=part.dtype) for part in own],
        scratch_shapes=[
            pltpu.VMEM(up.shape, f32),
            pltpu.VMEM(down.shape, f32),
            pltpu.VMEM(pieces, bf16),
            pltpu.VMEM(down.shape, bf16),
            dma((4,)),
            dma((2, count - 1)),
            dma((2, reach, parts)),
            dma((2, reach, parts)),
            dma((2, reach, parts)),
            dma((2, count, parts)),
            dma((parts,)),
            dma((2, tokens.shape[0])),
        ],
        compiler_params=comm_params(3),
        name="weights_gather",
    )(tokens, up, down, *own)


def grads_reduce_kernel(count, micro, vec, pieces, *refs):
    refs = list(refs)

    def take(number):
        taken = refs[:number]
        del refs[:number]
        return taken

    given = [take(8) for _ in range(micro)]
    (up_out,), out = take(1), take(4)
    wholes, halves, (vecs, landed) = take(4), take(5), take(2)
    part, sides, ins = take(4), take(4), (take(4), take(4))
    whole_sems, half_sems, vec_sems, after_sems, before_sems, side_sems, piece_sems, local_sem = refs
    a, b, core, after, before, beside, partner = grid_here(count)
    line = count // 2
    parts = len(part)
    half = halves[0].shape[1]
    length = given[0][0].shape[0]
    greet_all(count)

    def lanes(side, begin):
        return pl.ds(pl.multiple_of(begin + side * half, LANES), half)

    def moves_of(i, n, which):
        place, there = pl.ds(i * length, length), pl.ds((micro + i) * length, length)
        if n < 4:
            src, dst = given[i][n], wholes[n]
            if which == 0:
                return pltpu.make_async_copy(src, dst.at[place], whole_sems.at[2, i, n])
            return remote(src, dst.at[there], whole_sems.at[0, i, n], whole_sems.at[1, i, n], partner)
        n -= 4
        src, begin = (given[i][4], n * 2 * half) if n < 2 else (given[i][3 + n], 0)
        dst = halves[n]
        if which == 0:
            return pltpu.make_async_copy(
                src.at[:, lanes(core, begin)], dst.at[place], half_sems.at[2, i, n]
            )
        return remote(
            src.at[:, lanes(1 - core, begin)], dst.at[there], half_sems.at[0, i, n], half_sems.at[1, i, n],
            partner,
        )

    order = (0, 4, 5, 1, 6, 2, 7, 3, 8)
    for n in order:
        for i in range(micro):
            for which in range(2):
                moves_of(i, n, which).start()
    vec_copies = (
        pltpu.make_async_copy(vec.at[core], vecs.at[0], vec_sems.at[2]),
        remote(vec.at[1 - core], vecs.at[1], vec_sems.at[0], vec_sems.at[1], partner),
    )
    for copy in vec_copies:
        copy.start()
    start, end = exchange(count, pieces, landed, piece_sems, local_sem)
    start(0)

    def ready(n):
        for i in range(micro):
            moves_of(i, n, 0).wait()
            moves_of(i, n, 1).wait_recv()

    def aside(place, p):
        return remote(
            part[p].at[2 * place + 1 - b], sides[p].at[place], side_sems.at[0, place, p],
            side_sems.at[1, place, p], beside,
        )

    def along(way, place, p):
        sems = after_sems if way == 0 else before_sems
        return remote(
            part[p].at[2 * place + b], ins[way][p].at[place], sems.at[0, place, p], sems.at[1, place, p],
            after if way == 0 else before,
        )

    def far(way, k):
        return line - 1 - k if way == 0 else k

    def put(p, value):
        share = part[p].shape[1]
        for index in range(count):
            part[p][index] = value[index * share : (index + 1) * share].astype(bf16)

        def starts(k, unused):
            for way in range(2):

                @pl.when((way == 0) | (far(0, k) != far(1, k)))
                def _(way=way):
                    aside(far(way, k), p).start()

            return unused

        lax.fori_loop(0, (line + 1) // 2, starts, 0)

    def both_lines(place, p):
        aside(place, p).wait_recv()
        return part[p][2 * place + b].astype(f32) + sides[p][place].astype(f32)

    def passing(k, p):
        for way in range(2):
            place = far(way, k)

            @pl.when(place > a if way == 0 else place < a)
            def _(way=way, place=place):
                index = 2 * place + b
                part[p][index] = both_lines(place, p).astype(bf16)

                @pl.when(a > 0 if way == 0 else a < line - 1)
                def _():
                    along(way, place, p).wait_recv()
                    value = part[p][index].astype(f32) + ins[way][p][place].astype(f32)
                    part[p][index] = value.astype(bf16)

                along(way, place, p).start()

    over = ((0,), (0,))
    ready(0)
    ready(4)
    put(0, mm(halves[0][...], wholes[0][...], over))
    ready(5)
    put(1, mm(halves[1][...], wholes[0][...], over))
    ready(1)
    ready(6)
    put(2, mm(halves[2][...], wholes[1][...], over))
    start(1)
    for n in (2, 7, 3, 8):
        ready(n)
    vec_copies[0].wait()
    vec_copies[1].wait_recv()
    put(
        3,
        mm(halves[3][...], wholes[2][...], over)
        + mm(halves[4][...], wholes[3][...], over)
        + vecs[0].astype(f32)
        + vecs[1].astype(f32),
    )
    for p in range(parts):

        def passing_on(k, unused, p=p):
            passing(k, p)
            return unused

        lax.fori_loop(0, line - 1, passing_on, 0)
    for p in range(parts):
        out[p][...] = both_lines(a, p)
        for way in range(2):

            @pl.when(a > 0 if way == 0 else a < line - 1)
            def _(way=way, p=p):
                along(way, a, p).wait_recv()
                out[p][...] = out[p][...] + ins[way][p][a].astype(f32)

    def finish(place, unused):
        for p in range(parts):
            aside(place, p).wait_send()
            for way in range(2):

                @pl.when(place > a if way == 0 else place < a)
                def _(way=way, p=p):
                    along(way, place, p).wait_send()

        return unused

    lax.fori_loop(0, line, finish, 0)
    for n in order:
        for i in range(micro):
            moves_of(i, n, 1).wait_send()
    vec_copies[1].wait_send()
    end()
    each, depth, hidden = up_out.shape
    cut = hidden // count
    for piece in range(count):
        for e in range(each):
            up_out[e, :, piece * cut : (piece + 1) * cut] = landed[
                piece, :, e * cut : (e + 1) * cut
            ]


def grads_reduce(vec, pieces, given):
    count = lax.axis_size("dp")
    line = count // 2
    micro = len(given)
    length, model = given[0][0].shape
    half, lanes = vec.shape[1:]
    share = half // count
    each = EXPERTS // 2
    rows = 2 * micro * length
    shares = [(share, model)] * 3 + [(share, lanes)]
    wholes = [model, model, lanes, lanes]
    return pl.pallas_call(
        functools.partial(grads_reduce_kernel, count, micro),
        in_specs=[anywhere] * (2 + 8 * micro),
        out_specs=[in_vmem] * 5,
        out_shape=[shape_of(each, pieces.shape[1], count * pieces.shape[2] // each, dtype=bf16)]
        + [shape_of(*shape) for shape in shares],
        scratch_shapes=[pltpu.VMEM((rows, width), bf16) for width in wholes]
        + [pltpu.VMEM((rows, half), bf16)] * 5
        + [pltpu.VMEM((2, half, lanes), bf16), pltpu.VMEM(pieces.shape, bf16)]
        + [pltpu.VMEM((count,) + shape, bf16) for shape in shares]
        + [pltpu.VMEM((line,) + shape, bf16) for shape in shares] * 3
        + [dma((3, micro, 4)), dma((3, micro, 5)), dma((3,))]
        + [dma((2, line, 4))] * 3
        + [dma((2, count - 1)), dma(())],
        compiler_params=comm_params(4, 60),
        name="grads_reduce",
    )(vec, pieces, *[value for one in given for value in one])


def join(
    count, forward, state_ref, total_ref, rates, out_ref, other_state, other_total, mine, mine_total, states,
    totals, back, back_in, pair_sems, sems,
):
    section, dp, core = (lax.axis_index(name) for name in ("section", "dp", "expert"))
    partner = (section, dp, 1 - core)
    swap = [
        remote(state_ref.at[1 - core], other_state, pair_sems.at[0, 0], pair_sems.at[1, 0], partner),
        remote(total_ref.at[1 - core], other_total, pair_sems.at[0, 1], pair_sems.at[1, 1], partner),
    ]
    for copy in swap:
        copy.start()
    own_state, own_total = state_ref[core], total_ref[core]
    for copy in swap:
        copy.wait_recv()
    leads = core == (0 if forward else 1)
    first_state = jnp.where(leads, own_state, other_state[...])
    first_total = jnp.where(leads, own_total, other_total[...])
    second_state = jnp.where(leads, other_state[...], own_state)
    second_total = jnp.where(leads, other_total[...], own_total)
    mine[...] = (jnp.exp2(rates * second_total) * first_state + second_state).astype(bf16)
    mine_total[...] = first_total + second_total
    copies = []
    for d, peer in enumerate(dp_peers(count)):
        for n, (src, dst) in enumerate(((mine, states), (mine_total, totals))):
            copy = remote(src, dst.at[dp], sems.at[0, d, n], sems.at[1, d, n], peer)
            copy.start()
            copies.append(copy)
    states[dp] = mine[...]
    totals[dp] = mine_total[...]
    for copy in copies:
        copy.wait_recv()

    entering = jnp.zeros_like(own_state)
    for k in range(count):
        source = k if forward else count - 1 - k
        reached = (source < dp) if forward else (source > dp)
        fresh = jnp.exp2(rates * totals[source]) * entering + states[source].astype(f32)
        entering = jnp.where(reached, fresh, entering)
    after = jnp.exp2(rates * first_total) * entering + first_state
    back[...] = jnp.where(leads, after, entering)
    swap_back = remote(back, back_in, pair_sems.at[0, 2], pair_sems.at[1, 2], partner)
    swap_back.start()
    out_ref[core] = jnp.where(leads, entering, after)
    swap_back.wait_recv()
    out_ref[1 - core] = back_in[...]
    for copy in swap + copies + [swap_back]:
        copy.wait_send()


def join_scratch(count, states, half):
    one, sums = pltpu.VMEM((states, half), f32), pltpu.VMEM((1, half), f32)
    return [
        pltpu.VMEM((2, states, half), f32),
        pltpu.VMEM((2, 1, half), f32),
        pltpu.VMEM((2, states, half), f32),
        one,
        sums,
        pltpu.VMEM((states, half), bf16),
        sums,
        pltpu.VMEM((count, states, half), bf16),
        pltpu.VMEM((count, 1, half), f32),
        one,
        one,
        dma((2, 3)),
        dma((2, count - 1, 2)),
    ]


def own_lanes(a_ref, half):
    return a_ref[:, lanes_at(lax.axis_index("expert"), half)]


def greet_all(count):
    section, dp, core = (lax.axis_index(name) for name in ("section", "dp", "expert"))
    greet(dp_peers(count) + [(section, dp, 1 - core)])


def exchange(count, pieces_ref, out_ref, sems, local_sem):
    dp = lax.axis_index("dp")
    keep = pltpu.make_async_copy(pieces_ref.at[dp], out_ref.at[dp], local_sem)
    keep.start()
    copies = []
    for by, peer in enumerate(dp_peers(count)):
        copies.append(
            remote(pieces_ref.at[peer[1]], out_ref.at[dp], sems.at[0, by], sems.at[1, by], peer)
        )

    def start(beside):
        for copy in copies[1 - beside :: 2]:
            copy.start()

    def end():
        keep.wait()
        for copy in copies:
            copy.wait()

    return start, end


def mixer_forward_kernel(
    count, step_ref, drive_ref, bb_ref, cb_ref, a_ref, y_ref, starts_ref, state, total, entering, *rest
):
    half = state.shape[2]
    width = block_width(half, 384)
    scan_final(step_ref, drive_ref, bb_ref, a_ref, state, total, width)
    greet_all(count)
    join(count, True, state, total, own_lanes(a_ref, half), entering, *rest)
    scan_outputs(step_ref, drive_ref, bb_ref, cb_ref, a_ref, entering, y_ref, starts_ref, width)


def mixer_forward(step, drive, in_map, out_map, rates):
    count = lax.axis_size("dp")
    (length, width), states = step.shape, rates.shape[0]
    return pl.pallas_call(
        functools.partial(mixer_forward_kernel, count),
        in_specs=[in_vmem] * 5,
        out_specs=[in_vmem] * 2,
        out_shape=[shape_of(length, width), shape_of(length // CHUNK, states, width)],
        scratch_shapes=join_scratch(count, states, width // 2),
        compiler_params=comm_params(5),
        name="mixer_forward",
    )(step, drive, in_map, out_map, rates)


def mixer_backward_kernel(
    count, step_ref, drive_ref, dy_ref, bb_ref, cb_ref, a_ref, starts_ref, through_ref, flow_ref, db_ref, dc_ref,
    da_ref, state, total, inflow, *rest,
):
    half = state.shape[2]
    width = block_width(half, 384)
    scan_leak(step_ref, dy_ref, cb_ref, a_ref, state, total, width)
    greet_all(count)
    join(count, False, state, total, own_lanes(a_ref, half), inflow, *rest)
    scan_back(
        step_ref, drive_ref, dy_ref, bb_ref, cb_ref, a_ref, starts_ref, inflow, through_ref, flow_ref, db_ref,
        dc_ref, da_ref, width,
    )


def mixer_backward(step, drive, dy, in_map, out_map, rates, starts):
    count = lax.axis_size("dp")
    (length, width), states = step.shape, rates.shape[0]
    wide, maps = shape_of(length, width), shape_of(*in_map.shape)
    return pl.pallas_call(
        functools.partial(mixer_backward_kernel, count),
        in_specs=[in_vmem] * 7,
        out_specs=[in_vmem] * 5,
        out_shape=[wide, wide, maps, maps, shape_of(states, width)],
        scratch_shapes=join_scratch(count, states, width // 2),
        compiler_params=comm_params(6),
        name="mixer_backward",
    )(step, drive, dy, in_map, out_map, rates, starts)


def dot(a, b, dims, dtype=f32):
    return lax.dot_general(a, b, (dims, ((), ())), preferred_element_type=f32).astype(dtype)


def nn(a, b, dtype=f32):
    return dot(a, b, ((1,), (0,)), dtype)


def nt(a, b, dtype=f32):
    return dot(a, b, ((1,), (1,)), dtype)


def tn(a, b, dtype=f32):
    return dot(a, b, ((0,), (0,)), dtype)


def normalize(values, gain):
    return values * lax.rsqrt(jnp.mean(values * values, axis=-1, keepdims=True) + epsilon) * gain


def sums(value):
    return jnp.sum(value, 0)


def normalize_back(values, gain, upstream):
    scale = lax.rsqrt(jnp.mean(values * values, axis=-1, keepdims=True) + epsilon)
    unit = values * scale
    inner = upstream * gain
    d_values = scale * (inner - unit * jnp.mean(inner * unit, axis=-1, keepdims=True))
    return d_values, sums(upstream * unit)


def from_behind(shard, axis, by):
    count = 1
    for name in (axis,) if isinstance(axis, str) else axis:
        count *= lax.axis_size(name)
    pairs = [(i, i + by) for i in range(count) if 0 <= i + by < count]
    return lax.ppermute(shard, axis, pairs)


def swap_pair(value):
    return lax.ppermute(value, "expert", [(0, 1), (1, 0)])


def spread(values):
    return jnp.broadcast_to(values[:, :, None], values.shape + (LANES,))


def routing(resid, moe_gain, router, chosen, placed, dropped):
    normed = normalize(resid, moe_gain)
    probs = jax.nn.softmax(jnp.dot(normed, router, precision=highest), axis=-1)
    keep = (1 - dropped).astype(f32)
    pick = (chosen[:, None] == jnp.arange(EXPERTS)[None]).astype(f32)
    gate = jnp.sum(probs * pick, -1) * keep
    flat = chosen * CAP + placed
    table = ((flat[:, None] == jnp.arange(EXPERTS * CAP)[None]) & (dropped[:, None] == 0)).astype(
        bf16
    )
    return normed, probs, pick, keep, gate, table


def by_core(buffer):
    return buffer.reshape(2, -1, buffer.shape[1])


def mixed(xz, weights):
    width = weights["w_out"].shape[0]
    taps = weights["conv_w"].shape[0]
    length = xz.shape[0] - HALO
    padded = xz[HALO - taps + 1 :, :width]
    summed = weights["conv_b"]
    for tap in range(taps):
        summed = summed + weights["conv_w"][tap : tap + 1] * padded[tap : tap + length]
    return padded, summed, xz[HALO:, width:]


def selective(projected, weights):
    rank = weights["dt_proj"].shape[0]
    states = weights["rates"].shape[0]
    dt_low = projected[:, :rank].astype(bf16)
    dt_raw = nn(dt_low, weights["dt_proj"]) + weights["dt_bias"]
    in_map = projected[:, rank : rank + states]
    out_map = projected[:, rank + states : rank + 2 * states]
    return dt_low, dt_raw, jax.nn.softplus(dt_raw), spread(in_map), spread(out_map)


def forward(rows, halo, chosen, placed, dropped, weights):
    inputs = jnp.concatenate([halo, rows], 0).astype(f32)
    normed = normalize(inputs, weights["norm_gain"]).astype(bf16)
    xz = nt(normed, weights["w_in"])
    padded, summed, gate_in = mixed(xz, weights)
    signal = jax.nn.silu(summed).astype(bf16)
    projected = nn(signal, weights["x_proj"])
    dt_low, dt_raw, step, in_map, out_map = selective(projected, weights)
    wide = signal.astype(f32)
    drive = step * wide
    rates = weights["rates"] * LOG2E
    scanned, starts = mixer_forward(step, drive, in_map, out_map, rates)
    gated = ((scanned + weights["skip"] * wide) * jax.nn.silu(gate_in)).astype(bf16)
    resid = rows.astype(f32) + nn(gated, weights["w_out"])
    normed_moe, probs, pick, keep, gate, table = routing(
        resid, weights["moe_gain"], weights["router"], chosen, placed, dropped
    )
    buffer = tn(table, normed_moe.astype(bf16), bf16)
    ahead = (by_core(buffer), resid, table, gate[:, None])
    kept = dict(
        rows=rows, halo=halo, xz=xz, projected=projected, scanned=scanned, starts=starts, resid=resid,
    )
    return ahead, kept


def backward_routing(kept, chosen, placed, dropped, weights):
    return routing(
        kept["resid"], weights["moe_gain"], weights["router"], chosen, placed, dropped
    )


def backward_experts(routed, returned, upstream, d_sent, weights):
    normed_moe, probs, pick, keep, gate, table = routed
    d_sent = d_sent.reshape(-1, d_sent.shape[2])
    returned = returned.reshape(d_sent.shape)
    upstream = upstream.astype(f32)
    d_gate = jnp.sum(upstream * nn(table, returned), -1)
    d_choice = d_gate[:, None] * pick * keep[:, None]
    d_logits = probs * (d_choice - jnp.sum(probs * d_choice, -1, keepdims=True))
    d_normed = nn(table, d_sent) + jnp.dot(d_logits, weights["router"].T, precision=highest)
    return upstream, d_normed, d_logits


def backward_mixer(upstream, kept, d_normed, d_logits, weights):
    resid = kept["resid"]
    normed_moe = normalize(resid, weights["moe_gain"])
    grad_router = lax.dot_general(
        normed_moe, d_logits, (((0,), (0,)), ((), ())), precision=highest
    )
    d_norm, grad_moe = normalize_back(resid, weights["moe_gain"], d_normed)
    d_resid = upstream + d_norm

    inputs = kept["rows"].astype(f32)
    normed = normalize(inputs, weights["norm_gain"]).astype(bf16)
    xz = kept["xz"]
    padded, summed, gate_in = mixed(xz, weights)
    signal_act, signal_back = jax.vjp(jax.nn.silu, summed)
    signal = signal_act.astype(bf16)
    wide = signal.astype(f32)
    dt_low, dt_raw, step, in_map, out_map = selective(kept["projected"], weights)
    drive = step * wide
    rates = weights["rates"] * LOG2E
    skip = weights["skip"]
    total_out = kept["scanned"] + skip * wide
    gate_act, gate_back = jax.vjp(jax.nn.silu, gate_in)
    gated = (total_out * gate_act).astype(bf16)
    d_mixer = d_resid.astype(bf16)
    d_gated = nt(d_mixer, weights["w_out"])
    d_total = d_gated * gate_act
    d_gate_in = gate_back(d_gated * total_out)[0]
    grad_skip = sums(d_total * wide)
    through, flow, d_in_map, d_out_map, d_rates = mixer_backward(
        step, drive, d_total, in_map, out_map, rates, kept["starts"]
    )
    d_step = flow / LOG2E + through * wide
    d_signal = step * through + d_total * skip
    d_raw = d_step * jax.nn.sigmoid(dt_raw)
    grad_dt_bias = sums(d_raw)
    d_raw_low = d_raw.astype(bf16)
    d_low = nt(d_raw_low, weights["dt_proj"])
    d_projected = jnp.concatenate(
        [d_low, jnp.sum(d_in_map, -1), jnp.sum(d_out_map, -1)], 1
    ).astype(bf16)
    d_signal = d_signal + nt(d_projected, weights["x_proj"])
    d_summed = signal_back(d_signal)[0]
    taps = weights["conv_w"].shape[0]
    length = d_summed.shape[0]
    ahead = from_behind(d_summed[:8], ("dp", "expert"), -1)
    extended = jnp.concatenate([d_summed, ahead], 0)
    d_conv_in = jnp.zeros_like(d_summed)
    for tap in range(taps):
        begin = taps - 1 - tap
        d_conv_in = d_conv_in + weights["conv_w"][tap : tap + 1] * extended[begin : begin + length]
    grad_conv = [
        sums(d_summed * padded[tap : tap + length]) for tap in range(taps)
    ]
    d_xz = jnp.concatenate([d_conv_in, d_gate_in], 1).astype(bf16)
    d_normed_in = nn(d_xz, weights["w_in"])
    d_inputs, grad_norm = normalize_back(inputs, weights["norm_gain"], d_normed_in)
    result = (d_resid + d_inputs).astype(bf16)
    low, rank = d_projected.shape[1], dt_low.shape[1]
    lanes = (-sum(weights["sizes"])) % LANES + sum(weights["sizes"])
    given = (
        normed,
        d_mixer,
        jnp.pad(d_projected, ((0, 0), (0, lanes - low))),
        jnp.pad(dt_low, ((0, 0), (low, lanes - low - rank))),
        d_xz,
        gated,
        signal,
        d_raw_low,
    )
    vectors = (
        grad_conv + [sums(d_summed), grad_dt_bias, grad_skip], d_rates * weights["rates"],
        [grad_norm, grad_moe], grad_router,
    )
    return result, given, vectors


def gather_weights(
    tokens, norm_gain, w_in, conv_w, conv_b, x_proj, dt_proj, dt_bias, a_log, skip, w_out, moe_gain, router,
    w_up, w_down,
):
    count = lax.axis_size("dp")
    share = x_proj.shape[1]
    model = w_out.shape[2]
    low_in = jnp.transpose(w_in[0].astype(bf16), (1, 2, 0))
    pieces = [
        x_proj[0], dt_proj[0].T, conv_w[0].T, conv_b[0][:, None], dt_bias[0][:, None],
        skip[0][:, None], a_log[0].T, norm_gain[0][:, None], moe_gain[0][:, None], router[0],
    ]
    sizes = [piece.shape[1] for piece in pieces]
    pad = (-sum(sizes)) % LANES
    small = jnp.concatenate(pieces + [jnp.zeros((share, pad), f32)], 1).astype(bf16)
    halos, up, low_down, in_x, in_z, out, small = weights_gather(
        tokens, w_up[0], w_down[0], [low_in[0], low_in[1], w_out[0].astype(bf16), small]
    )
    width = 2 * count * share
    w_in_all = jnp.concatenate([in_x.reshape(width, model), in_z.reshape(width, model)], 0)
    table = small.reshape(width, -1)
    rows = table.astype(f32).T
    at = 0
    found = []
    for size in sizes:
        found.append(rows[at : at + size])
        at += size
    unused, dt_proj, conv_w, conv_b, dt_bias, a_skip, a_log, norm_gain, moe_gain, router = found
    weights = dict(
        sizes=sizes,
        w_in=w_in_all,
        w_out=out.reshape(width, model),
        x_proj=table[:, : sizes[0]],
        dt_proj=dt_proj.astype(bf16),
        conv_w=conv_w,
        conv_b=conv_b,
        dt_bias=dt_bias,
        skip=a_skip,
        rates=-jnp.exp(a_log),
        norm_gain=norm_gain[:, :model],
        moe_gain=moe_gain[:, :model],
        router=router[:, :model].T,
        w_up=up.reshape(-1, up.shape[2]),
        w_down=low_down.reshape(-1, model),
    )
    return weights, sizes, halos


def mixer_grads(given, vectors, sizes, up, count):
    channel, d_rates, feature, grad_router = vectors
    feature = jnp.concatenate([piece[None] for piece in feature] + [grad_router.T], 0)
    rows = jnp.concatenate(
        [piece[None] for piece in channel] + [d_rates, jnp.concatenate([feature, feature], 1)], 0
    )
    begin = sizes[0] + sizes[1]
    lanes = -(-sum(sizes) // LANES) * LANES
    vec = jnp.pad(rows.T.astype(bf16), ((0, 0), (begin, lanes - begin - rows.shape[0])))
    vec = vec.reshape(2, -1, lanes)
    up, grad_x, grad_z, grad_out, small = grads_reduce(vec, up, given)
    at = 0
    found = []
    for size in sizes:
        found.append(small[:, at : at + size])
        at += size
    x_proj, dt_proj, conv_w, conv_b, dt_bias, skip, a_log, norm_gain, moe_gain, router = found
    return (
        norm_gain[:, 0],
        jnp.transpose(jnp.stack([grad_x, grad_z], 0), (2, 0, 1)),
        conv_w.T,
        conv_b[:, 0],
        x_proj,
        dt_proj.T,
        dt_bias[:, 0],
        a_log.T,
        skip[:, 0],
        grad_out,
        moe_gain[:, 0],
        router,
        up.astype(f32),
    )


def rows_flat(value):
    return value.reshape(-1, value.shape[-1])


def down_grad(first, second):
    hidden, d_produced = (
        jnp.concatenate([rows_flat(a), rows_flat(b)], 0)
        for a, b in zip(first, second, strict=True)
    )
    return tn(hidden, d_produced).reshape(EXPERTS // 2, -1, d_produced.shape[1])


def up_pieces(first, second, count):
    arrived, d_pre = (
        jnp.concatenate([rows_flat(a), rows_flat(b)], 0)
        for a, b in zip(first, second, strict=True)
    )
    return tn(arrived, d_pre, bf16).reshape(count, arrived.shape[1] // count, -1)


def shards(
    tokens, cotangent, routes, slots, drops, norm_gain, w_in, conv_w, conv_b, x_proj, dt_proj, dt_bias,
    a_log, skip, w_out, moe_gain, router, w_up, w_down,
):
    count = lax.axis_size("dp")
    section = lax.axis_index("section")
    top = section == 1
    weights, sizes, halos = gather_weights(
        tokens, norm_gain, w_in, conv_w, conv_b, x_proj, dt_proj, dt_bias, a_log, skip, w_out, moe_gain,
        router, w_up, w_down,
    )
    micro = tokens.shape[0]
    blocks = ("dp", "expert")
    steps = micro + 1

    def pick(which):
        return [lax.dynamic_index_in_dim(v[0], which, 0, False) for v in (routes, slots, drops)]

    begins = (lax.axis_index("dp") == 0) & (lax.axis_index("expert") == 0)
    halos = jnp.where(begins, jnp.zeros_like(halos), halos)
    incoming, incoming_halo = jnp.zeros_like(tokens[0]), jnp.zeros_like(halos[0])
    results, bank, grads, found, last = [], [], [], [], []
    below = None

    def micro_of(step, first):
        return jnp.clip(step - first, 0, micro - 1)

    def back_parts(step):
        if step == 1:
            kept = jax.tree.map(lambda a, b: jnp.where(top, a, b), bank[2], bank[0])
        else:
            kept = bank[1]
        routed = backward_routing(kept, *pick(micro_of(step, 1 - section)), weights)
        above = cotangent[step] if step < micro else jnp.zeros_like(cotangent[0])
        above = jnp.where(top, above, jnp.zeros_like(above))
        crossing = () if below is None else (below,)
        return kept, routed, crossing + (above, routed[5].T, routed[4][:, None], kept["arrived"])

    for step in range(2 * steps - 1):
        ahead = behind = None
        if step < steps:
            fresh = min(step, micro - 1)
            rows = jnp.where(top, incoming, tokens[fresh])
            halo = jnp.where(top, incoming_halo, halos[fresh])
            ahead, fresh_kept = forward(rows, halo, *pick(micro_of(step, section)), weights)
        if step >= steps - 1:
            kept, routed, behind = back_parts(step - steps + 1)
        cross = (ahead is None) != (behind is None)
        if cross or count <= 8:
            done = experts(weights["w_up"], weights["w_down"], ahead, behind, cross)
        else:
            done = experts(weights["w_up"], weights["w_down"], ahead, None, False)
            done = [*done, *experts(weights["w_up"], weights["w_down"], None, behind, False)]
        if ahead is not None:
            fresh_kept["returned"], result = done[:2]
            if cross:
                incoming, incoming_halo = done[2:4]
            number = 5 if cross else 3
            fresh_kept["arrived"] = done[number - 1]
            results.append(result)
            bank.append(fresh_kept)
            done = done[number:]
        if behind is not None:
            upstream, d_sent, d_produced, hidden, d_pre = done
            last.append((hidden, d_produced, kept["arrived"], d_pre))
            upstream, d_normed, d_logits = backward_experts(
                routed, kept["returned"], upstream, d_sent, weights
            )
            if len(last) == steps:
                one = jax.tree.map(lambda a, b: jnp.where(top, a, b), last[0], last[2])
                moving = up_pieces(one[2:], last[1][2:], count)
            below, *pieces = backward_mixer(upstream, kept, d_normed, d_logits, weights)
            grads.append(below)
            found.append(pieces)
    outputs = jnp.stack(
        [jnp.where(top, results[m + 1], results[m]) for m in range(micro)], 0
    )
    backs = jnp.stack([jnp.where(top, grads[m], grads[m + 1]) for m in range(micro)], 0)

    def valid_one(place):
        return jax.tree.map(lambda a, b: jnp.where(top, a, b), found[0][place], found[2][place])

    vectors = jax.tree.map(lambda a, b: a + b, valid_one(1), found[1][1])
    mixer = mixer_grads([valid_one(0), found[1][0]], vectors, sizes, moving, count)
    down = down_grad(one[:2], last[1][:2])
    return (outputs[None], backs[None]) + tuple(v[None] for v in mixer) + (down[None],)


def solution(mesh):
    both = ("dp", "expert")
    weights = (
        P("section", "dp"),
        P("section", None, None, both),
        P("section", None, both),
        P("section", both),
        P("section", both, None),
        P("section", None, both),
        P("section", both),
        P("section", None, both),
        P("section", both),
        P("section", both, None),
        P("section", "dp"),
        P("section", "dp", None),
        P("section", "expert", "dp", None),
        P("section", "expert", "dp", None),
    )
    return jax.shard_map(
        shards,
        mesh=mesh,
        in_specs=(P(None, both, None),) * 2 + (P("section", None, both),) * 3 + weights,
        out_specs=(P("section", None, both, None),) * 2 + weights,
        check_vma=False,
    )
```

```python
import functools

import jax
import jax.numpy as jnp
from jax import lax
from jax.experimental import pallas as pl
from jax.experimental.pallas import tpu as pltpu
from jax.sharding import PartitionSpec as P

EXPERTS = 8
CAP = 12
LANES = 128
CHUNK = 8
HALO = 16
LOG2E = 1.4426950408889634
MESH = pl.DeviceIdType.MESH
MIB = 2**20

epsilon = 1e-05
highest = lax.Precision.HIGHEST
f32 = jnp.float32
bf16 = jnp.bfloat16


def tiles_of(width):
    return [slice(i * LANES, (i + 1) * LANES) for i in range(width // LANES)]


def lanes_at(block, width):
    return pl.ds(pl.multiple_of(block * width, LANES), width)


def scan_final(step_ref, drive_ref, bb_ref, a_ref, state, total, width):
    states = a_ref.shape[0]
    tiles = tiles_of(width)
    each = state.shape[2] // width

    def block(b, unused):
        lanes = lanes_at(b, width)
        rates = [a_ref[:, lanes][:, t] for t in tiles]

        def body(i, carry):
            base = pl.multiple_of(i * CHUNK, CHUNK)
            step = step_ref[pl.ds(base, CHUNK), lanes]
            drive = drive_ref[pl.ds(base, CHUNK), lanes]
            carry, sums = list(carry[0]), carry[1]
            for k in range(CHUNK):
                in_map = bb_ref[base + k]
                for j, t in enumerate(tiles):
                    decay = jnp.exp2(step[k : k + 1, t] * rates[j])
                    carry[j] = decay * carry[j] + drive[k : k + 1, t] * in_map
            return tuple(carry), sums + step

        zeros = tuple(jnp.zeros((states, LANES), f32) for _ in tiles)
        final, sums = lax.fori_loop(
            0, step_ref.shape[0] // CHUNK, body, (zeros, jnp.zeros((CHUNK, width), f32))
        )
        side, at = lax.div(b, each), lanes_at(lax.rem(b, each), width)
        state[side, :, at] = jnp.concatenate(final, 1)
        total[side, :, at] = jnp.sum(sums, 0, keepdims=True)
        return unused

    lax.fori_loop(0, 2 * each, block, 0)


def scan_leak(step_ref, dy_ref, cb_ref, a_ref, state, total, width):
    states = a_ref.shape[0]
    tiles = tiles_of(width)
    each = state.shape[2] // width
    count = step_ref.shape[0] // CHUNK

    def block(b, unused):
        lanes = lanes_at(b, width)
        rates = [a_ref[:, lanes][:, t] for t in tiles]

        def body(i, carry):
            base = pl.multiple_of((count - 1 - i) * CHUNK, CHUNK)
            step = step_ref[pl.ds(base, CHUNK), lanes]
            dys = dy_ref[pl.ds(base, CHUNK), lanes]
            carry, sums = list(carry[0]), carry[1]
            for k in reversed(range(CHUNK)):
                out_map = cb_ref[base + k]
                for j, t in enumerate(tiles):
                    decay = jnp.exp2(step[k : k + 1, t] * rates[j])
                    carry[j] = decay * (carry[j] + dys[k : k + 1, t] * out_map)
            return tuple(carry), sums + step

        zeros = tuple(jnp.zeros((states, LANES), f32) for _ in tiles)
        final, sums = lax.fori_loop(0, count, body, (zeros, jnp.zeros((CHUNK, width), f32)))
        side, at = lax.div(b, each), lanes_at(lax.rem(b, each), width)
        state[side, :, at] = jnp.concatenate(final, 1)
        total[side, :, at] = jnp.sum(sums, 0, keepdims=True)
        return unused

    lax.fori_loop(0, 2 * each, block, 0)


def scan_outputs(step_ref, drive_ref, bb_ref, cb_ref, a_ref, entering, y_ref, starts_ref, width):
    tiles = tiles_of(width)
    each = entering.shape[2] // width

    def block(b, unused):
        lanes = lanes_at(b, width)
        rates = [a_ref[:, lanes][:, t] for t in tiles]

        def body(i, carry):
            base = pl.multiple_of(i * CHUNK, CHUNK)
            step = step_ref[pl.ds(base, CHUNK), lanes]
            drive = drive_ref[pl.ds(base, CHUNK), lanes]
            carry = list(carry)
            starts_ref[i, :, lanes] = jnp.concatenate(carry, 1)
            rows = [[] for _ in tiles]
            for k in range(CHUNK):
                in_map = bb_ref[base + k]
                out_map = cb_ref[base + k]
                for j, t in enumerate(tiles):
                    decay = jnp.exp2(step[k : k + 1, t] * rates[j])
                    carry[j] = decay * carry[j] + drive[k : k + 1, t] * in_map
                    rows[j].append(jnp.sum(carry[j] * out_map, 0, keepdims=True))
            y_ref[pl.ds(base, CHUNK), lanes] = jnp.concatenate(
                [jnp.concatenate(row, 0) for row in rows], 1
            )
            return tuple(carry)

        first = entering[lax.div(b, each), :, lanes_at(lax.rem(b, each), width)]
        lax.fori_loop(0, step_ref.shape[0] // CHUNK, body, tuple(first[:, t] for t in tiles))
        return unused

    lax.fori_loop(0, 2 * each, block, 0)


def scan_back(
    step_ref, drive_ref, dy_ref, bb_ref, cb_ref, a_ref, starts_ref, inflow, through_ref, flow_ref, db_ref,
    dc_ref, da_ref, width,
):
    tiles = tiles_of(width)
    each = inflow.shape[2] // width
    count = step_ref.shape[0] // CHUNK
    db_ref[...] = jnp.zeros_like(db_ref)
    dc_ref[...] = jnp.zeros_like(dc_ref)

    def block(b, unused):
        lanes = lanes_at(b, width)
        rates = [a_ref[:, lanes][:, t] for t in tiles]

        def body(i, carry):
            grads, d_rates = list(carry[0]), list(carry[1])
            chunk = count - 1 - i
            base = pl.multiple_of(chunk * CHUNK, CHUNK)
            step = step_ref[pl.ds(base, CHUNK), lanes]
            drive = drive_ref[pl.ds(base, CHUNK), lanes]
            dys = dy_ref[pl.ds(base, CHUNK), lanes]
            start = starts_ref[chunk, :, lanes]
            d_in, d_out = [None] * CHUNK, [None] * CHUNK
            all_through, all_flows = [], []
            for j, t in enumerate(tiles):
                current = start[:, t]
                decays, states = [], [current]
                for k in range(CHUNK):
                    decay = jnp.exp2(step[k : k + 1, t] * rates[j])
                    current = decay * current + drive[k : k + 1, t] * bb_ref[base + k]
                    decays.append(decay)
                    states.append(current)
                grad = grads[j]
                through, flows = [None] * CHUNK, [None] * CHUNK
                for k in reversed(range(CHUNK)):
                    dy = dys[k : k + 1, t]
                    grad = grad + dy * cb_ref[base + k]
                    through[k] = jnp.sum(grad * bb_ref[base + k], 0, keepdims=True)
                    piece = grad * drive[k : k + 1, t]
                    d_in[k] = piece if d_in[k] is None else d_in[k] + piece
                    piece = dy * states[k + 1]
                    d_out[k] = piece if d_out[k] is None else d_out[k] + piece
                    grad = decays[k] * grad
                    flow = grad * states[k]
                    flows[k] = jnp.sum(flow * rates[j], 0, keepdims=True)
                    d_rates[j] = d_rates[j] + flow * step[k : k + 1, t]
                grads[j] = grad
                all_through.append(jnp.concatenate(through, 0))
                all_flows.append(jnp.concatenate(flows, 0))
            through_ref[pl.ds(base, CHUNK), lanes] = jnp.concatenate(all_through, 1)
            flow_ref[pl.ds(base, CHUNK), lanes] = jnp.concatenate(all_flows, 1)
            for k in range(CHUNK):
                db_ref[base + k] += d_in[k]
                dc_ref[base + k] += d_out[k]
            return tuple(grads), tuple(d_rates)

        first = inflow[lax.div(b, each), :, lanes_at(lax.rem(b, each), width)]
        zeros = tuple(jnp.zeros((a_ref.shape[0], LANES), f32) for _ in tiles)
        d_rates = lax.fori_loop(0, count, body, (tuple(first[:, t] for t in tiles), zeros))[1]
        da_ref[:, lanes] = jnp.concatenate(d_rates, 1)
        return unused

    lax.fori_loop(0, 2 * each, block, 0)


def block_width(width, most):
    while width % most:
        most -= LANES
    return most


def shape_of(*shape, dtype=f32):
    return jax.ShapeDtypeStruct(shape, dtype)


def place_of(index, count):
    return jnp.where(
        lax.rem(index, 2) == 0, lax.div(index, 2), count - 1 - lax.div(index, 2)
    )


def index_at(place, count):
    place = lax.rem(place + 2 * count, count)
    return jnp.where(place < (count + 1) // 2, 2 * place, 2 * (count - 1 - place) + 1)


def greet(devices):
    barrier = pltpu.get_barrier_semaphore()
    for device in devices:
        pl.semaphore_signal(barrier, inc=1, device_id=device, device_id_type=MESH)
    pl.semaphore_wait(barrier, len(devices))


def remote(src, dst, send, recv, device):
    return pltpu.make_async_remote_copy(
        src_ref=src, dst_ref=dst, send_sem=send, recv_sem=recv, device_id=device,
        device_id_type=MESH,
    )


def here(count):
    section, dp, core = (lax.axis_index(name) for name in ("section", "dp", "expert"))
    place = place_of(dp, count)
    right = (section, index_at(place + 1, count), core)
    left = (section, index_at(place - 1, count), core)
    return dp, core, place, right, left, (section, dp, 1 - core)


def dp_peers(count):
    section, dp, core = (lax.axis_index(name) for name in ("section", "dp", "expert"))
    return [(section, lax.rem(dp + by, count), core) for by in range(1, count)]


def comm_params(identity, vmem=48):
    return pltpu.CompilerParams(
        collective_id=identity, has_side_effects=True, vmem_limit_bytes=vmem * MIB
    )


anywhere = pl.BlockSpec(memory_space=pl.ANY)
in_vmem = pl.BlockSpec(memory_space=pltpu.VMEM)
dma = pltpu.SemaphoreType.DMA


def gelu_parts(x):
    scale, cubic = 0.7978845608028654, 0.044715
    square = x * x
    t = jnp.tanh(scale * x * (1.0 + cubic * square))
    act = 0.5 * x * (1.0 + t)
    slope = 0.5 * (1.0 + t) + 0.5 * x * (1.0 - t * t) * scale * (1.0 + 3.0 * cubic * square)
    return act, slope


def own_expert(rows, each_rows, hidden):
    each = each_rows // CAP
    row = lax.broadcasted_iota(jnp.int32, (rows, 1), 0)
    for _ in range(rows // each_rows - 1):
        row = jnp.where(row >= each_rows, row - each_rows, row)
    column = lax.broadcasted_iota(jnp.int32, (1, hidden), 1)
    row_expert, column_expert = jnp.zeros_like(row), jnp.zeros_like(column)
    for e in range(1, each):
        row_expert = row_expert + (row >= e * CAP).astype(jnp.int32)
        column_expert = column_expert + (column >= e * (hidden // each)).astype(jnp.int32)
    return row_expert == column_expert


def mm(a, b, dims):
    return lax.dot_general(a, b, (dims, ((), ())), preferred_element_type=f32)


class Round:
    def __init__(self, count, own, held, work, part, out, scratch):
        self.own, self.held, self.work, self.part, self.out = own, held, work, part, out
        self.slots, (self.total, self.pair_in, self.pair_sems) = scratch[:4], scratch[4:7]
        self.sems, self.back_sems, self.local_sem = scratch[7:9], scratch[9:11], scratch[11]
        self.count, self.reach = count, count // 2
        self.dp, self.core, self.place, right, left, self.partner = here(count)
        self.towards = (right, left)

    def source(self, way, k):
        return index_at(self.place - k if way == 0 else self.place + k, self.count)

    def hop(self, way, k, half, src=None):
        sem = self.sems[way]
        slot = self.held.at[self.source(way, k), self.core if half == 0 else 1 - self.core]
        return remote(
            slot if src is None else src, slot, sem.at[0, k, half], sem.at[1, k, half],
            self.towards[way],
        )

    def first(self, half):
        return self.own.at[self.core] if half == 0 else None

    def swap(self):
        return remote(
            self.own.at[1 - self.core], self.held.at[self.dp, self.core], self.pair_sems.at[0, 0],
            self.pair_sems.at[1, 0], self.partner,
        )

    def keep(self):
        return pltpu.make_async_copy(
            self.own.at[self.core], self.held.at[self.dp, self.core], self.local_sem
        )

    def begin(self):
        self.swap().start()
        self.keep().start()
        for way in range(2):
            if self.reach > 1 or way == 0:
                self.hop(way, 0, 0, self.first(0)).start()

    def begin_other(self):
        self.swap().wait_recv()
        for way in range(2):
            if self.reach > 1 or way == 1:
                self.hop(way, 0, 1).start()
        self.keep().wait()

    def further(self, k):
        for half in range(2):
            for way in range(2):
                self.hop(way, k - 1, half).wait_recv()
                if half == way:
                    self.hop(way, k, half).start()
                else:

                    @pl.when(k < self.reach - 1)
                    def _(way=way, half=half):
                        self.hop(way, k, half).start()

    def arrive(self):
        for way in range(2):
            self.hop(way, self.reach - 1, way).wait_recv()

    def back(self, way, k, half):
        sem = self.back_sems[way]
        return remote(
            self.slots[way].at[k, half], self.slots[way + 2].at[k, half], sem.at[0, k, half],
            sem.at[1, k, half], self.towards[way],
        )

    def begin_back(self):
        for way in range(2):
            self.slots[way + 2][0, 1 - way] = jnp.zeros(self.slots[0].shape[2:], bf16)
            self.slots[way][0, way] = self.part[self.source(way, self.reach), way]
            self.back(way, 0, way).start()

    def nearer(self, k):
        for half in range(2):
            for way in range(2):
                owner = self.source(1 - way, self.reach - k)
                piece = self.part[owner, half].astype(f32)
                if half == way:
                    self.back(way, k - 1, half).wait_recv()
                else:

                    @pl.when(k > 1)
                    def _(way=way, half=half):
                        self.back(way, k - 1, half).wait_recv()

                before = self.slots[way + 2][k - 1, half].astype(f32)
                self.slots[way][k, half] = (piece + before).astype(bf16)
                self.back(way, k, half).start()

    def swap_back(self):
        return remote(
            self.total.at[1 - self.core], self.pair_in, self.pair_sems.at[0, 1], self.pair_sems.at[1, 1],
            self.partner,
        )

    def sum_up(self):
        for half in range(2):
            value = self.part[self.dp, half].astype(f32)
            for way in range(2):
                if self.reach > 1 or half == way:
                    self.back(way, self.reach - 1, half).wait_recv()
                    value = value + self.slots[way + 2][self.reach - 1, half].astype(f32)
            self.total[half] = value.astype(bf16)
        self.swap_back().start()

    def end(self):
        self.out[self.core] = self.total[self.core]
        self.swap_back().wait_recv()
        self.out[1 - self.core] = self.pair_in[...]
        self.swap().wait_send()
        self.swap_back().wait_send()

    def finish(self, k):
        for half in range(2):
            for way in range(2):
                if half == way:
                    self.hop(way, k, half, self.first(half)).wait_send()
                    self.back(way, k, half).wait_send()
                else:

                    @pl.when(k < self.reach - 1)
                    def _(way=way, half=half):
                        self.hop(way, k, half, self.first(half)).wait_send()

                    @pl.when(k > 0)
                    def _(way=way, half=half):
                        self.back(way, k, half).wait_send()


def go_round(rounds):
    reach = rounds[0].reach

    def steps(from_step, step):
        def body(k, unused):
            step(k)
            return unused

        lax.fori_loop(from_step, reach, body, 0)

    for one in rounds:
        one.begin()
    for one in rounds:
        one.begin_other()
    for one in rounds:
        one.work([one.dp])

    def further(k):
        for one in rounds:
            one.further(k)
        for one in rounds:
            one.work([one.source(0, k), one.source(1, k)])

    steps(1, further)
    for one in rounds:
        one.arrive()
        one.work([one.source(0, reach)])
        one.begin_back()

    def nearer(k):
        for one in rounds:
            one.nearer(k)

    steps(1, nearer)
    for one in rounds:
        one.sum_up()
    for one in rounds:
        one.end()

    def finish(k):
        for one in rounds:
            one.finish(k)

    steps(0, finish)


def rows_of(held, sources):
    pieces = [held[s].reshape(-1, held.shape[-1]) for s in sources]
    return pieces[0] if len(pieces) == 1 else jnp.concatenate(pieces, 0)


def put_rows(ref, sources, value):
    size = value.shape[0] // len(sources)
    for i, s in enumerate(sources):
        ref[s] = value[i * size : (i + 1) * size].reshape(ref.shape[1:]).astype(ref.dtype)


def block_at(section, index, count):
    index = lax.rem(index + 2 * count, 2 * count)
    return section, lax.div(index, 2), lax.rem(index, 2)


def experts_kernel(count, ahead, behind, cross, *refs):
    refs = list(refs)

    def take(number):
        taken = refs[:number]
        del refs[:number]
        return taken

    if ahead:
        own, resid, table, gate = take(4)
    if behind:
        below = take(1)[0] if cross else None
        above, table_back, gate_back, arrived_hbm = take(4)
    up_hbm, down_hbm = take(2)
    if ahead:
        out, result = take(2)
        next_rows, next_halo = take(2) if cross else (None, None)
        (arrived_out,) = take(1)
    if behind:
        upstream_out, out_back, given_out, hidden_out, slope_out = take(5)
    up, down, load_sems = take(3)
    section = lax.axis_index("section")
    dp, core, place, right, left, partner = here(count)
    block = 2 * dp + core
    across, before, after = (block_at(1 - section, block + by, count) for by in (0, -1, 1))
    greet([right, left, partner] + [across] * cross + [before] * (cross and ahead))
    loads = [
        pltpu.make_async_copy(up_hbm, up, load_sems.at[0]),
        pltpu.make_async_copy(down_hbm, down, load_sems.at[1]),
    ]
    rounds = []
    if ahead:
        held, part = take(2)
        landed, landed_halo, cross_sems = take(3) if cross else (None, None, None)
        scratch = take(12)
        (save_sem,) = take(1)

        def work(sources):
            pre = mm(rows_of(held, sources), up[...], ((1,), (0,)))
            mask = own_expert(pre.shape[0], held.shape[2], pre.shape[1])
            hidden = jnp.where(mask, gelu_parts(pre)[0], 0.0).astype(bf16)
            put_rows(part, sources, mm(hidden, down[...], ((1,), (0,))))

        rounds.append(Round(count, own, held, work, part, out, scratch))
    if behind:
        own_back, held_back, arrived, hidden_all, slope_all, part_back = take(6)
        landed_back, cross_back = take(2) if cross else (None, None)
        scratch_back = take(12)
        (back_sems,) = take(1)
        loads.append(pltpu.make_async_copy(arrived_hbm, arrived, back_sems.at[0]))

        def work_back(sources):
            pre = mm(rows_of(arrived, sources), up[...], ((1,), (0,)))
            mask = own_expert(pre.shape[0], held_back.shape[2], pre.shape[1])
            act, slope = gelu_parts(pre)
            put_rows(hidden_all, sources, jnp.where(mask, act, 0.0))
            d_hidden = mm(rows_of(held_back, sources), down[...], ((1,), (1,)))
            d_pre = jnp.where(mask, d_hidden * slope, 0.0).astype(bf16)
            put_rows(slope_all, sources, d_pre)
            put_rows(part_back, sources, mm(d_pre, up[...], ((1,), (1,))))

        rounds.append(Round(count, own_back, held_back, work_back, part_back, out_back, scratch_back))
    if behind:
        if cross:
            crossing = remote(below, landed_back, cross_back.at[0], cross_back.at[1], across)
            crossing.start()
    for load in loads:
        load.start()
    if behind:
        upstream = above[...].astype(f32)
        if cross:
            crossing.wait_recv()
            upstream = jnp.where(section == 1, upstream, landed_back[...].astype(f32))
        upstream_out[...] = upstream.astype(bf16)
        slots_grad = mm(table_back[...], (upstream * gate_back[...]).astype(bf16), ((1,), (0,)))
        own_back[...] = slots_grad.astype(bf16).reshape(own_back.shape)
    waiting = list(loads)
    for one in rounds:

        def work_first(sources, work=one.work):
            while waiting:
                waiting.pop().wait()
            work(sources)

        one.work = work_first
    go_round(rounds)
    saves = []
    if ahead:
        saves.append(pltpu.make_async_copy(held, arrived_out, save_sem))
    if behind:
        for n, (src, dst) in enumerate(
            ((held_back, given_out), (hidden_all, hidden_out), (slope_all, slope_out))
        ):
            saves.append(pltpu.make_async_copy(src, dst, back_sems.at[1 + n]))
    for save in saves:
        save.start()
    if ahead:
        returned = out[...].reshape(-1, out.shape[2])
        combined = mm(table[...], returned, ((1,), (0,))) * gate[...]
        result[...] = (resid[...] + combined).astype(bf16)
    if ahead and cross:
        length, halo = result.shape[0], next_halo.shape[0]
        copies = [
            remote(result, landed, cross_sems.at[0, 0], cross_sems.at[1, 0], across),
            remote(
                result.at[length - halo : length], landed_halo, cross_sems.at[0, 1], cross_sems.at[1, 1], after
            ),
        ]
        for copy in copies:
            copy.start()
        for copy in copies:
            copy.wait_recv()
        next_rows[...] = landed[...]
        next_halo[...] = jnp.where(block > 0, landed_halo[...].astype(f32), 0.0).astype(bf16)
        for copy in copies:
            copy.wait_send()
    if behind and cross:
        crossing.wait_send()
    for save in saves:
        save.wait()


def experts(up, down, ahead, behind, cross):
    count = lax.axis_size("dp")
    reach = count // 2
    width = (ahead[1] if ahead else behind[-4]).shape[1]
    length = (ahead[1] if ahead else behind[-4]).shape[0]
    rows = (2, EXPERTS * CAP // 2, width)
    gathered = (count,) + rows
    units = (count, 2 * rows[1], up.shape[1])
    around = (
        [pltpu.VMEM((reach,) + rows, bf16)] * 4
        + [pltpu.VMEM(rows, bf16), pltpu.VMEM(rows[1:], bf16), dma((2, 2))]
        + [dma((2, reach, 2))] * 4
        + [dma(())]
    )
    in_specs, out_specs, shapes, scratch = [], [], [], []
    if ahead:
        landing = [(length, width), (HALO, width)] if cross else []
        in_specs += [in_vmem] * 4
        out_specs += [in_vmem] * (2 + len(landing)) + [anywhere]
        shapes += [rows, (length, width)] + landing + [gathered]
        scratch += [pltpu.VMEM(gathered, bf16)] * 2 + [pltpu.VMEM(shape, bf16) for shape in landing]
        scratch += [dma((2, 2))] * cross + around + [dma(())]
    if behind:
        in_specs += [in_vmem] * (len(behind) - 1) + [anywhere]
        out_specs += [in_vmem] * 2 + [anywhere] * 3
        shapes += [(length, width), rows, gathered, units, units]
        scratch += [pltpu.VMEM(rows, bf16)] + [pltpu.VMEM(gathered, bf16)] * 2
        scratch += [pltpu.VMEM(units, bf16)] * 2 + [pltpu.VMEM(gathered, bf16)]
        scratch += [pltpu.VMEM((length, width), bf16), dma((2,))] if cross else []
        scratch += around + [dma((4,))]
    number = 7 if ahead and behind else 1 if ahead else 2
    number += 0 if cross or number == 7 else 7
    return pl.pallas_call(
        functools.partial(experts_kernel, count, bool(ahead), bool(behind), cross),
        in_specs=in_specs + [anywhere] * 2,
        out_specs=out_specs,
        out_shape=[shape_of(*shape, dtype=bf16) for shape in shapes],
        scratch_shapes=[pltpu.VMEM(up.shape, bf16), pltpu.VMEM(down.shape, bf16), dma((2,))] + scratch,
        compiler_params=comm_params(number, 60),
        name="experts_both" if number == 7 else "experts_forward" if ahead else "experts_backward",
    )(*(ahead or ()), *(behind or ()), up, down)


def grid_here(count):
    section, dp, core = (lax.axis_index(name) for name in ("section", "dp", "expert"))
    a, b = lax.div(dp, 2), lax.rem(dp, 2)
    line = count // 2

    def at(place):
        return section, 2 * lax.rem(place + line, line) + b, core

    return a, b, core, at(a + 1), at(a - 1), (section, 2 * a + 1 - b, core), (section, dp, 1 - core)


def weights_gather_kernel(count, parts, tokens, wide_up, wide_down, *refs):
    own, refs = refs[:parts], refs[parts:]
    (halos, up_out, low_down), out, refs = refs[:3], refs[3 : parts + 3], refs[parts + 3 :]
    buffer_up, buffer_down, rounded_up, rounded_down, load_sems, up_sems = refs[:6]
    after_sems, before_sems, side_sems, pair_sems, local_sems, halo_sems = refs[6:]
    a, b, core, after, before, beside, partner = grid_here(count)
    line = count // 2
    section, block = lax.axis_index("section"), 2 * (2 * a + b) + core
    greet(dp_peers(count) + [partner, block_at(section, block - 1, count)])
    micro, length = tokens.shape[:2]
    ends = [
        remote(
            tokens.at[m, length - HALO : length], halos.at[m], halo_sems.at[0, m], halo_sems.at[1, m],
            block_at(section, block + 1, count),
        )
        for m in range(micro)
    ]
    for copy in ends:
        copy.start()

    def slot(p, place, which):
        return out[p].at[core, 2 * place + which]

    def source(p, place, k):
        return own[p] if isinstance(k, int) and k == 0 else slot(p, place, b)

    def along(way, k, p):
        place = a - k if way == 0 else a + k
        sems = after_sems if way == 0 else before_sems
        return remote(
            source(p, place, k), slot(p, place, b), sems.at[0, k, p], sems.at[1, k, p],
            after if way == 0 else before,
        )

    def aside(place, k, p):
        return remote(
            source(p, place, k), slot(p, place, b), side_sems.at[0, place, p], side_sems.at[1, place, p],
            beside,
        )

    def across(place, which, k, p):
        src = source(p, place, k) if which is b else slot(p, place, which)
        number = 2 * place + which
        return remote(
            src, slot(p, place, which), pair_sems.at[0, number, p], pair_sems.at[1, number, p], partner
        )

    def has(way, k):
        return a - k >= 0 if way == 0 else a + k < line

    def goes(way):
        return a + 1 < line if way == 0 else a >= 1

    for p in range(parts):
        aside(a, 0, p).start()
        for way in range(2):

            @pl.when(goes(way))
            def _(way=way, p=p):
                along(way, 0, p).start()

    keeps = [
        pltpu.make_async_copy(own[p], slot(p, a, b), local_sems.at[p]) for p in range(parts)
    ]
    for p in range(parts):
        across(a, b, 0, p).start()
        keeps[p].start()
    loads = [
        pltpu.make_async_copy(wide_up, buffer_up, load_sems.at[0]),
        pltpu.make_async_copy(wide_down, buffer_down, load_sems.at[1]),
    ]
    save = pltpu.make_async_copy(rounded_down, low_down, load_sems.at[2])
    for load in loads:
        load.start()
    loads[0].wait()
    each, depth, hidden = wide_up.shape
    cut = hidden // count
    for piece in range(count):
        for e in range(each):
            rounded_up[piece, :, e * cut : (e + 1) * cut] = buffer_up[
                e, :, piece * cut : (piece + 1) * cut
            ].astype(bf16)
    start, end = exchange(count, rounded_up, up_out, up_sems, load_sems.at[3])
    start(0)
    start(1)
    loads[1].wait()

    def rounding(e, unused):
        rounded_down[e] = buffer_down[e].astype(bf16)
        return unused

    lax.fori_loop(0, each, rounding, 0)
    save.start()

    def came_aside(place, p):
        aside(place, None, p).wait_recv()
        across(place, 1 - b, None, p).start()

    def arrivals(k, unused):
        for p in range(parts):
            for way in range(2):

                @pl.when(has(way, k))
                def _(way=way, p=p):
                    place = a - k if way == 0 else a + k
                    along(way, k - 1, p).wait_recv()

                    @pl.when(goes(way))
                    def _():
                        along(way, k, p).start()

                    aside(place, None, p).start()
                    across(place, b, None, p).start()

        for p in range(parts):

            @pl.when(k == 1)
            def _(p=p):
                came_aside(a, p)

            for way in range(2):

                @pl.when((k > 1) & has(way, k - 1))
                def _(way=way, p=p):
                    came_aside(a - k + 1 if way == 0 else a + k - 1, p)

        return unused

    lax.fori_loop(1, line, arrivals, 0)
    for p in range(parts):
        if line == 1:
            came_aside(a, p)
        for way in range(2):

            @pl.when((line > 1) & has(way, line - 1))
            def _(way=way, p=p):
                came_aside(a - line + 1 if way == 0 else a + line - 1, p)

    for p in range(parts):
        keeps[p].wait()

    def finish(place, unused):
        for p in range(parts):
            for which in range(2):
                copy = across(place, which, None, p)
                copy.wait_recv()
                copy.wait_send()
            aside(place, None, p).wait_send()
        return unused

    lax.fori_loop(0, line, finish, 0)

    def sent(k, unused):
        for p in range(parts):
            for way in range(2):

                @pl.when(has(way, k) & goes(way))
                def _(way=way, p=p):
                    along(way, k, p).wait_send()

        return unused

    lax.fori_loop(0, line, sent, 0)
    save.wait()
    end()
    for copy in ends:
        copy.wait()


def weights_gather(tokens, up, down, own):
    count = lax.axis_size("dp")
    reach = count // 2
    parts = len(own)
    pieces = (count, up.shape[1], up.shape[0] * up.shape[2] // count)
    return pl.pallas_call(
        functools.partial(weights_gather_kernel, count, parts),
        in_specs=[anywhere] * (parts + 3),
        out_specs=[anywhere] * (parts + 3),
        out_shape=[shape_of(tokens.shape[0], HALO, tokens.shape[2], dtype=bf16)]
        + [shape_of(*pieces, dtype=bf16), shape_of(*down.shape, dtype=bf16)]
        + [shape_of(2, count, *part.shape, dtype=part.dtype) for part in own],
        scratch_shapes=[
            pltpu.VMEM(up.shape, f32),
            pltpu.VMEM(down.shape, f32),
            pltpu.VMEM(pieces, bf16),
            pltpu.VMEM(down.shape, bf16),
            dma((4,)),
            dma((2, count - 1)),
            dma((2, reach, parts)),
            dma((2, reach, parts)),
            dma((2, reach, parts)),
            dma((2, count, parts)),
            dma((parts,)),
            dma((2, tokens.shape[0])),
        ],
        compiler_params=comm_params(3),
        name="weights_gather",
    )(tokens, up, down, *own)


def grads_reduce_kernel(count, micro, vec, pieces, *refs):
    refs = list(refs)

    def take(number):
        taken = refs[:number]
        del refs[:number]
        return taken

    given = [take(8) for _ in range(micro)]
    (up_out,), out = take(1), take(4)
    wholes, halves, (vecs, landed) = take(4), take(5), take(2)
    part, sides, ins = take(4), take(4), (take(4), take(4))
    whole_sems, half_sems, vec_sems, after_sems, before_sems, side_sems, piece_sems, local_sem = refs
    a, b, core, after, before, beside, partner = grid_here(count)
    line = count // 2
    parts = len(part)
    half = halves[0].shape[1]
    length = given[0][0].shape[0]
    greet_all(count)

    def lanes(side, begin):
        return pl.ds(pl.multiple_of(begin + side * half, LANES), half)

    def moves_of(i, n, which):
        place, there = pl.ds(i * length, length), pl.ds((micro + i) * length, length)
        if n < 4:
            src, dst = given[i][n], wholes[n]
            if which == 0:
                return pltpu.make_async_copy(src, dst.at[place], whole_sems.at[2, i, n])
            return remote(src, dst.at[there], whole_sems.at[0, i, n], whole_sems.at[1, i, n], partner)
        n -= 4
        src, begin = (given[i][4], n * 2 * half) if n < 2 else (given[i][3 + n], 0)
        dst = halves[n]
        if which == 0:
            return pltpu.make_async_copy(
                src.at[:, lanes(core, begin)], dst.at[place], half_sems.at[2, i, n]
            )
        return remote(
            src.at[:, lanes(1 - core, begin)], dst.at[there], half_sems.at[0, i, n], half_sems.at[1, i, n],
            partner,
        )

    order = (0, 4, 5, 1, 6, 2, 7, 3, 8)
    for n in order:
        for i in range(micro):
            for which in range(2):
                moves_of(i, n, which).start()
    vec_copies = (
        pltpu.make_async_copy(vec.at[core], vecs.at[0], vec_sems.at[2]),
        remote(vec.at[1 - core], vecs.at[1], vec_sems.at[0], vec_sems.at[1], partner),
    )
    for copy in vec_copies:
        copy.start()
    start, end = exchange(count, pieces, landed, piece_sems, local_sem)
    start(0)

    def ready(n):
        for i in range(micro):
            moves_of(i, n, 0).wait()
            moves_of(i, n, 1).wait_recv()

    def aside(place, p):
        return remote(
            part[p].at[2 * place + 1 - b], sides[p].at[place], side_sems.at[0, place, p],
            side_sems.at[1, place, p], beside,
        )

    def along(way, place, p):
        sems = after_sems if way == 0 else before_sems
        return remote(
            part[p].at[2 * place + b], ins[way][p].at[place], sems.at[0, place, p], sems.at[1, place, p],
            after if way == 0 else before,
        )

    def far(way, k):
        return line - 1 - k if way == 0 else k

    def put(p, value):
        share = part[p].shape[1]
        for index in range(count):
            part[p][index] = value[index * share : (index + 1) * share].astype(bf16)

        def starts(k, unused):
            for way in range(2):

                @pl.when((way == 0) | (far(0, k) != far(1, k)))
                def _(way=way):
                    aside(far(way, k), p).start()

            return unused

        lax.fori_loop(0, (line + 1) // 2, starts, 0)

    def both_lines(place, p):
        aside(place, p).wait_recv()
        return part[p][2 * place + b].astype(f32) + sides[p][place].astype(f32)

    def passing(k, p):
        for way in range(2):
            place = far(way, k)

            @pl.when(place > a if way == 0 else place < a)
            def _(way=way, place=place):
                index = 2 * place + b
                part[p][index] = both_lines(place, p).astype(bf16)

                @pl.when(a > 0 if way == 0 else a < line - 1)
                def _():
                    along(way, place, p).wait_recv()
                    value = part[p][index].astype(f32) + ins[way][p][place].astype(f32)
                    part[p][index] = value.astype(bf16)

                along(way, place, p).start()

    over = ((0,), (0,))
    ready(0)
    ready(4)
    put(0, mm(halves[0][...], wholes[0][...], over))
    ready(5)
    put(1, mm(halves[1][...], wholes[0][...], over))
    ready(1)
    ready(6)
    put(2, mm(halves[2][...], wholes[1][...], over))
    start(1)
    for n in (2, 7, 3, 8):
        ready(n)
    vec_copies[0].wait()
    vec_copies[1].wait_recv()
    put(
        3,
        jnp.concatenate(
            [
                mm(halves[3][...], wholes[2][...], over),
                mm(halves[4][...], wholes[3][...], over),
            ],
            1,
        )
        + vecs[0].astype(f32)
        + vecs[1].astype(f32),
    )
    for p in range(parts):

        def passing_on(k, unused, p=p):
            passing(k, p)
            return unused

        lax.fori_loop(0, line - 1, passing_on, 0)
    for p in range(parts):
        out[p][...] = both_lines(a, p)
        for way in range(2):

            @pl.when(a > 0 if way == 0 else a < line - 1)
            def _(way=way, p=p):
                along(way, a, p).wait_recv()
                out[p][...] = out[p][...] + ins[way][p][a].astype(f32)

    def finish(place, unused):
        for p in range(parts):
            aside(place, p).wait_send()
            for way in range(2):

                @pl.when(place > a if way == 0 else place < a)
                def _(way=way, p=p):
                    along(way, place, p).wait_send()

        return unused

    lax.fori_loop(0, line, finish, 0)
    for n in order:
        for i in range(micro):
            moves_of(i, n, 1).wait_send()
    vec_copies[1].wait_send()
    end()
    each, depth, hidden = up_out.shape
    cut = hidden // count
    for piece in range(count):
        for e in range(each):
            up_out[e, :, piece * cut : (piece + 1) * cut] = landed[
                piece, :, e * cut : (e + 1) * cut
            ]


def grads_reduce(vec, pieces, given):
    count = lax.axis_size("dp")
    line = count // 2
    micro = len(given)
    length, model = given[0][0].shape
    half, lanes = vec.shape[1:]
    share = half // count
    each = EXPERTS // 2
    rows = 2 * micro * length
    shares = [(share, model)] * 3 + [(share, lanes)]
    wholes = [value.shape[1] for value in given[0][:4]]
    return pl.pallas_call(
        functools.partial(grads_reduce_kernel, count, micro),
        in_specs=[anywhere] * (2 + 8 * micro),
        out_specs=[in_vmem] * 5,
        out_shape=[shape_of(each, pieces.shape[1], count * pieces.shape[2] // each, dtype=bf16)]
        + [shape_of(*shape) for shape in shares],
        scratch_shapes=[pltpu.VMEM((rows, width), bf16) for width in wholes]
        + [pltpu.VMEM((rows, half), bf16)] * 5
        + [pltpu.VMEM((2, half, lanes), bf16), pltpu.VMEM(pieces.shape, bf16)]
        + [pltpu.VMEM((count,) + shape, bf16) for shape in shares]
        + [pltpu.VMEM((line,) + shape, bf16) for shape in shares] * 3
        + [dma((3, micro, 4)), dma((3, micro, 5)), dma((3,))]
        + [dma((2, line, 4))] * 3
        + [dma((2, count - 1)), dma(())],
        compiler_params=comm_params(4, 60),
        name="grads_reduce",
    )(vec, pieces, *[value for one in given for value in one])


def join(
    count, forward, state_ref, total_ref, rates, out_ref, other_state, other_total, mine, mine_total, states,
    totals, back, back_in, pair_sems, sems,
):
    section, dp, core = (lax.axis_index(name) for name in ("section", "dp", "expert"))
    partner = (section, dp, 1 - core)
    swap = [
        remote(state_ref.at[1 - core], other_state, pair_sems.at[0, 0], pair_sems.at[1, 0], partner),
        remote(total_ref.at[1 - core], other_total, pair_sems.at[0, 1], pair_sems.at[1, 1], partner),
    ]
    for copy in swap:
        copy.start()
    own_state, own_total = state_ref[core], total_ref[core]
    for copy in swap:
        copy.wait_recv()
    leads = core == (0 if forward else 1)
    first_state = jnp.where(leads, own_state, other_state[...])
    first_total = jnp.where(leads, own_total, other_total[...])
    second_state = jnp.where(leads, other_state[...], own_state)
    second_total = jnp.where(leads, other_total[...], own_total)
    mine[...] = (jnp.exp2(rates * second_total) * first_state + second_state).astype(bf16)
    mine_total[...] = first_total + second_total
    copies = []
    for d, peer in enumerate(dp_peers(count)):
        for n, (src, dst) in enumerate(((mine, states), (mine_total, totals))):
            copy = remote(src, dst.at[dp], sems.at[0, d, n], sems.at[1, d, n], peer)
            copy.start()
            copies.append(copy)
    states[dp] = mine[...]
    totals[dp] = mine_total[...]
    for copy in copies:
        copy.wait_recv()

    entering = jnp.zeros_like(own_state)
    for k in range(count):
        source = k if forward else count - 1 - k
        reached = (source < dp) if forward else (source > dp)
        fresh = jnp.exp2(rates * totals[source]) * entering + states[source].astype(f32)
        entering = jnp.where(reached, fresh, entering)
    after = jnp.exp2(rates * first_total) * entering + first_state
    back[...] = jnp.where(leads, after, entering)
    swap_back = remote(back, back_in, pair_sems.at[0, 2], pair_sems.at[1, 2], partner)
    swap_back.start()
    out_ref[core] = jnp.where(leads, entering, after)
    swap_back.wait_recv()
    out_ref[1 - core] = back_in[...]
    for copy in swap + copies + [swap_back]:
        copy.wait_send()


def join_scratch(count, states, half):
    one, sums = pltpu.VMEM((states, half), f32), pltpu.VMEM((1, half), f32)
    return [
        pltpu.VMEM((2, states, half), f32),
        pltpu.VMEM((2, 1, half), f32),
        pltpu.VMEM((2, states, half), f32),
        one,
        sums,
        pltpu.VMEM((states, half), bf16),
        sums,
        pltpu.VMEM((count, states, half), bf16),
        pltpu.VMEM((count, 1, half), f32),
        one,
        one,
        dma((2, 3)),
        dma((2, count - 1, 2)),
    ]


def own_lanes(a_ref, half):
    return a_ref[:, lanes_at(lax.axis_index("expert"), half)]


def greet_all(count):
    section, dp, core = (lax.axis_index(name) for name in ("section", "dp", "expert"))
    greet(dp_peers(count) + [(section, dp, 1 - core)])


def exchange(count, pieces_ref, out_ref, sems, local_sem):
    dp = lax.axis_index("dp")
    keep = pltpu.make_async_copy(pieces_ref.at[dp], out_ref.at[dp], local_sem)
    keep.start()
    copies = []
    for by, peer in enumerate(dp_peers(count)):
        copies.append(
            remote(pieces_ref.at[peer[1]], out_ref.at[dp], sems.at[0, by], sems.at[1, by], peer)
        )

    def start(beside):
        for copy in copies[1 - beside :: 2]:
            copy.start()

    def end():
        keep.wait()
        for copy in copies:
            copy.wait()

    return start, end


def mixer_forward_kernel(
    count, step_ref, drive_ref, bb_ref, cb_ref, a_ref, y_ref, starts_ref, state, total, entering, *rest
):
    half = state.shape[2]
    width = block_width(half, 384)
    scan_final(step_ref, drive_ref, bb_ref, a_ref, state, total, width)
    greet_all(count)
    join(count, True, state, total, own_lanes(a_ref, half), entering, *rest)
    scan_outputs(step_ref, drive_ref, bb_ref, cb_ref, a_ref, entering, y_ref, starts_ref, width)


def mixer_forward(step, drive, in_map, out_map, rates):
    count = lax.axis_size("dp")
    (length, width), states = step.shape, rates.shape[0]
    return pl.pallas_call(
        functools.partial(mixer_forward_kernel, count),
        in_specs=[in_vmem] * 5,
        out_specs=[in_vmem] * 2,
        out_shape=[shape_of(length, width), shape_of(length // CHUNK, states, width)],
        scratch_shapes=join_scratch(count, states, width // 2),
        compiler_params=comm_params(5),
        name="mixer_forward",
    )(step, drive, in_map, out_map, rates)


def mixer_backward_kernel(
    count, step_ref, drive_ref, dy_ref, bb_ref, cb_ref, a_ref, starts_ref, through_ref, flow_ref, db_ref, dc_ref,
    da_ref, state, total, inflow, *rest,
):
    half = state.shape[2]
    width = block_width(half, 384)
    scan_leak(step_ref, dy_ref, cb_ref, a_ref, state, total, width)
    greet_all(count)
    join(count, False, state, total, own_lanes(a_ref, half), inflow, *rest)
    scan_back(
        step_ref, drive_ref, dy_ref, bb_ref, cb_ref, a_ref, starts_ref, inflow, through_ref, flow_ref, db_ref,
        dc_ref, da_ref, width,
    )


def mixer_backward(step, drive, dy, in_map, out_map, rates, starts):
    count = lax.axis_size("dp")
    (length, width), states = step.shape, rates.shape[0]
    wide, maps = shape_of(length, width), shape_of(*in_map.shape)
    return pl.pallas_call(
        functools.partial(mixer_backward_kernel, count),
        in_specs=[in_vmem] * 7,
        out_specs=[in_vmem] * 5,
        out_shape=[wide, wide, maps, maps, shape_of(states, width)],
        scratch_shapes=join_scratch(count, states, width // 2),
        compiler_params=comm_params(6),
        name="mixer_backward",
    )(step, drive, dy, in_map, out_map, rates, starts)


def dot(a, b, dims, dtype=f32):
    return lax.dot_general(a, b, (dims, ((), ())), preferred_element_type=f32).astype(dtype)


def nn(a, b, dtype=f32):
    return dot(a, b, ((1,), (0,)), dtype)


def nt(a, b, dtype=f32):
    return dot(a, b, ((1,), (1,)), dtype)


def tn(a, b, dtype=f32):
    return dot(a, b, ((0,), (0,)), dtype)


def normalize(values, gain):
    return values * lax.rsqrt(jnp.mean(values * values, axis=-1, keepdims=True) + epsilon) * gain


def sums(value):
    return jnp.sum(value, 0)


def normalize_back(values, gain, upstream):
    scale = lax.rsqrt(jnp.mean(values * values, axis=-1, keepdims=True) + epsilon)
    unit = values * scale
    inner = upstream * gain
    d_values = scale * (inner - unit * jnp.mean(inner * unit, axis=-1, keepdims=True))
    return d_values, sums(upstream * unit)


def from_behind(shard, axis, by):
    count = 1
    for name in (axis,) if isinstance(axis, str) else axis:
        count *= lax.axis_size(name)
    pairs = [(i, i + by) for i in range(count) if 0 <= i + by < count]
    return lax.ppermute(shard, axis, pairs)


def swap_pair(value):
    return lax.ppermute(value, "expert", [(0, 1), (1, 0)])


def spread(values):
    return jnp.broadcast_to(values[:, :, None], values.shape + (LANES,))


def routing(resid, moe_gain, router, chosen, placed, dropped):
    normed = normalize(resid, moe_gain)
    probs = jax.nn.softmax(jnp.dot(normed, router, precision=highest), axis=-1)
    keep = (1 - dropped).astype(f32)
    pick = (chosen[:, None] == jnp.arange(EXPERTS)[None]).astype(f32)
    gate = jnp.sum(probs * pick, -1) * keep
    flat = chosen * CAP + placed
    table = ((flat[:, None] == jnp.arange(EXPERTS * CAP)[None]) & (dropped[:, None] == 0)).astype(
        bf16
    )
    return normed, probs, pick, keep, gate, table


def by_core(buffer):
    return buffer.reshape(2, -1, buffer.shape[1])


def mixed(xz, weights):
    width = weights["w_out"].shape[0]
    taps = weights["conv_w"].shape[0]
    length = xz.shape[0] - HALO
    padded = xz[HALO - taps + 1 :, :width]
    summed = weights["conv_b"]
    for tap in range(taps):
        summed = summed + weights["conv_w"][tap : tap + 1] * padded[tap : tap + length]
    return padded, summed, xz[HALO:, width:]


def selective(projected, weights):
    rank = weights["rank"]
    states = weights["rates"].shape[0]
    dt_low = jnp.where(jnp.arange(projected.shape[1])[None] < rank, projected, 0.0).astype(bf16)
    dt_raw = nn(dt_low, weights["dt_proj"]) + weights["dt_bias"]
    in_map = projected[:, rank : rank + states]
    out_map = projected[:, rank + states : rank + 2 * states]
    return dt_low, dt_raw, jax.nn.softplus(dt_raw), spread(in_map), spread(out_map)


def forward(rows, halo, chosen, placed, dropped, weights):
    inputs = jnp.concatenate([halo, rows], 0).astype(f32)
    normed = normalize(inputs, weights["norm_gain"]).astype(bf16)
    xz = nt(normed, weights["w_in"])
    padded, summed, gate_in = mixed(xz, weights)
    signal = jax.nn.silu(summed).astype(bf16)
    projected = nn(signal, weights["x_proj"])
    dt_low, dt_raw, step, in_map, out_map = selective(projected, weights)
    wide = signal.astype(f32)
    drive = step * wide
    rates = weights["rates"] * LOG2E
    scanned, starts = mixer_forward(step, drive, in_map, out_map, rates)
    gated = ((scanned + weights["skip"] * wide) * jax.nn.silu(gate_in)).astype(bf16)
    resid = rows.astype(f32) + nn(gated, weights["w_out"])
    normed_moe, probs, pick, keep, gate, table = routing(
        resid, weights["moe_gain"], weights["router"], chosen, placed, dropped
    )
    buffer = tn(table, normed_moe.astype(bf16), bf16)
    ahead = (by_core(buffer), resid, table, gate[:, None])
    kept = dict(
        rows=rows, halo=halo, xz=xz, projected=projected, scanned=scanned, starts=starts, resid=resid,
    )
    return ahead, kept


def backward_routing(kept, chosen, placed, dropped, weights):
    return routing(
        kept["resid"], weights["moe_gain"], weights["router"], chosen, placed, dropped
    )


def backward_experts(routed, returned, upstream, d_sent, weights):
    normed_moe, probs, pick, keep, gate, table = routed
    d_sent = d_sent.reshape(-1, d_sent.shape[2])
    returned = returned.reshape(d_sent.shape)
    upstream = upstream.astype(f32)
    d_gate = jnp.sum(upstream * nn(table, returned), -1)
    d_choice = d_gate[:, None] * pick * keep[:, None]
    d_logits = probs * (d_choice - jnp.sum(probs * d_choice, -1, keepdims=True))
    d_normed = nn(table, d_sent) + jnp.dot(d_logits, weights["router"].T, precision=highest)
    return upstream, d_normed, d_logits


def backward_mixer(upstream, kept, d_normed, d_logits, weights):
    resid = kept["resid"]
    normed_moe = normalize(resid, weights["moe_gain"])
    grad_router = lax.dot_general(
        normed_moe, d_logits, (((0,), (0,)), ((), ())), precision=highest
    )
    d_norm, grad_moe = normalize_back(resid, weights["moe_gain"], d_normed)
    d_resid = upstream + d_norm

    inputs = kept["rows"].astype(f32)
    normed = normalize(inputs, weights["norm_gain"]).astype(bf16)
    xz = kept["xz"]
    padded, summed, gate_in = mixed(xz, weights)
    signal_act, signal_back = jax.vjp(jax.nn.silu, summed)
    signal = signal_act.astype(bf16)
    wide = signal.astype(f32)
    dt_low, dt_raw, step, in_map, out_map = selective(kept["projected"], weights)
    drive = step * wide
    rates = weights["rates"] * LOG2E
    skip = weights["skip"]
    total_out = kept["scanned"] + skip * wide
    gate_act, gate_back = jax.vjp(jax.nn.silu, gate_in)
    gated = (total_out * gate_act).astype(bf16)
    d_mixer = d_resid.astype(bf16)
    d_gated = nt(d_mixer, weights["w_out"])
    d_total = d_gated * gate_act
    d_gate_in = gate_back(d_gated * total_out)[0]
    grad_skip = sums(d_total * wide)
    through, flow, d_in_map, d_out_map, d_rates = mixer_backward(
        step, drive, d_total, in_map, out_map, rates, kept["starts"]
    )
    d_step = flow / LOG2E + through * wide
    d_signal = step * through + d_total * skip
    d_raw = d_step * jax.nn.sigmoid(dt_raw)
    grad_dt_bias = sums(d_raw)
    d_raw_low = d_raw.astype(bf16)
    d_low = nt(d_raw_low, weights["dt_proj"])
    rank, states = weights["rank"], weights["rates"].shape[0]
    d_maps = jnp.concatenate([jnp.sum(d_in_map, -1), jnp.sum(d_out_map, -1)], 1)
    d_maps = jnp.pad(d_maps, ((0, 0), (rank, d_low.shape[1] - rank - 2 * states)))
    d_projected = (d_low + d_maps).astype(bf16)
    d_signal = d_signal + nt(d_projected, weights["x_proj"])
    d_summed = signal_back(d_signal)[0]
    taps = weights["conv_w"].shape[0]
    length = d_summed.shape[0]
    ahead = from_behind(d_summed[:8], ("dp", "expert"), -1)
    extended = jnp.concatenate([d_summed, ahead], 0)
    d_conv_in = jnp.zeros_like(d_summed)
    for tap in range(taps):
        begin = taps - 1 - tap
        d_conv_in = d_conv_in + weights["conv_w"][tap : tap + 1] * extended[begin : begin + length]
    grad_conv = [
        sums(d_summed * padded[tap : tap + length]) for tap in range(taps)
    ]
    d_xz = jnp.concatenate([d_conv_in, d_gate_in], 1).astype(bf16)
    d_normed_in = nn(d_xz, weights["w_in"])
    d_inputs, grad_norm = normalize_back(inputs, weights["norm_gain"], d_normed_in)
    result = (d_resid + d_inputs).astype(bf16)
    given = (
        normed,
        d_mixer,
        d_projected,
        dt_low,
        d_xz,
        gated,
        signal,
        d_raw_low,
    )
    vectors = (
        grad_conv + [sums(d_summed), grad_dt_bias, grad_skip], d_rates * weights["rates"],
        [grad_norm, grad_moe], grad_router,
    )
    return result, given, vectors


def gather_weights(
    tokens, norm_gain, w_in, conv_w, conv_b, x_proj, dt_proj, dt_bias, a_log, skip, w_out, moe_gain, router,
    w_up, w_down,
):
    count = lax.axis_size("dp")
    share = x_proj.shape[1]
    model = w_out.shape[2]
    low_in = jnp.transpose(w_in[0].astype(bf16), (1, 2, 0))
    pieces = [
        x_proj[0], dt_proj[0].T, conv_w[0].T, conv_b[0][:, None], dt_bias[0][:, None],
        skip[0][:, None], a_log[0].T, norm_gain[0][:, None], moe_gain[0][:, None], router[0],
    ]
    sizes = [piece.shape[1] for piece in pieces]
    lead = -(-sizes[0] // LANES) * LANES
    begins = [0] + [lead + sum(sizes[1:n]) for n in range(1, len(sizes))]
    places = list(zip(begins, sizes, strict=True))
    pieces.insert(1, jnp.zeros((share, lead - sizes[0]), f32))
    pad = (-sum(sizes[1:])) % LANES
    small = jnp.concatenate(pieces + [jnp.zeros((share, pad), f32)], 1).astype(bf16)
    halos, up, low_down, in_x, in_z, out, small = weights_gather(
        tokens, w_up[0], w_down[0], [low_in[0], low_in[1], w_out[0].astype(bf16), small]
    )
    width = 2 * count * share
    w_in_all = jnp.concatenate([in_x.reshape(width, model), in_z.reshape(width, model)], 0)
    table = small.reshape(width, -1)
    rows = table.astype(f32).T
    found = [rows[begin : begin + size] for begin, size in places]
    unused, dt_proj, conv_w, conv_b, dt_bias, a_skip, a_log, norm_gain, moe_gain, router = found
    weights = dict(
        rank=sizes[1],
        w_in=w_in_all,
        w_out=out.reshape(width, model),
        x_proj=table[:, :lead],
        dt_proj=jnp.pad(dt_proj, ((0, lead - sizes[1]), (0, 0))).astype(bf16),
        conv_w=conv_w,
        conv_b=conv_b,
        dt_bias=dt_bias,
        skip=a_skip,
        rates=-jnp.exp(a_log),
        norm_gain=norm_gain[:, :model],
        moe_gain=moe_gain[:, :model],
        router=router[:, :model].T,
        w_up=up.reshape(-1, up.shape[2]),
        w_down=low_down.reshape(-1, model),
    )
    return weights, places, halos


def mixer_grads(given, vectors, places, up, count):
    channel, d_rates, feature, grad_router = vectors
    feature = jnp.concatenate([piece[None] for piece in feature] + [grad_router.T], 0)
    rows = jnp.concatenate(
        [piece[None] for piece in channel] + [d_rates, jnp.concatenate([feature, feature], 1)], 0
    )
    begin = places[2][0]
    lanes = -(-sum(places[-1]) // LANES) * LANES
    vec = jnp.pad(rows.T.astype(bf16), ((0, 0), (begin, lanes - begin - rows.shape[0])))
    vec = vec.reshape(2, -1, lanes)
    up, grad_x, grad_z, grad_out, small = grads_reduce(vec, up, given)
    found = [small[:, begin : begin + size] for begin, size in places]
    x_proj, dt_proj, conv_w, conv_b, dt_bias, skip, a_log, norm_gain, moe_gain, router = found
    return (
        norm_gain[:, 0],
        jnp.transpose(jnp.stack([grad_x, grad_z], 0), (2, 0, 1)),
        conv_w.T,
        conv_b[:, 0],
        x_proj,
        dt_proj.T,
        dt_bias[:, 0],
        a_log.T,
        skip[:, 0],
        grad_out,
        moe_gain[:, 0],
        router,
        up.astype(f32),
    )


def rows_flat(value):
    return value.reshape(-1, value.shape[-1])


def down_grad(first, second):
    hidden, d_produced = (
        jnp.concatenate([rows_flat(a), rows_flat(b)], 0)
        for a, b in zip(first, second, strict=True)
    )
    return tn(hidden, d_produced).reshape(EXPERTS // 2, -1, d_produced.shape[1])


def up_pieces(first, second, count):
    arrived, d_pre = (
        jnp.concatenate([rows_flat(a), rows_flat(b)], 0)
        for a, b in zip(first, second, strict=True)
    )
    return tn(arrived, d_pre, bf16).reshape(count, arrived.shape[1] // count, -1)


def shards(
    tokens, cotangent, routes, slots, drops, norm_gain, w_in, conv_w, conv_b, x_proj, dt_proj, dt_bias,
    a_log, skip, w_out, moe_gain, router, w_up, w_down,
):
    count = lax.axis_size("dp")
    section = lax.axis_index("section")
    top = section == 1
    weights, places, halos = gather_weights(
        tokens, norm_gain, w_in, conv_w, conv_b, x_proj, dt_proj, dt_bias, a_log, skip, w_out, moe_gain,
        router, w_up, w_down,
    )
    micro = tokens.shape[0]
    blocks = ("dp", "expert")
    steps = micro + 1

    def pick(which):
        return [lax.dynamic_index_in_dim(v[0], which, 0, False) for v in (routes, slots, drops)]

    begins = (lax.axis_index("dp") == 0) & (lax.axis_index("expert") == 0)
    halos = jnp.where(begins, jnp.zeros_like(halos), halos)
    incoming, incoming_halo = jnp.zeros_like(tokens[0]), jnp.zeros_like(halos[0])
    results, bank, grads, found, last = [], [], [], [], []
    below = None

    def micro_of(step, first):
        return jnp.clip(step - first, 0, micro - 1)

    def back_parts(step):
        if step == 1:
            kept = jax.tree.map(lambda a, b: jnp.where(top, a, b), bank[2], bank[0])
        else:
            kept = bank[1]
        routed = backward_routing(kept, *pick(micro_of(step, 1 - section)), weights)
        above = cotangent[step] if step < micro else jnp.zeros_like(cotangent[0])
        above = jnp.where(top, above, jnp.zeros_like(above))
        crossing = () if below is None else (below,)
        return kept, routed, crossing + (above, routed[5].T, routed[4][:, None], kept["arrived"])

    for step in range(2 * steps - 1):
        ahead = behind = None
        if step < steps:
            fresh = min(step, micro - 1)
            rows = jnp.where(top, incoming, tokens[fresh])
            halo = jnp.where(top, incoming_halo, halos[fresh])
            ahead, fresh_kept = forward(rows, halo, *pick(micro_of(step, section)), weights)
        if step >= steps - 1:
            kept, routed, behind = back_parts(step - steps + 1)
        cross = (ahead is None) != (behind is None)
        if cross or count <= 8:
            done = experts(weights["w_up"], weights["w_down"], ahead, behind, cross)
        else:
            done = experts(weights["w_up"], weights["w_down"], ahead, None, False)
            done = [*done, *experts(weights["w_up"], weights["w_down"], None, behind, False)]
        if ahead is not None:
            fresh_kept["returned"], result = done[:2]
            if cross:
                incoming, incoming_halo = done[2:4]
            number = 5 if cross else 3
            fresh_kept["arrived"] = done[number - 1]
            results.append(result)
            bank.append(fresh_kept)
            done = done[number:]
        if behind is not None:
            upstream, d_sent, d_produced, hidden, d_pre = done
            last.append((hidden, d_produced, kept["arrived"], d_pre))
            upstream, d_normed, d_logits = backward_experts(
                routed, kept["returned"], upstream, d_sent, weights
            )
            if len(last) == steps:
                one = jax.tree.map(lambda a, b: jnp.where(top, a, b), last[0], last[2])
                moving = up_pieces(one[2:], last[1][2:], count)
            below, *pieces = backward_mixer(upstream, kept, d_normed, d_logits, weights)
            grads.append(below)
            found.append(pieces)
    outputs = jnp.stack(
        [jnp.where(top, results[m + 1], results[m]) for m in range(micro)], 0
    )
    backs = jnp.stack([jnp.where(top, grads[m], grads[m + 1]) for m in range(micro)], 0)

    def valid_one(place):
        return jax.tree.map(lambda a, b: jnp.where(top, a, b), found[0][place], found[2][place])

    vectors = jax.tree.map(lambda a, b: a + b, valid_one(1), found[1][1])
    mixer = mixer_grads([valid_one(0), found[1][0]], vectors, places, moving, count)
    down = down_grad(one[:2], last[1][:2])
    return (outputs[None], backs[None]) + tuple(v[None] for v in mixer) + (down[None],)


def solution(mesh):
    both = ("dp", "expert")
    weights = (
        P("section", "dp"),
        P("section", None, None, both),
        P("section", None, both),
        P("section", both),
        P("section", both, None),
        P("section", None, both),
        P("section", both),
        P("section", None, both),
        P("section", both),
        P("section", both, None),
        P("section", "dp"),
        P("section", "dp", None),
        P("section", "expert", "dp", None),
        P("section", "expert", "dp", None),
    )
    return jax.shard_map(
        shards,
        mesh=mesh,
        in_specs=(P(None, both, None),) * 2 + (P("section", None, both),) * 3 + weights,
        out_specs=(P("section", None, both, None),) * 2 + weights,
        check_vma=False,
    )
```

```python
import functools

import jax
import jax.numpy as jnp
from jax import lax
from jax.experimental import pallas as pl
from jax.experimental.pallas import tpu as pltpu
from jax.sharding import PartitionSpec as P

EXPERTS = 8
CAP = 12
LANES = 128
CHUNK = 8
HALO = 16
LOG2E = 1.4426950408889634
MESH = pl.DeviceIdType.MESH
MIB = 2**20

epsilon = 1e-05
highest = lax.Precision.HIGHEST
f32 = jnp.float32
bf16 = jnp.bfloat16


def tiles_of(width):
    return [slice(i * LANES, (i + 1) * LANES) for i in range(width // LANES)]


def lanes_at(block, width):
    return pl.ds(pl.multiple_of(block * width, LANES), width)


def scan_final(step_ref, drive_ref, bb_ref, a_ref, state, total, width):
    states = a_ref.shape[0]
    tiles = tiles_of(width)
    each = state.shape[2] // width

    def block(b, unused):
        lanes = lanes_at(b, width)
        rates = [a_ref[:, lanes][:, t] for t in tiles]

        def body(i, carry):
            base = pl.multiple_of(i * CHUNK, CHUNK)
            step = step_ref[pl.ds(base, CHUNK), lanes]
            drive = drive_ref[pl.ds(base, CHUNK), lanes]
            carry, sums = list(carry[0]), carry[1]
            for k in range(CHUNK):
                in_map = bb_ref[base + k]
                for j, t in enumerate(tiles):
                    decay = jnp.exp2(step[k : k + 1, t] * rates[j])
                    carry[j] = decay * carry[j] + drive[k : k + 1, t] * in_map
            return tuple(carry), sums + step

        zeros = tuple(jnp.zeros((states, LANES), f32) for _ in tiles)
        final, sums = lax.fori_loop(
            0, step_ref.shape[0] // CHUNK, body, (zeros, jnp.zeros((CHUNK, width), f32))
        )
        side, at = lax.div(b, each), lanes_at(lax.rem(b, each), width)
        state[side, :, at] = jnp.concatenate(final, 1)
        total[side, :, at] = jnp.sum(sums, 0, keepdims=True)
        return unused

    lax.fori_loop(0, 2 * each, block, 0)


def scan_leak(step_ref, dy_ref, cb_ref, a_ref, state, total, width):
    states = a_ref.shape[0]
    tiles = tiles_of(width)
    each = state.shape[2] // width
    count = step_ref.shape[0] // CHUNK

    def block(b, unused):
        lanes = lanes_at(b, width)
        rates = [a_ref[:, lanes][:, t] for t in tiles]

        def body(i, carry):
            base = pl.multiple_of((count - 1 - i) * CHUNK, CHUNK)
            step = step_ref[pl.ds(base, CHUNK), lanes]
            dys = dy_ref[pl.ds(base, CHUNK), lanes]
            carry, sums = list(carry[0]), carry[1]
            for k in reversed(range(CHUNK)):
                out_map = cb_ref[base + k]
                for j, t in enumerate(tiles):
                    decay = jnp.exp2(step[k : k + 1, t] * rates[j])
                    carry[j] = decay * (carry[j] + dys[k : k + 1, t] * out_map)
            return tuple(carry), sums + step

        zeros = tuple(jnp.zeros((states, LANES), f32) for _ in tiles)
        final, sums = lax.fori_loop(0, count, body, (zeros, jnp.zeros((CHUNK, width), f32)))
        side, at = lax.div(b, each), lanes_at(lax.rem(b, each), width)
        state[side, :, at] = jnp.concatenate(final, 1)
        total[side, :, at] = jnp.sum(sums, 0, keepdims=True)
        return unused

    lax.fori_loop(0, 2 * each, block, 0)


def scan_outputs(step_ref, drive_ref, bb_ref, cb_ref, a_ref, entering, y_ref, starts_ref, width):
    tiles = tiles_of(width)
    each = entering.shape[2] // width

    def block(b, unused):
        lanes = lanes_at(b, width)
        rates = [a_ref[:, lanes][:, t] for t in tiles]

        def body(i, carry):
            base = pl.multiple_of(i * CHUNK, CHUNK)
            step = step_ref[pl.ds(base, CHUNK), lanes]
            drive = drive_ref[pl.ds(base, CHUNK), lanes]
            carry = list(carry)
            starts_ref[i, :, lanes] = jnp.concatenate(carry, 1)
            rows = [[] for _ in tiles]
            for k in range(CHUNK):
                in_map = bb_ref[base + k]
                out_map = cb_ref[base + k]
                for j, t in enumerate(tiles):
                    decay = jnp.exp2(step[k : k + 1, t] * rates[j])
                    carry[j] = decay * carry[j] + drive[k : k + 1, t] * in_map
                    rows[j].append(jnp.sum(carry[j] * out_map, 0, keepdims=True))
            y_ref[pl.ds(base, CHUNK), lanes] = jnp.concatenate(
                [jnp.concatenate(row, 0) for row in rows], 1
            )
            return tuple(carry)

        first = entering[lax.div(b, each), :, lanes_at(lax.rem(b, each), width)]
        lax.fori_loop(0, step_ref.shape[0] // CHUNK, body, tuple(first[:, t] for t in tiles))
        return unused

    lax.fori_loop(0, 2 * each, block, 0)


def scan_back(
    step_ref, drive_ref, dy_ref, bb_ref, cb_ref, a_ref, starts_ref, inflow, through_ref, flow_ref, db_ref,
    dc_ref, da_ref, width,
):
    tiles = tiles_of(width)
    each = inflow.shape[2] // width
    count = step_ref.shape[0] // CHUNK
    db_ref[...] = jnp.zeros_like(db_ref)
    dc_ref[...] = jnp.zeros_like(dc_ref)

    def block(b, unused):
        lanes = lanes_at(b, width)
        rates = [a_ref[:, lanes][:, t] for t in tiles]

        def body(i, carry):
            grads, d_rates = list(carry[0]), list(carry[1])
            chunk = count - 1 - i
            base = pl.multiple_of(chunk * CHUNK, CHUNK)
            step = step_ref[pl.ds(base, CHUNK), lanes]
            drive = drive_ref[pl.ds(base, CHUNK), lanes]
            dys = dy_ref[pl.ds(base, CHUNK), lanes]
            start = starts_ref[chunk, :, lanes]
            d_in, d_out = [None] * CHUNK, [None] * CHUNK
            all_through, all_flows = [], []
            for j, t in enumerate(tiles):
                current = start[:, t]
                decays, states = [], [current]
                for k in range(CHUNK):
                    decay = jnp.exp2(step[k : k + 1, t] * rates[j])
                    current = decay * current + drive[k : k + 1, t] * bb_ref[base + k]
                    decays.append(decay)
                    states.append(current)
                grad = grads[j]
                through, flows = [None] * CHUNK, [None] * CHUNK
                for k in reversed(range(CHUNK)):
                    dy = dys[k : k + 1, t]
                    grad = grad + dy * cb_ref[base + k]
                    through[k] = jnp.sum(grad * bb_ref[base + k], 0, keepdims=True)
                    piece = grad * drive[k : k + 1, t]
                    d_in[k] = piece if d_in[k] is None else d_in[k] + piece
                    piece = dy * states[k + 1]
                    d_out[k] = piece if d_out[k] is None else d_out[k] + piece
                    grad = decays[k] * grad
                    flow = grad * states[k]
                    flows[k] = jnp.sum(flow * rates[j], 0, keepdims=True)
                    d_rates[j] = d_rates[j] + flow * step[k : k + 1, t]
                grads[j] = grad
                all_through.append(jnp.concatenate(through, 0))
                all_flows.append(jnp.concatenate(flows, 0))
            through_ref[pl.ds(base, CHUNK), lanes] = jnp.concatenate(all_through, 1)
            flow_ref[pl.ds(base, CHUNK), lanes] = jnp.concatenate(all_flows, 1)
            for k in range(CHUNK):
                db_ref[base + k] += d_in[k]
                dc_ref[base + k] += d_out[k]
            return tuple(grads), tuple(d_rates)

        first = inflow[lax.div(b, each), :, lanes_at(lax.rem(b, each), width)]
        zeros = tuple(jnp.zeros((a_ref.shape[0], LANES), f32) for _ in tiles)
        d_rates = lax.fori_loop(0, count, body, (tuple(first[:, t] for t in tiles), zeros))[1]
        da_ref[:, lanes] = jnp.concatenate(d_rates, 1)
        return unused

    lax.fori_loop(0, 2 * each, block, 0)


def block_width(width, most):
    while width % most:
        most -= LANES
    return most


def shape_of(*shape, dtype=f32):
    return jax.ShapeDtypeStruct(shape, dtype)


def place_of(index, count):
    return jnp.where(
        lax.rem(index, 2) == 0, lax.div(index, 2), count - 1 - lax.div(index, 2)
    )


def index_at(place, count):
    place = lax.rem(place + 2 * count, count)
    return jnp.where(place < (count + 1) // 2, 2 * place, 2 * (count - 1 - place) + 1)


def greet(devices):
    barrier = pltpu.get_barrier_semaphore()
    for device in devices:
        pl.semaphore_signal(barrier, inc=1, device_id=device, device_id_type=MESH)
    pl.semaphore_wait(barrier, len(devices))


def remote(src, dst, send, recv, device):
    return pltpu.make_async_remote_copy(
        src_ref=src, dst_ref=dst, send_sem=send, recv_sem=recv, device_id=device,
        device_id_type=MESH,
    )


def here(count):
    section, dp, core = (lax.axis_index(name) for name in ("section", "dp", "expert"))
    place = place_of(dp, count)
    right = (section, index_at(place + 1, count), core)
    left = (section, index_at(place - 1, count), core)
    return dp, core, place, right, left, (section, dp, 1 - core)


def dp_peers(count):
    section, dp, core = (lax.axis_index(name) for name in ("section", "dp", "expert"))
    return [(section, lax.rem(dp + by, count), core) for by in range(1, count)]


def comm_params(identity, vmem=48):
    return pltpu.CompilerParams(
        collective_id=identity, has_side_effects=True, vmem_limit_bytes=vmem * MIB
    )


anywhere = pl.BlockSpec(memory_space=pl.ANY)
in_vmem = pl.BlockSpec(memory_space=pltpu.VMEM)
dma = pltpu.SemaphoreType.DMA


def gelu_parts(x):
    scale, cubic = 0.7978845608028654, 0.044715
    square = x * x
    t = jnp.tanh(scale * x * (1.0 + cubic * square))
    act = 0.5 * x * (1.0 + t)
    slope = 0.5 * (1.0 + t) + 0.5 * x * (1.0 - t * t) * scale * (1.0 + 3.0 * cubic * square)
    return act, slope


def own_expert(rows, each_rows, hidden):
    each = each_rows // CAP
    row = lax.broadcasted_iota(jnp.int32, (rows, 1), 0)
    for _ in range(rows // each_rows - 1):
        row = jnp.where(row >= each_rows, row - each_rows, row)
    column = lax.broadcasted_iota(jnp.int32, (1, hidden), 1)
    row_expert, column_expert = jnp.zeros_like(row), jnp.zeros_like(column)
    for e in range(1, each):
        row_expert = row_expert + (row >= e * CAP).astype(jnp.int32)
        column_expert = column_expert + (column >= e * (hidden // each)).astype(jnp.int32)
    return row_expert == column_expert


def mm(a, b, dims):
    return lax.dot_general(a, b, (dims, ((), ())), preferred_element_type=f32)


class Round:
    def __init__(self, count, own, held, work, part, out, scratch):
        self.own, self.held, self.work, self.part, self.out = own, held, work, part, out
        self.slots, (self.total, self.pair_in, self.pair_sems) = scratch[:4], scratch[4:7]
        self.sems, self.back_sems, self.local_sem = scratch[7:9], scratch[9:11], scratch[11]
        self.count, self.reach = count, count // 2
        self.dp, self.core, self.place, right, left, self.partner = here(count)
        self.towards = (right, left)

    def source(self, way, k):
        return index_at(self.place - k if way == 0 else self.place + k, self.count)

    def hop(self, way, k, half, src=None):
        sem = self.sems[way]
        slot = self.held.at[self.source(way, k), self.core if half == 0 else 1 - self.core]
        return remote(
            slot if src is None else src, slot, sem.at[0, k, half], sem.at[1, k, half],
            self.towards[way],
        )

    def first(self, half):
        return self.own.at[self.core] if half == 0 else None

    def swap(self):
        return remote(
            self.own.at[1 - self.core], self.held.at[self.dp, self.core], self.pair_sems.at[0, 0],
            self.pair_sems.at[1, 0], self.partner,
        )

    def keep(self):
        return pltpu.make_async_copy(
            self.own.at[self.core], self.held.at[self.dp, self.core], self.local_sem
        )

    def begin(self):
        self.swap().start()
        self.keep().start()
        for way in range(2):
            if self.reach > 1 or way == 0:
                self.hop(way, 0, 0, self.first(0)).start()

    def begin_other(self):
        self.swap().wait_recv()
        for way in range(2):
            if self.reach > 1 or way == 1:
                self.hop(way, 0, 1).start()
        self.keep().wait()

    def further(self, k):
        for half in range(2):
            for way in range(2):
                self.hop(way, k - 1, half).wait_recv()
                if half == way:
                    self.hop(way, k, half).start()
                else:

                    @pl.when(k < self.reach - 1)
                    def _(way=way, half=half):
                        self.hop(way, k, half).start()

    def arrive(self):
        for way in range(2):
            self.hop(way, self.reach - 1, way).wait_recv()

    def back(self, way, k, half):
        sem = self.back_sems[way]
        return remote(
            self.slots[way].at[k, half], self.slots[way + 2].at[k, half], sem.at[0, k, half],
            sem.at[1, k, half], self.towards[way],
        )

    def begin_back(self):
        for way in range(2):
            self.slots[way + 2][0, 1 - way] = jnp.zeros(self.slots[0].shape[2:], bf16)
            self.slots[way][0, way] = self.part[self.source(way, self.reach), way]
            self.back(way, 0, way).start()

    def nearer(self, k):
        for half in range(2):
            for way in range(2):
                owner = self.source(1 - way, self.reach - k)
                piece = self.part[owner, half].astype(f32)
                if half == way:
                    self.back(way, k - 1, half).wait_recv()
                else:

                    @pl.when(k > 1)
                    def _(way=way, half=half):
                        self.back(way, k - 1, half).wait_recv()

                before = self.slots[way + 2][k - 1, half].astype(f32)
                self.slots[way][k, half] = (piece + before).astype(bf16)
                self.back(way, k, half).start()

    def swap_back(self):
        return remote(
            self.total.at[1 - self.core], self.pair_in, self.pair_sems.at[0, 1], self.pair_sems.at[1, 1],
            self.partner,
        )

    def sum_up(self):
        for half in range(2):
            value = self.part[self.dp, half].astype(f32)
            for way in range(2):
                if self.reach > 1 or half == way:
                    self.back(way, self.reach - 1, half).wait_recv()
                    value = value + self.slots[way + 2][self.reach - 1, half].astype(f32)
            self.total[half] = value.astype(bf16)
        self.swap_back().start()

    def end(self):
        self.out[self.core] = self.total[self.core]
        self.swap_back().wait_recv()
        self.out[1 - self.core] = self.pair_in[...]
        self.swap().wait_send()
        self.swap_back().wait_send()

    def finish(self, k):
        for half in range(2):
            for way in range(2):
                if half == way:
                    self.hop(way, k, half, self.first(half)).wait_send()
                    self.back(way, k, half).wait_send()
                else:

                    @pl.when(k < self.reach - 1)
                    def _(way=way, half=half):
                        self.hop(way, k, half, self.first(half)).wait_send()

                    @pl.when(k > 0)
                    def _(way=way, half=half):
                        self.back(way, k, half).wait_send()


def go_round(rounds):
    reach = rounds[0].reach

    def steps(from_step, step):
        def body(k, unused):
            step(k)
            return unused

        lax.fori_loop(from_step, reach, body, 0)

    for one in rounds:
        one.begin()
    for one in rounds:
        one.begin_other()
    for one in rounds:
        one.work([one.dp])

    def further(k):
        for one in rounds:
            one.further(k)
        for one in rounds:
            one.work([one.source(0, k), one.source(1, k)])

    steps(1, further)
    for one in rounds:
        one.arrive()
        one.work([one.source(0, reach)])
        one.begin_back()

    def nearer(k):
        for one in rounds:
            one.nearer(k)

    steps(1, nearer)
    for one in rounds:
        one.sum_up()
    for one in rounds:
        one.end()

    def finish(k):
        for one in rounds:
            one.finish(k)

    steps(0, finish)


def rows_of(held, sources):
    pieces = [held[s].reshape(-1, held.shape[-1]) for s in sources]
    return pieces[0] if len(pieces) == 1 else jnp.concatenate(pieces, 0)


def put_rows(ref, sources, value):
    size = value.shape[0] // len(sources)
    for i, s in enumerate(sources):
        ref[s] = value[i * size : (i + 1) * size].reshape(ref.shape[1:]).astype(ref.dtype)


def block_at(section, index, count):
    index = lax.rem(index + 2 * count, 2 * count)
    return section, lax.div(index, 2), lax.rem(index, 2)


def experts_kernel(count, ahead, behind, cross, *refs):
    refs = list(refs)

    def take(number):
        taken = refs[:number]
        del refs[:number]
        return taken

    if ahead:
        own, resid, table, gate = take(4)
    if behind:
        below = take(1)[0] if cross else None
        above, table_back, gate_back, arrived_hbm = take(4)
    up_hbm, down_hbm = take(2)
    if ahead:
        out, result = take(2)
        next_rows, next_halo = take(2) if cross else (None, None)
        (arrived_out,) = take(1)
    if behind:
        upstream_out, out_back, given_out, hidden_out, slope_out = take(5)
    up, down, load_sems = take(3)
    section = lax.axis_index("section")
    dp, core, place, right, left, partner = here(count)
    block = 2 * dp + core
    across, before, after = (block_at(1 - section, block + by, count) for by in (0, -1, 1))
    greet([right, left, partner] + [across] * cross + [before] * (cross and ahead))
    loads = [
        pltpu.make_async_copy(up_hbm, up, load_sems.at[0]),
        pltpu.make_async_copy(down_hbm, down, load_sems.at[1]),
    ]
    rounds = []
    if ahead:
        held, part = take(2)
        landed, landed_halo, cross_sems = take(3) if cross else (None, None, None)
        scratch = take(12)
        (save_sem,) = take(1)

        def work(sources):
            pre = mm(rows_of(held, sources), up[...], ((1,), (0,)))
            mask = own_expert(pre.shape[0], held.shape[2], pre.shape[1])
            hidden = jnp.where(mask, gelu_parts(pre)[0], 0.0).astype(bf16)
            put_rows(part, sources, mm(hidden, down[...], ((1,), (0,))))

        rounds.append(Round(count, own, held, work, part, out, scratch))
    if behind:
        own_back, held_back, arrived, hidden_all, slope_all, part_back = take(6)
        landed_back, cross_back = take(2) if cross else (None, None)
        scratch_back = take(12)
        (back_sems,) = take(1)
        loads.append(pltpu.make_async_copy(arrived_hbm, arrived, back_sems.at[0]))

        def work_back(sources):
            pre = mm(rows_of(arrived, sources), up[...], ((1,), (0,)))
            mask = own_expert(pre.shape[0], held_back.shape[2], pre.shape[1])
            act, slope = gelu_parts(pre)
            put_rows(hidden_all, sources, jnp.where(mask, act, 0.0))
            d_hidden = mm(rows_of(held_back, sources), down[...], ((1,), (1,)))
            d_pre = jnp.where(mask, d_hidden * slope, 0.0).astype(bf16)
            put_rows(slope_all, sources, d_pre)
            put_rows(part_back, sources, mm(d_pre, up[...], ((1,), (1,))))

        rounds.append(Round(count, own_back, held_back, work_back, part_back, out_back, scratch_back))
    if behind:
        if cross:
            crossing = remote(below, landed_back, cross_back.at[0], cross_back.at[1], across)
            crossing.start()
    for load in loads:
        load.start()
    if behind:
        upstream = above[...].astype(f32)
        if cross:
            crossing.wait_recv()
            upstream = jnp.where(section == 1, upstream, landed_back[...].astype(f32))
        upstream_out[...] = upstream.astype(bf16)
        slots_grad = mm(table_back[...], (upstream * gate_back[...]).astype(bf16), ((1,), (0,)))
        own_back[...] = slots_grad.astype(bf16).reshape(own_back.shape)
    waiting = list(loads)
    for one in rounds:

        def work_first(sources, work=one.work):
            while waiting:
                waiting.pop().wait()
            work(sources)

        one.work = work_first
    go_round(rounds)
    saves = []
    if ahead:
        saves.append(pltpu.make_async_copy(held, arrived_out, save_sem))
    if behind:
        for n, (src, dst) in enumerate(
            ((held_back, given_out), (hidden_all, hidden_out), (slope_all, slope_out))
        ):
            saves.append(pltpu.make_async_copy(src, dst, back_sems.at[1 + n]))
    for save in saves:
        save.start()
    if ahead:
        returned = out[...].reshape(-1, out.shape[2])
        combined = mm(table[...], returned, ((1,), (0,))) * gate[...]
        result[...] = (resid[...] + combined).astype(bf16)
    if ahead and cross:
        length, halo = result.shape[0], next_halo.shape[0]
        copies = [
            remote(result, landed, cross_sems.at[0, 0], cross_sems.at[1, 0], across),
            remote(
                result.at[length - halo : length], landed_halo, cross_sems.at[0, 1], cross_sems.at[1, 1], after
            ),
        ]
        for copy in copies:
            copy.start()
        for copy in copies:
            copy.wait_recv()
        next_rows[...] = landed[...]
        next_halo[...] = jnp.where(block > 0, landed_halo[...].astype(f32), 0.0).astype(bf16)
        for copy in copies:
            copy.wait_send()
    if behind and cross:
        crossing.wait_send()
    for save in saves:
        save.wait()


def experts(up, down, ahead, behind, cross):
    count = lax.axis_size("dp")
    reach = count // 2
    width = (ahead[1] if ahead else behind[-4]).shape[1]
    length = (ahead[1] if ahead else behind[-4]).shape[0]
    rows = (2, EXPERTS * CAP // 2, width)
    gathered = (count,) + rows
    units = (count, 2 * rows[1], up.shape[1])
    around = (
        [pltpu.VMEM((reach,) + rows, bf16)] * 4
        + [pltpu.VMEM(rows, bf16), pltpu.VMEM(rows[1:], bf16), dma((2, 2))]
        + [dma((2, reach, 2))] * 4
        + [dma(())]
    )
    in_specs, out_specs, shapes, scratch = [], [], [], []
    if ahead:
        landing = [(length, width), (HALO, width)] if cross else []
        in_specs += [in_vmem] * 4
        out_specs += [in_vmem] * (2 + len(landing)) + [anywhere]
        shapes += [rows, (length, width)] + landing + [gathered]
        scratch += [pltpu.VMEM(gathered, bf16)] * 2 + [pltpu.VMEM(shape, bf16) for shape in landing]
        scratch += [dma((2, 2))] * cross + around + [dma(())]
    if behind:
        in_specs += [in_vmem] * (len(behind) - 1) + [anywhere]
        out_specs += [in_vmem] * 2 + [anywhere] * 3
        shapes += [(length, width), rows, gathered, units, units]
        scratch += [pltpu.VMEM(rows, bf16)] + [pltpu.VMEM(gathered, bf16)] * 2
        scratch += [pltpu.VMEM(units, bf16)] * 2 + [pltpu.VMEM(gathered, bf16)]
        scratch += [pltpu.VMEM((length, width), bf16), dma((2,))] if cross else []
        scratch += around + [dma((4,))]
    number = 7 if ahead and behind else 1 if ahead else 2
    number += 0 if cross or number == 7 else 7
    return pl.pallas_call(
        functools.partial(experts_kernel, count, bool(ahead), bool(behind), cross),
        in_specs=in_specs + [anywhere] * 2,
        out_specs=out_specs,
        out_shape=[shape_of(*shape, dtype=bf16) for shape in shapes],
        scratch_shapes=[pltpu.VMEM(up.shape, bf16), pltpu.VMEM(down.shape, bf16), dma((2,))] + scratch,
        compiler_params=comm_params(number, 40 if number == 2 and count <= 8 else 60),
        name="experts_both" if number == 7 else "experts_forward" if ahead else "experts_backward",
    )(*(ahead or ()), *(behind or ()), up, down)


def grid_here(count):
    section, dp, core = (lax.axis_index(name) for name in ("section", "dp", "expert"))
    a, b = lax.div(dp, 2), lax.rem(dp, 2)
    line = count // 2

    def at(place):
        return section, 2 * lax.rem(place + line, line) + b, core

    return a, b, core, at(a + 1), at(a - 1), (section, 2 * a + 1 - b, core), (section, dp, 1 - core)


def weights_gather_kernel(count, parts, tokens, wide_up, wide_down, *refs):
    own, refs = refs[:parts], refs[parts:]
    (halos, up_out, low_down), out, refs = refs[:3], refs[3 : parts + 3], refs[parts + 3 :]
    buffer_up, buffer_down, rounded_up, rounded_down, load_sems, up_sems = refs[:6]
    after_sems, before_sems, side_sems, pair_sems, local_sems, halo_sems = refs[6:]
    a, b, core, after, before, beside, partner = grid_here(count)
    line = count // 2
    section, block = lax.axis_index("section"), 2 * (2 * a + b) + core
    greet(dp_peers(count) + [partner, block_at(section, block - 1, count)])
    micro, length = tokens.shape[:2]
    ends = [
        remote(
            tokens.at[m, length - HALO : length], halos.at[m], halo_sems.at[0, m], halo_sems.at[1, m],
            block_at(section, block + 1, count),
        )
        for m in range(micro)
    ]
    for copy in ends:
        copy.start()

    def slot(p, place, which):
        return out[p].at[core, 2 * place + which]

    def source(p, place, k):
        return own[p] if isinstance(k, int) and k == 0 else slot(p, place, b)

    def along(way, k, p):
        place = a - k if way == 0 else a + k
        sems = after_sems if way == 0 else before_sems
        return remote(
            source(p, place, k), slot(p, place, b), sems.at[0, k, p], sems.at[1, k, p],
            after if way == 0 else before,
        )

    def aside(place, k, p):
        return remote(
            source(p, place, k), slot(p, place, b), side_sems.at[0, place, p], side_sems.at[1, place, p],
            beside,
        )

    def across(place, which, k, p):
        src = source(p, place, k) if which is b else slot(p, place, which)
        number = 2 * place + which
        return remote(
            src, slot(p, place, which), pair_sems.at[0, number, p], pair_sems.at[1, number, p], partner
        )

    def has(way, k):
        return a - k >= 0 if way == 0 else a + k < line

    def goes(way):
        return a + 1 < line if way == 0 else a >= 1

    for p in range(parts):
        aside(a, 0, p).start()
        for way in range(2):

            @pl.when(goes(way))
            def _(way=way, p=p):
                along(way, 0, p).start()

    keeps = [
        pltpu.make_async_copy(own[p], slot(p, a, b), local_sems.at[p]) for p in range(parts)
    ]
    for p in range(parts):
        across(a, b, 0, p).start()
        keeps[p].start()
    loads = [
        pltpu.make_async_copy(wide_up, buffer_up, load_sems.at[0]),
        pltpu.make_async_copy(wide_down, buffer_down, load_sems.at[1]),
    ]
    save = pltpu.make_async_copy(rounded_down, low_down, load_sems.at[2])
    for load in loads:
        load.start()
    loads[0].wait()
    each, depth, hidden = wide_up.shape
    cut = hidden // count
    for piece in range(count):
        for e in range(each):
            rounded_up[piece, :, e * cut : (e + 1) * cut] = buffer_up[
                e, :, piece * cut : (piece + 1) * cut
            ].astype(bf16)
    start, end = exchange(count, rounded_up, up_out, up_sems, load_sems.at[3])
    start(0)
    start(1)
    loads[1].wait()

    def rounding(e, unused):
        rounded_down[e] = buffer_down[e].astype(bf16)
        return unused

    lax.fori_loop(0, each, rounding, 0)
    save.start()

    def came_aside(place, p):
        aside(place, None, p).wait_recv()
        across(place, 1 - b, None, p).start()

    def arrivals(k, unused):
        for p in range(parts):
            for way in range(2):

                @pl.when(has(way, k))
                def _(way=way, p=p):
                    place = a - k if way == 0 else a + k
                    along(way, k - 1, p).wait_recv()

                    @pl.when(goes(way))
                    def _():
                        along(way, k, p).start()

                    aside(place, None, p).start()
                    across(place, b, None, p).start()

        for p in range(parts):

            @pl.when(k == 1)
            def _(p=p):
                came_aside(a, p)

            for way in range(2):

                @pl.when((k > 1) & has(way, k - 1))
                def _(way=way, p=p):
                    came_aside(a - k + 1 if way == 0 else a + k - 1, p)

        return unused

    lax.fori_loop(1, line, arrivals, 0)
    for p in range(parts):
        if line == 1:
            came_aside(a, p)
        for way in range(2):

            @pl.when((line > 1) & has(way, line - 1))
            def _(way=way, p=p):
                came_aside(a - line + 1 if way == 0 else a + line - 1, p)

    for p in range(parts):
        keeps[p].wait()

    def finish(place, unused):
        for p in range(parts):
            for which in range(2):
                copy = across(place, which, None, p)
                copy.wait_recv()
                copy.wait_send()
            aside(place, None, p).wait_send()
        return unused

    lax.fori_loop(0, line, finish, 0)

    def sent(k, unused):
        for p in range(parts):
            for way in range(2):

                @pl.when(has(way, k) & goes(way))
                def _(way=way, p=p):
                    along(way, k, p).wait_send()

        return unused

    lax.fori_loop(0, line, sent, 0)
    save.wait()
    end()
    for copy in ends:
        copy.wait()


def weights_gather(tokens, up, down, own):
    count = lax.axis_size("dp")
    reach = count // 2
    parts = len(own)
    pieces = (count, up.shape[1], up.shape[0] * up.shape[2] // count)
    return pl.pallas_call(
        functools.partial(weights_gather_kernel, count, parts),
        in_specs=[anywhere] * (parts + 3),
        out_specs=[anywhere] * (parts + 3),
        out_shape=[shape_of(tokens.shape[0], HALO, tokens.shape[2], dtype=bf16)]
        + [shape_of(*pieces, dtype=bf16), shape_of(*down.shape, dtype=bf16)]
        + [shape_of(2, count, *part.shape, dtype=part.dtype) for part in own],
        scratch_shapes=[
            pltpu.VMEM(up.shape, f32),
            pltpu.VMEM(down.shape, f32),
            pltpu.VMEM(pieces, bf16),
            pltpu.VMEM(down.shape, bf16),
            dma((4,)),
            dma((2, count - 1)),
            dma((2, reach, parts)),
            dma((2, reach, parts)),
            dma((2, reach, parts)),
            dma((2, count, parts)),
            dma((parts,)),
            dma((2, tokens.shape[0])),
        ],
        compiler_params=comm_params(3),
        name="weights_gather",
    )(tokens, up, down, *own)


def grads_reduce_kernel(count, micro, vec, pieces, *refs):
    refs = list(refs)

    def take(number):
        taken = refs[:number]
        del refs[:number]
        return taken

    given = [take(8) for _ in range(micro)]
    (up_out,), out = take(1), take(4)
    wholes, halves, (vecs, landed) = take(4), take(5), take(2)
    part, sides, ins = take(4), take(4), (take(4), take(4))
    whole_sems, half_sems, vec_sems, after_sems, before_sems, side_sems, piece_sems, local_sem = refs
    a, b, core, after, before, beside, partner = grid_here(count)
    line = count // 2
    parts = len(part)
    half = halves[0].shape[1]
    length = given[0][0].shape[0]
    greet_all(count)

    def lanes(side, begin):
        return pl.ds(pl.multiple_of(begin + side * half, LANES), half)

    def moves_of(i, n, which):
        place, there = pl.ds(i * length, length), pl.ds((micro + i) * length, length)
        if n < 4:
            src, dst = given[i][n], wholes[n]
            if which == 0:
                return pltpu.make_async_copy(src, dst.at[place], whole_sems.at[2, i, n])
            return remote(src, dst.at[there], whole_sems.at[0, i, n], whole_sems.at[1, i, n], partner)
        n -= 4
        src, begin = (given[i][4], n * 2 * half) if n < 2 else (given[i][3 + n], 0)
        dst = halves[n]
        if which == 0:
            return pltpu.make_async_copy(
                src.at[:, lanes(core, begin)], dst.at[place], half_sems.at[2, i, n]
            )
        return remote(
            src.at[:, lanes(1 - core, begin)], dst.at[there], half_sems.at[0, i, n], half_sems.at[1, i, n],
            partner,
        )

    order = (0, 4, 5, 1, 6, 2, 7, 3, 8)
    for n in order:
        for i in range(micro):
            for which in range(2):
                moves_of(i, n, which).start()
    vec_copies = (
        pltpu.make_async_copy(vec.at[core], vecs.at[0], vec_sems.at[2]),
        remote(vec.at[1 - core], vecs.at[1], vec_sems.at[0], vec_sems.at[1], partner),
    )
    for copy in vec_copies:
        copy.start()
    start, end = exchange(count, pieces, landed, piece_sems, local_sem)
    start(0)

    def ready(n):
        for i in range(micro):
            moves_of(i, n, 0).wait()
            moves_of(i, n, 1).wait_recv()

    def aside(place, p):
        return remote(
            part[p].at[2 * place + 1 - b], sides[p].at[place], side_sems.at[0, place, p],
            side_sems.at[1, place, p], beside,
        )

    def along(way, place, p):
        sems = after_sems if way == 0 else before_sems
        return remote(
            part[p].at[2 * place + b], ins[way][p].at[place], sems.at[0, place, p], sems.at[1, place, p],
            after if way == 0 else before,
        )

    def far(way, k):
        return line - 1 - k if way == 0 else k

    def put(p, value):
        share = part[p].shape[1]
        for index in range(count):
            part[p][index] = value[index * share : (index + 1) * share].astype(bf16)

        def starts(k, unused):
            for way in range(2):

                @pl.when((way == 0) | (far(0, k) != far(1, k)))
                def _(way=way):
                    aside(far(way, k), p).start()

            return unused

        lax.fori_loop(0, (line + 1) // 2, starts, 0)

    def both_lines(place, p):
        aside(place, p).wait_recv()
        return part[p][2 * place + b].astype(f32) + sides[p][place].astype(f32)

    def passing(k, p):
        for way in range(2):
            place = far(way, k)

            @pl.when(place > a if way == 0 else place < a)
            def _(way=way, place=place):
                index = 2 * place + b
                part[p][index] = both_lines(place, p).astype(bf16)

                @pl.when(a > 0 if way == 0 else a < line - 1)
                def _():
                    along(way, place, p).wait_recv()
                    value = part[p][index].astype(f32) + ins[way][p][place].astype(f32)
                    part[p][index] = value.astype(bf16)

                along(way, place, p).start()

    over = ((0,), (0,))
    ready(0)
    ready(4)
    put(0, mm(halves[0][...], wholes[0][...], over))
    ready(5)
    put(1, mm(halves[1][...], wholes[0][...], over))
    ready(1)
    ready(6)
    put(2, mm(halves[2][...], wholes[1][...], over))
    start(1)
    for n in (2, 7, 3, 8):
        ready(n)
    vec_copies[0].wait()
    vec_copies[1].wait_recv()
    put(
        3,
        jnp.concatenate(
            [
                mm(halves[3][...], wholes[2][...], over),
                mm(halves[4][...], wholes[3][...], over),
            ],
            1,
        )
        + vecs[0].astype(f32)
        + vecs[1].astype(f32),
    )
    for p in range(parts):

        def passing_on(k, unused, p=p):
            passing(k, p)
            return unused

        lax.fori_loop(0, line - 1, passing_on, 0)
    for p in range(parts):
        out[p][...] = both_lines(a, p)
        for way in range(2):

            @pl.when(a > 0 if way == 0 else a < line - 1)
            def _(way=way, p=p):
                along(way, a, p).wait_recv()
                out[p][...] = out[p][...] + ins[way][p][a].astype(f32)

    def finish(place, unused):
        for p in range(parts):
            aside(place, p).wait_send()
            for way in range(2):

                @pl.when(place > a if way == 0 else place < a)
                def _(way=way, p=p):
                    along(way, place, p).wait_send()

        return unused

    lax.fori_loop(0, line, finish, 0)
    for n in order:
        for i in range(micro):
            moves_of(i, n, 1).wait_send()
    vec_copies[1].wait_send()
    end()
    each, depth, hidden = up_out.shape
    cut = hidden // count
    for piece in range(count):
        for e in range(each):
            up_out[e, :, piece * cut : (piece + 1) * cut] = landed[
                piece, :, e * cut : (e + 1) * cut
            ]


def grads_reduce(vec, pieces, given):
    count = lax.axis_size("dp")
    line = count // 2
    micro = len(given)
    length, model = given[0][0].shape
    half, lanes = vec.shape[1:]
    share = half // count
    each = EXPERTS // 2
    rows = 2 * micro * length
    shares = [(share, model)] * 3 + [(share, lanes)]
    wholes = [value.shape[1] for value in given[0][:4]]
    return pl.pallas_call(
        functools.partial(grads_reduce_kernel, count, micro),
        in_specs=[anywhere] * (2 + 8 * micro),
        out_specs=[in_vmem] * 5,
        out_shape=[shape_of(each, pieces.shape[1], count * pieces.shape[2] // each, dtype=bf16)]
        + [shape_of(*shape) for shape in shares],
        scratch_shapes=[pltpu.VMEM((rows, width), bf16) for width in wholes]
        + [pltpu.VMEM((rows, half), bf16)] * 5
        + [pltpu.VMEM((2, half, lanes), bf16), pltpu.VMEM(pieces.shape, bf16)]
        + [pltpu.VMEM((count,) + shape, bf16) for shape in shares]
        + [pltpu.VMEM((line,) + shape, bf16) for shape in shares] * 3
        + [dma((3, micro, 4)), dma((3, micro, 5)), dma((3,))]
        + [dma((2, line, 4))] * 3
        + [dma((2, count - 1)), dma(())],
        compiler_params=comm_params(4, 60),
        name="grads_reduce",
    )(vec, pieces, *[value for one in given for value in one])


def join(
    count, forward, state_ref, total_ref, rates, out_ref, other_state, other_total, mine, mine_total, states,
    totals, back, back_in, pair_sems, sems,
):
    section, dp, core = (lax.axis_index(name) for name in ("section", "dp", "expert"))
    partner = (section, dp, 1 - core)
    swap = [
        remote(state_ref.at[1 - core], other_state, pair_sems.at[0, 0], pair_sems.at[1, 0], partner),
        remote(total_ref.at[1 - core], other_total, pair_sems.at[0, 1], pair_sems.at[1, 1], partner),
    ]
    for copy in swap:
        copy.start()
    own_state, own_total = state_ref[core], total_ref[core]
    for copy in swap:
        copy.wait_recv()
    leads = core == (0 if forward else 1)
    first_state = jnp.where(leads, own_state, other_state[...])
    first_total = jnp.where(leads, own_total, other_total[...])
    second_state = jnp.where(leads, other_state[...], own_state)
    second_total = jnp.where(leads, other_total[...], own_total)
    mine[...] = (jnp.exp2(rates * second_total) * first_state + second_state).astype(bf16)
    mine_total[...] = first_total + second_total
    copies = []
    for d, peer in enumerate(dp_peers(count)):
        for n, (src, dst) in enumerate(((mine, states), (mine_total, totals))):
            copy = remote(src, dst.at[dp], sems.at[0, d, n], sems.at[1, d, n], peer)
            copy.start()
            copies.append(copy)
    states[dp] = mine[...]
    totals[dp] = mine_total[...]
    for copy in copies:
        copy.wait_recv()

    entering = jnp.zeros_like(own_state)
    for k in range(count):
        source = k if forward else count - 1 - k
        reached = (source < dp) if forward else (source > dp)
        fresh = jnp.exp2(rates * totals[source]) * entering + states[source].astype(f32)
        entering = jnp.where(reached, fresh, entering)
    after = jnp.exp2(rates * first_total) * entering + first_state
    back[...] = jnp.where(leads, after, entering)
    swap_back = remote(back, back_in, pair_sems.at[0, 2], pair_sems.at[1, 2], partner)
    swap_back.start()
    out_ref[core] = jnp.where(leads, entering, after)
    swap_back.wait_recv()
    out_ref[1 - core] = back_in[...]
    for copy in swap + copies + [swap_back]:
        copy.wait_send()


def join_scratch(count, states, half):
    one, sums = pltpu.VMEM((states, half), f32), pltpu.VMEM((1, half), f32)
    return [
        pltpu.VMEM((2, states, half), f32),
        pltpu.VMEM((2, 1, half), f32),
        pltpu.VMEM((2, states, half), f32),
        one,
        sums,
        pltpu.VMEM((states, half), bf16),
        sums,
        pltpu.VMEM((count, states, half), bf16),
        pltpu.VMEM((count, 1, half), f32),
        one,
        one,
        dma((2, 3)),
        dma((2, count - 1, 2)),
    ]


def own_lanes(a_ref, half):
    return a_ref[:, lanes_at(lax.axis_index("expert"), half)]


def greet_all(count):
    section, dp, core = (lax.axis_index(name) for name in ("section", "dp", "expert"))
    greet(dp_peers(count) + [(section, dp, 1 - core)])


def exchange(count, pieces_ref, out_ref, sems, local_sem):
    dp = lax.axis_index("dp")
    keep = pltpu.make_async_copy(pieces_ref.at[dp], out_ref.at[dp], local_sem)
    keep.start()
    copies = []
    for by, peer in enumerate(dp_peers(count)):
        copies.append(
            remote(pieces_ref.at[peer[1]], out_ref.at[dp], sems.at[0, by], sems.at[1, by], peer)
        )

    def start(beside):
        for copy in copies[1 - beside :: 2]:
            copy.start()

    def end():
        keep.wait()
        for copy in copies:
            copy.wait()

    return start, end


def mixer_forward_kernel(
    count, step_ref, drive_ref, bb_ref, cb_ref, a_ref, y_ref, starts_ref, state, total, entering, *rest
):
    half = state.shape[2]
    width = block_width(half, 384)
    scan_final(step_ref, drive_ref, bb_ref, a_ref, state, total, width)
    greet_all(count)
    join(count, True, state, total, own_lanes(a_ref, half), entering, *rest)
    scan_outputs(step_ref, drive_ref, bb_ref, cb_ref, a_ref, entering, y_ref, starts_ref, width)


def mixer_forward(step, drive, in_map, out_map, rates):
    count = lax.axis_size("dp")
    (length, width), states = step.shape, rates.shape[0]
    return pl.pallas_call(
        functools.partial(mixer_forward_kernel, count),
        in_specs=[in_vmem] * 5,
        out_specs=[in_vmem] * 2,
        out_shape=[shape_of(length, width), shape_of(length // CHUNK, states, width)],
        scratch_shapes=join_scratch(count, states, width // 2),
        compiler_params=comm_params(5),
        name="mixer_forward",
    )(step, drive, in_map, out_map, rates)


def mixer_backward_kernel(
    count, step_ref, drive_ref, dy_ref, bb_ref, cb_ref, a_ref, starts_ref, through_ref, flow_ref, db_ref, dc_ref,
    da_ref, state, total, inflow, *rest,
):
    half = state.shape[2]
    width = block_width(half, 384)
    scan_leak(step_ref, dy_ref, cb_ref, a_ref, state, total, width)
    greet_all(count)
    join(count, False, state, total, own_lanes(a_ref, half), inflow, *rest)
    scan_back(
        step_ref, drive_ref, dy_ref, bb_ref, cb_ref, a_ref, starts_ref, inflow, through_ref, flow_ref, db_ref,
        dc_ref, da_ref, width,
    )


def mixer_backward(step, drive, dy, in_map, out_map, rates, starts):
    count = lax.axis_size("dp")
    (length, width), states = step.shape, rates.shape[0]
    wide, maps = shape_of(length, width), shape_of(*in_map.shape)
    return pl.pallas_call(
        functools.partial(mixer_backward_kernel, count),
        in_specs=[in_vmem] * 7,
        out_specs=[in_vmem] * 5,
        out_shape=[wide, wide, maps, maps, shape_of(states, width)],
        scratch_shapes=join_scratch(count, states, width // 2),
        compiler_params=comm_params(6),
        name="mixer_backward",
    )(step, drive, dy, in_map, out_map, rates, starts)


def dot(a, b, dims, dtype=f32):
    return lax.dot_general(a, b, (dims, ((), ())), preferred_element_type=f32).astype(dtype)


def nn(a, b, dtype=f32):
    return dot(a, b, ((1,), (0,)), dtype)


def nt(a, b, dtype=f32):
    return dot(a, b, ((1,), (1,)), dtype)


def tn(a, b, dtype=f32):
    return dot(a, b, ((0,), (0,)), dtype)


def normalize(values, gain):
    return values * lax.rsqrt(jnp.mean(values * values, axis=-1, keepdims=True) + epsilon) * gain


def sums(value):
    return jnp.sum(value, 0)


def normalize_back(values, gain, upstream):
    scale = lax.rsqrt(jnp.mean(values * values, axis=-1, keepdims=True) + epsilon)
    unit = values * scale
    inner = upstream * gain
    d_values = scale * (inner - unit * jnp.mean(inner * unit, axis=-1, keepdims=True))
    return d_values, sums(upstream * unit)


def from_behind(shard, axis, by):
    count = 1
    for name in (axis,) if isinstance(axis, str) else axis:
        count *= lax.axis_size(name)
    pairs = [(i, i + by) for i in range(count) if 0 <= i + by < count]
    return lax.ppermute(shard, axis, pairs)


def swap_pair(value):
    return lax.ppermute(value, "expert", [(0, 1), (1, 0)])


def spread(values):
    return jnp.broadcast_to(values[:, :, None], values.shape + (LANES,))


def routing(resid, moe_gain, router, chosen, placed, dropped):
    normed = normalize(resid, moe_gain)
    probs = jax.nn.softmax(jnp.dot(normed, router, precision=highest), axis=-1)
    keep = (1 - dropped).astype(f32)
    pick = (chosen[:, None] == jnp.arange(EXPERTS)[None]).astype(f32)
    gate = jnp.sum(probs * pick, -1) * keep
    flat = chosen * CAP + placed
    table = ((flat[:, None] == jnp.arange(EXPERTS * CAP)[None]) & (dropped[:, None] == 0)).astype(
        bf16
    )
    return normed, probs, pick, keep, gate, table


def by_core(buffer):
    return buffer.reshape(2, -1, buffer.shape[1])


def mixed(xz, weights):
    width = weights["w_out"].shape[0]
    taps = weights["conv_w"].shape[0]
    length = xz.shape[0] - HALO
    padded = xz[HALO - taps + 1 :, :width]
    summed = weights["conv_b"]
    for tap in range(taps):
        summed = summed + weights["conv_w"][tap : tap + 1] * padded[tap : tap + length]
    return padded, summed, xz[HALO:, width:]


def selective(projected, weights):
    rank = weights["rank"]
    states = weights["rates"].shape[0]
    dt_low = jnp.where(jnp.arange(projected.shape[1])[None] < rank, projected, 0.0).astype(bf16)
    dt_raw = nn(dt_low, weights["dt_proj"]) + weights["dt_bias"]
    in_map = projected[:, rank : rank + states]
    out_map = projected[:, rank + states : rank + 2 * states]
    return dt_low, dt_raw, jax.nn.softplus(dt_raw), spread(in_map), spread(out_map)


def forward(rows, halo, chosen, placed, dropped, weights):
    inputs = jnp.concatenate([halo, rows], 0).astype(f32)
    normed = normalize(inputs, weights["norm_gain"]).astype(bf16)
    xz = nt(normed, weights["w_in"])
    padded, summed, gate_in = mixed(xz, weights)
    signal = jax.nn.silu(summed).astype(bf16)
    projected = nn(signal, weights["x_proj"])
    dt_low, dt_raw, step, in_map, out_map = selective(projected, weights)
    wide = signal.astype(f32)
    drive = step * wide
    rates = weights["rates"] * LOG2E
    scanned, starts = mixer_forward(step, drive, in_map, out_map, rates)
    gated = ((scanned + weights["skip"] * wide) * jax.nn.silu(gate_in)).astype(bf16)
    resid = rows.astype(f32) + nn(gated, weights["w_out"])
    normed_moe, probs, pick, keep, gate, table = routing(
        resid, weights["moe_gain"], weights["router"], chosen, placed, dropped
    )
    buffer = tn(table, normed_moe.astype(bf16), bf16)
    ahead = (by_core(buffer), resid, table, gate[:, None])
    kept = dict(
        rows=rows, halo=halo, xz=xz, projected=projected, scanned=scanned, starts=starts, resid=resid,
    )
    return ahead, kept


def backward_routing(kept, chosen, placed, dropped, weights):
    return routing(
        kept["resid"], weights["moe_gain"], weights["router"], chosen, placed, dropped
    )


def backward_experts(routed, returned, upstream, d_sent, weights):
    normed_moe, probs, pick, keep, gate, table = routed
    d_sent = d_sent.reshape(-1, d_sent.shape[2])
    returned = returned.reshape(d_sent.shape)
    upstream = upstream.astype(f32)
    d_gate = jnp.sum(upstream * nn(table, returned), -1)
    d_choice = d_gate[:, None] * pick * keep[:, None]
    d_logits = probs * (d_choice - jnp.sum(probs * d_choice, -1, keepdims=True))
    d_normed = nn(table, d_sent) + jnp.dot(d_logits, weights["router"].T, precision=highest)
    return upstream, d_normed, d_logits


def backward_mixer(upstream, kept, d_normed, d_logits, weights):
    resid = kept["resid"]
    normed_moe = normalize(resid, weights["moe_gain"])
    grad_router = lax.dot_general(
        normed_moe, d_logits, (((0,), (0,)), ((), ())), precision=highest
    )
    d_norm, grad_moe = normalize_back(resid, weights["moe_gain"], d_normed)
    d_resid = upstream + d_norm

    inputs = kept["rows"].astype(f32)
    normed = normalize(inputs, weights["norm_gain"]).astype(bf16)
    xz = kept["xz"]
    padded, summed, gate_in = mixed(xz, weights)
    signal_act, signal_back = jax.vjp(jax.nn.silu, summed)
    signal = signal_act.astype(bf16)
    wide = signal.astype(f32)
    dt_low, dt_raw, step, in_map, out_map = selective(kept["projected"], weights)
    drive = step * wide
    rates = weights["rates"] * LOG2E
    skip = weights["skip"]
    total_out = kept["scanned"] + skip * wide
    gate_act, gate_back = jax.vjp(jax.nn.silu, gate_in)
    gated = (total_out * gate_act).astype(bf16)
    d_mixer = d_resid.astype(bf16)
    d_gated = nt(d_mixer, weights["w_out"])
    d_total = d_gated * gate_act
    d_gate_in = gate_back(d_gated * total_out)[0]
    grad_skip = sums(d_total * wide)
    through, flow, d_in_map, d_out_map, d_rates = mixer_backward(
        step, drive, d_total, in_map, out_map, rates, kept["starts"]
    )
    d_step = flow / LOG2E + through * wide
    d_signal = step * through + d_total * skip
    d_raw = d_step * jax.nn.sigmoid(dt_raw)
    grad_dt_bias = sums(d_raw)
    d_raw_low = d_raw.astype(bf16)
    d_low = nt(d_raw_low, weights["dt_proj"])
    rank, states = weights["rank"], weights["rates"].shape[0]
    d_maps = jnp.concatenate([jnp.sum(d_in_map, -1), jnp.sum(d_out_map, -1)], 1)
    d_maps = jnp.pad(d_maps, ((0, 0), (rank, d_low.shape[1] - rank - 2 * states)))
    d_projected = (d_low + d_maps).astype(bf16)
    d_signal = d_signal + nt(d_projected, weights["x_proj"])
    d_summed = signal_back(d_signal)[0]
    taps = weights["conv_w"].shape[0]
    length = d_summed.shape[0]
    ahead = from_behind(d_summed[:8], ("dp", "expert"), -1)
    extended = jnp.concatenate([d_summed, ahead], 0)
    d_conv_in = jnp.zeros_like(d_summed)
    for tap in range(taps):
        begin = taps - 1 - tap
        d_conv_in = d_conv_in + weights["conv_w"][tap : tap + 1] * extended[begin : begin + length]
    grad_conv = [
        sums(d_summed * padded[tap : tap + length]) for tap in range(taps)
    ]
    d_xz = jnp.concatenate([d_conv_in, d_gate_in], 1).astype(bf16)
    d_normed_in = nn(d_xz, weights["w_in"])
    d_inputs, grad_norm = normalize_back(inputs, weights["norm_gain"], d_normed_in)
    result = (d_resid + d_inputs).astype(bf16)
    given = (
        normed,
        d_mixer,
        d_projected,
        dt_low,
        d_xz,
        gated,
        signal,
        d_raw_low,
    )
    vectors = (
        grad_conv + [sums(d_summed), grad_dt_bias, grad_skip], d_rates * weights["rates"],
        [grad_norm, grad_moe], grad_router,
    )
    return result, given, vectors


def gather_weights(
    tokens, norm_gain, w_in, conv_w, conv_b, x_proj, dt_proj, dt_bias, a_log, skip, w_out, moe_gain, router,
    w_up, w_down,
):
    count = lax.axis_size("dp")
    share = x_proj.shape[1]
    model = w_out.shape[2]
    low_in = jnp.transpose(w_in[0].astype(bf16), (1, 2, 0))
    pieces = [
        x_proj[0], dt_proj[0].T, conv_w[0].T, conv_b[0][:, None], dt_bias[0][:, None],
        skip[0][:, None], a_log[0].T, norm_gain[0][:, None], moe_gain[0][:, None], router[0],
    ]
    sizes = [piece.shape[1] for piece in pieces]
    lead = -(-sizes[0] // LANES) * LANES
    begins = [0] + [lead + sum(sizes[1:n]) for n in range(1, len(sizes))]
    places = list(zip(begins, sizes, strict=True))
    pieces.insert(1, jnp.zeros((share, lead - sizes[0]), f32))
    pad = (-sum(sizes[1:])) % LANES
    small = jnp.concatenate(pieces + [jnp.zeros((share, pad), f32)], 1).astype(bf16)
    halos, up, low_down, in_x, in_z, out, small = weights_gather(
        tokens, w_up[0], w_down[0], [low_in[0], low_in[1], w_out[0].astype(bf16), small]
    )
    width = 2 * count * share
    w_in_all = jnp.concatenate([in_x.reshape(width, model), in_z.reshape(width, model)], 0)
    table = small.reshape(width, -1)
    rows = table.astype(f32).T
    found = [rows[begin : begin + size] for begin, size in places]
    unused, dt_proj, conv_w, conv_b, dt_bias, a_skip, a_log, norm_gain, moe_gain, router = found
    weights = dict(
        rank=sizes[1],
        w_in=w_in_all,
        w_out=out.reshape(width, model),
        x_proj=table[:, :lead],
        dt_proj=jnp.pad(dt_proj, ((0, lead - sizes[1]), (0, 0))).astype(bf16),
        conv_w=conv_w,
        conv_b=conv_b,
        dt_bias=dt_bias,
        skip=a_skip,
        rates=-jnp.exp(a_log),
        norm_gain=norm_gain[:, :model],
        moe_gain=moe_gain[:, :model],
        router=router[:, :model].T,
        w_up=up.reshape(-1, up.shape[2]),
        w_down=low_down.reshape(-1, model),
    )
    return weights, places, halos


def mixer_grads(given, vectors, places, up, count):
    channel, d_rates, feature, grad_router = vectors
    feature = jnp.concatenate([piece[None] for piece in feature] + [grad_router.T], 0)
    rows = jnp.concatenate(
        [piece[None] for piece in channel] + [d_rates, jnp.concatenate([feature, feature], 1)], 0
    )
    begin = places[2][0]
    lanes = -(-sum(places[-1]) // LANES) * LANES
    vec = jnp.pad(rows.T.astype(bf16), ((0, 0), (begin, lanes - begin - rows.shape[0])))
    vec = vec.reshape(2, -1, lanes)
    up, grad_x, grad_z, grad_out, small = grads_reduce(vec, up, given)
    found = [small[:, begin : begin + size] for begin, size in places]
    x_proj, dt_proj, conv_w, conv_b, dt_bias, skip, a_log, norm_gain, moe_gain, router = found
    return (
        norm_gain[:, 0],
        jnp.transpose(jnp.stack([grad_x, grad_z], 0), (2, 0, 1)),
        conv_w.T,
        conv_b[:, 0],
        x_proj,
        dt_proj.T,
        dt_bias[:, 0],
        a_log.T,
        skip[:, 0],
        grad_out,
        moe_gain[:, 0],
        router,
        up.astype(f32),
    )


def rows_flat(value):
    return value.reshape(-1, value.shape[-1])


def down_grad(first, second):
    hidden, d_produced = (
        jnp.concatenate([rows_flat(a), rows_flat(b)], 0)
        for a, b in zip(first, second, strict=True)
    )
    return tn(hidden, d_produced).reshape(EXPERTS // 2, -1, d_produced.shape[1])


def up_pieces(first, second, count):
    arrived, d_pre = (
        jnp.concatenate([rows_flat(a), rows_flat(b)], 0)
        for a, b in zip(first, second, strict=True)
    )
    return tn(arrived, d_pre, bf16).reshape(count, arrived.shape[1] // count, -1)


def shards(
    tokens, cotangent, routes, slots, drops, norm_gain, w_in, conv_w, conv_b, x_proj, dt_proj, dt_bias,
    a_log, skip, w_out, moe_gain, router, w_up, w_down,
):
    count = lax.axis_size("dp")
    section = lax.axis_index("section")
    top = section == 1
    weights, places, halos = gather_weights(
        tokens, norm_gain, w_in, conv_w, conv_b, x_proj, dt_proj, dt_bias, a_log, skip, w_out, moe_gain,
        router, w_up, w_down,
    )
    micro = tokens.shape[0]
    blocks = ("dp", "expert")
    steps = micro + 1

    def pick(which):
        return [lax.dynamic_index_in_dim(v[0], which, 0, False) for v in (routes, slots, drops)]

    begins = (lax.axis_index("dp") == 0) & (lax.axis_index("expert") == 0)
    halos = jnp.where(begins, jnp.zeros_like(halos), halos)
    incoming, incoming_halo = jnp.zeros_like(tokens[0]), jnp.zeros_like(halos[0])
    results, bank, grads, found, last = [], [], [], [], []
    below = None

    def micro_of(step, first):
        return jnp.clip(step - first, 0, micro - 1)

    def back_parts(step):
        if step == 1:
            kept = jax.tree.map(lambda a, b: jnp.where(top, a, b), bank[2], bank[0])
        else:
            kept = bank[1]
        routed = backward_routing(kept, *pick(micro_of(step, 1 - section)), weights)
        above = cotangent[step] if step < micro else jnp.zeros_like(cotangent[0])
        above = jnp.where(top, above, jnp.zeros_like(above))
        crossing = () if below is None else (below,)
        return kept, routed, crossing + (above, routed[5].T, routed[4][:, None], kept["arrived"])

    for step in range(2 * steps - 1):
        ahead = behind = None
        if step < steps:
            fresh = min(step, micro - 1)
            rows = jnp.where(top, incoming, tokens[fresh])
            halo = jnp.where(top, incoming_halo, halos[fresh])
            ahead, fresh_kept = forward(rows, halo, *pick(micro_of(step, section)), weights)
        if step >= steps - 1:
            kept, routed, behind = back_parts(step - steps + 1)
        cross = (ahead is None) != (behind is None)
        if cross or count <= 8:
            done = experts(weights["w_up"], weights["w_down"], ahead, behind, cross)
        else:
            done = experts(weights["w_up"], weights["w_down"], ahead, None, False)
            done = [*done, *experts(weights["w_up"], weights["w_down"], None, behind, False)]
        if ahead is not None:
            fresh_kept["returned"], result = done[:2]
            if cross:
                incoming, incoming_halo = done[2:4]
            number = 5 if cross else 3
            fresh_kept["arrived"] = done[number - 1]
            results.append(result)
            bank.append(fresh_kept)
            done = done[number:]
        if behind is not None:
            upstream, d_sent, d_produced, hidden, d_pre = done
            last.append((hidden, d_produced, kept["arrived"], d_pre))
            upstream, d_normed, d_logits = backward_experts(
                routed, kept["returned"], upstream, d_sent, weights
            )
            if len(last) == steps:
                one = jax.tree.map(lambda a, b: jnp.where(top, a, b), last[0], last[2])
                moving = up_pieces(one[2:], last[1][2:], count)
            below, *pieces = backward_mixer(upstream, kept, d_normed, d_logits, weights)
            grads.append(below)
            found.append(pieces)
    outputs = jnp.stack(
        [jnp.where(top, results[m + 1], results[m]) for m in range(micro)], 0
    )
    backs = jnp.stack([jnp.where(top, grads[m], grads[m + 1]) for m in range(micro)], 0)

    def valid_one(place):
        return jax.tree.map(lambda a, b: jnp.where(top, a, b), found[0][place], found[2][place])

    vectors = jax.tree.map(lambda a, b: a + b, valid_one(1), found[1][1])
    mixer = mixer_grads([valid_one(0), found[1][0]], vectors, places, moving, count)
    down = down_grad(one[:2], last[1][:2])
    return (outputs[None], backs[None]) + tuple(v[None] for v in mixer) + (down[None],)


def solution(mesh):
    both = ("dp", "expert")
    weights = (
        P("section", "dp"),
        P("section", None, None, both),
        P("section", None, both),
        P("section", both),
        P("section", both, None),
        P("section", None, both),
        P("section", both),
        P("section", None, both),
        P("section", both),
        P("section", both, None),
        P("section", "dp"),
        P("section", "dp", None),
        P("section", "expert", "dp", None),
        P("section", "expert", "dp", None),
    )
    return jax.shard_map(
        shards,
        mesh=mesh,
        in_specs=(P(None, both, None),) * 2 + (P("section", None, both),) * 3 + weights,
        out_specs=(P("section", None, both, None),) * 2 + weights,
        check_vma=False,
    )
```

```python
import functools

import jax
import jax.numpy as jnp
from jax import lax
from jax.experimental import pallas as pl
from jax.experimental.pallas import tpu as pltpu
from jax.sharding import PartitionSpec as P

EXPERTS = 8
CAP = 12
LANES = 128
CHUNK = 8
HALO = 16
LOG2E = 1.4426950408889634
MESH = pl.DeviceIdType.MESH
MIB = 2**20

epsilon = 1e-05
highest = lax.Precision.HIGHEST
f32 = jnp.float32
bf16 = jnp.bfloat16


def tiles_of(width):
    return [slice(i * LANES, (i + 1) * LANES) for i in range(width // LANES)]


def lanes_at(block, width):
    return pl.ds(pl.multiple_of(block * width, LANES), width)


def scan_final(step_ref, drive_ref, bb_ref, a_ref, state, total, width):
    states = a_ref.shape[0]
    tiles = tiles_of(width)
    each = state.shape[2] // width

    def block(b, unused):
        lanes = lanes_at(b, width)
        rates = [a_ref[:, lanes][:, t] for t in tiles]

        def body(i, carry):
            base = pl.multiple_of(i * CHUNK, CHUNK)
            step = step_ref[pl.ds(base, CHUNK), lanes]
            drive = drive_ref[pl.ds(base, CHUNK), lanes]
            carry, sums = list(carry[0]), carry[1]
            for k in range(CHUNK):
                in_map = bb_ref[base + k]
                for j, t in enumerate(tiles):
                    decay = jnp.exp2(step[k : k + 1, t] * rates[j])
                    carry[j] = decay * carry[j] + drive[k : k + 1, t] * in_map
            return tuple(carry), sums + step

        zeros = tuple(jnp.zeros((states, LANES), f32) for _ in tiles)
        final, sums = lax.fori_loop(
            0, step_ref.shape[0] // CHUNK, body, (zeros, jnp.zeros((CHUNK, width), f32))
        )
        side, at = lax.div(b, each), lanes_at(lax.rem(b, each), width)
        state[side, :, at] = jnp.concatenate(final, 1)
        total[side, :, at] = jnp.sum(sums, 0, keepdims=True)
        return unused

    lax.fori_loop(0, 2 * each, block, 0)


def scan_leak(step_ref, dy_ref, cb_ref, a_ref, state, total, width):
    states = a_ref.shape[0]
    tiles = tiles_of(width)
    each = state.shape[2] // width
    count = step_ref.shape[0] // CHUNK

    def block(b, unused):
        lanes = lanes_at(b, width)
        rates = [a_ref[:, lanes][:, t] for t in tiles]

        def body(i, carry):
            base = pl.multiple_of((count - 1 - i) * CHUNK, CHUNK)
            step = step_ref[pl.ds(base, CHUNK), lanes]
            dys = dy_ref[pl.ds(base, CHUNK), lanes]
            carry, sums = list(carry[0]), carry[1]
            for k in reversed(range(CHUNK)):
                out_map = cb_ref[base + k]
                for j, t in enumerate(tiles):
                    decay = jnp.exp2(step[k : k + 1, t] * rates[j])
                    carry[j] = decay * (carry[j] + dys[k : k + 1, t] * out_map)
            return tuple(carry), sums + step

        zeros = tuple(jnp.zeros((states, LANES), f32) for _ in tiles)
        final, sums = lax.fori_loop(0, count, body, (zeros, jnp.zeros((CHUNK, width), f32)))
        side, at = lax.div(b, each), lanes_at(lax.rem(b, each), width)
        state[side, :, at] = jnp.concatenate(final, 1)
        total[side, :, at] = jnp.sum(sums, 0, keepdims=True)
        return unused

    lax.fori_loop(0, 2 * each, block, 0)


def scan_outputs(step_ref, drive_ref, bb_ref, cb_ref, a_ref, entering, y_ref, starts_ref, width):
    tiles = tiles_of(width)
    each = entering.shape[2] // width

    def block(b, unused):
        lanes = lanes_at(b, width)
        rates = [a_ref[:, lanes][:, t] for t in tiles]

        def body(i, carry):
            base = pl.multiple_of(i * CHUNK, CHUNK)
            step = step_ref[pl.ds(base, CHUNK), lanes]
            drive = drive_ref[pl.ds(base, CHUNK), lanes]
            carry = list(carry)
            starts_ref[i, :, lanes] = jnp.concatenate(carry, 1)
            rows = [[] for _ in tiles]
            for k in range(CHUNK):
                in_map = bb_ref[base + k]
                out_map = cb_ref[base + k]
                for j, t in enumerate(tiles):
                    decay = jnp.exp2(step[k : k + 1, t] * rates[j])
                    carry[j] = decay * carry[j] + drive[k : k + 1, t] * in_map
                    rows[j].append(jnp.sum(carry[j] * out_map, 0, keepdims=True))
            y_ref[pl.ds(base, CHUNK), lanes] = jnp.concatenate(
                [jnp.concatenate(row, 0) for row in rows], 1
            )
            return tuple(carry)

        first = entering[lax.div(b, each), :, lanes_at(lax.rem(b, each), width)]
        lax.fori_loop(0, step_ref.shape[0] // CHUNK, body, tuple(first[:, t] for t in tiles))
        return unused

    lax.fori_loop(0, 2 * each, block, 0)


def scan_back(
    step_ref, drive_ref, dy_ref, bb_ref, cb_ref, a_ref, starts_ref, inflow, through_ref, flow_ref, db_ref,
    dc_ref, da_ref, width,
):
    tiles = tiles_of(width)
    each = inflow.shape[2] // width
    count = step_ref.shape[0] // CHUNK
    db_ref[...] = jnp.zeros_like(db_ref)
    dc_ref[...] = jnp.zeros_like(dc_ref)

    def block(b, unused):
        lanes = lanes_at(b, width)
        rates = [a_ref[:, lanes][:, t] for t in tiles]

        def body(i, carry):
            grads, d_rates = list(carry[0]), list(carry[1])
            chunk = count - 1 - i
            base = pl.multiple_of(chunk * CHUNK, CHUNK)
            step = step_ref[pl.ds(base, CHUNK), lanes]
            drive = drive_ref[pl.ds(base, CHUNK), lanes]
            dys = dy_ref[pl.ds(base, CHUNK), lanes]
            start = starts_ref[chunk, :, lanes]
            d_in, d_out = [None] * CHUNK, [None] * CHUNK
            all_through, all_flows = [], []
            for j, t in enumerate(tiles):
                current = start[:, t]
                decays, states = [], [current]
                for k in range(CHUNK):
                    decay = jnp.exp2(step[k : k + 1, t] * rates[j])
                    current = decay * current + drive[k : k + 1, t] * bb_ref[base + k]
                    decays.append(decay)
                    states.append(current)
                grad = grads[j]
                through, flows = [None] * CHUNK, [None] * CHUNK
                for k in reversed(range(CHUNK)):
                    dy = dys[k : k + 1, t]
                    grad = grad + dy * cb_ref[base + k]
                    through[k] = jnp.sum(grad * bb_ref[base + k], 0, keepdims=True)
                    piece = grad * drive[k : k + 1, t]
                    d_in[k] = piece if d_in[k] is None else d_in[k] + piece
                    piece = dy * states[k + 1]
                    d_out[k] = piece if d_out[k] is None else d_out[k] + piece
                    grad = decays[k] * grad
                    flow = grad * states[k]
                    flows[k] = jnp.sum(flow * rates[j], 0, keepdims=True)
                    d_rates[j] = d_rates[j] + flow * step[k : k + 1, t]
                grads[j] = grad
                all_through.append(jnp.concatenate(through, 0))
                all_flows.append(jnp.concatenate(flows, 0))
            through_ref[pl.ds(base, CHUNK), lanes] = jnp.concatenate(all_through, 1)
            flow_ref[pl.ds(base, CHUNK), lanes] = jnp.concatenate(all_flows, 1)
            for k in range(CHUNK):
                db_ref[base + k] += d_in[k]
                dc_ref[base + k] += d_out[k]
            return tuple(grads), tuple(d_rates)

        first = inflow[lax.div(b, each), :, lanes_at(lax.rem(b, each), width)]
        zeros = tuple(jnp.zeros((a_ref.shape[0], LANES), f32) for _ in tiles)
        d_rates = lax.fori_loop(0, count, body, (tuple(first[:, t] for t in tiles), zeros))[1]
        da_ref[:, lanes] = jnp.concatenate(d_rates, 1)
        return unused

    lax.fori_loop(0, 2 * each, block, 0)


def block_width(width, most):
    while width % most:
        most -= LANES
    return most


def shape_of(*shape, dtype=f32):
    return jax.ShapeDtypeStruct(shape, dtype)


def place_of(index, count):
    return jnp.where(
        lax.rem(index, 2) == 0, lax.div(index, 2), count - 1 - lax.div(index, 2)
    )


def index_at(place, count):
    place = lax.rem(place + 2 * count, count)
    return jnp.where(place < (count + 1) // 2, 2 * place, 2 * (count - 1 - place) + 1)


def greet(devices):
    barrier = pltpu.get_barrier_semaphore()
    for device in devices:
        pl.semaphore_signal(barrier, inc=1, device_id=device, device_id_type=MESH)
    pl.semaphore_wait(barrier, len(devices))


def remote(src, dst, send, recv, device):
    return pltpu.make_async_remote_copy(
        src_ref=src, dst_ref=dst, send_sem=send, recv_sem=recv, device_id=device,
        device_id_type=MESH,
    )


def here(count):
    section, dp, core = (lax.axis_index(name) for name in ("section", "dp", "expert"))
    place = place_of(dp, count)
    right = (section, index_at(place + 1, count), core)
    left = (section, index_at(place - 1, count), core)
    return dp, core, place, right, left, (section, dp, 1 - core)


def dp_peers(count):
    section, dp, core = (lax.axis_index(name) for name in ("section", "dp", "expert"))
    return [(section, lax.rem(dp + by, count), core) for by in range(1, count)]


def comm_params(identity, vmem=48):
    return pltpu.CompilerParams(
        collective_id=identity, has_side_effects=True, vmem_limit_bytes=vmem * MIB
    )


anywhere = pl.BlockSpec(memory_space=pl.ANY)
in_vmem = pl.BlockSpec(memory_space=pltpu.VMEM)
dma = pltpu.SemaphoreType.DMA


def gelu_parts(x):
    scale, cubic = 0.7978845608028654, 0.044715
    square = x * x
    t = jnp.tanh(scale * x * (1.0 + cubic * square))
    act = 0.5 * x * (1.0 + t)
    slope = 0.5 * (1.0 + t) + 0.5 * x * (1.0 - t * t) * scale * (1.0 + 3.0 * cubic * square)
    return act, slope


def own_expert(rows, each_rows, hidden):
    each = each_rows // CAP
    row = lax.broadcasted_iota(jnp.int32, (rows, 1), 0)
    for _ in range(rows // each_rows - 1):
        row = jnp.where(row >= each_rows, row - each_rows, row)
    column = lax.broadcasted_iota(jnp.int32, (1, hidden), 1)
    row_expert, column_expert = jnp.zeros_like(row), jnp.zeros_like(column)
    for e in range(1, each):
        row_expert = row_expert + (row >= e * CAP).astype(jnp.int32)
        column_expert = column_expert + (column >= e * (hidden // each)).astype(jnp.int32)
    return row_expert == column_expert


def mm(a, b, dims):
    return lax.dot_general(a, b, (dims, ((), ())), preferred_element_type=f32)


class Round:
    def __init__(self, count, own, held, work, part, out, scratch):
        self.own, self.held, self.work, self.part, self.out = own, held, work, part, out
        self.slots, (self.total, self.pair_in, self.pair_sems) = scratch[:4], scratch[4:7]
        self.sems, self.back_sems, self.local_sem = scratch[7:9], scratch[9:11], scratch[11]
        self.count, self.reach = count, count // 2
        self.dp, self.core, self.place, right, left, self.partner = here(count)
        self.towards = (right, left)

    def source(self, way, k):
        return index_at(self.place - k if way == 0 else self.place + k, self.count)

    def hop(self, way, k, half, src=None):
        sem = self.sems[way]
        slot = self.held.at[self.source(way, k), self.core if half == 0 else 1 - self.core]
        return remote(
            slot if src is None else src, slot, sem.at[0, k, half], sem.at[1, k, half],
            self.towards[way],
        )

    def first(self, half):
        return self.own.at[self.core] if half == 0 else None

    def swap(self):
        return remote(
            self.own.at[1 - self.core], self.held.at[self.dp, self.core], self.pair_sems.at[0, 0],
            self.pair_sems.at[1, 0], self.partner,
        )

    def keep(self):
        return pltpu.make_async_copy(
            self.own.at[self.core], self.held.at[self.dp, self.core], self.local_sem
        )

    def begin(self):
        self.swap().start()
        self.keep().start()
        for way in range(2):
            if self.reach > 1 or way == 0:
                self.hop(way, 0, 0, self.first(0)).start()

    def begin_other(self):
        self.swap().wait_recv()
        for way in range(2):
            if self.reach > 1 or way == 1:
                self.hop(way, 0, 1).start()
        self.keep().wait()

    def further(self, k):
        for half in range(2):
            for way in range(2):
                self.hop(way, k - 1, half).wait_recv()
                if half == way:
                    self.hop(way, k, half).start()
                else:

                    @pl.when(k < self.reach - 1)
                    def _(way=way, half=half):
                        self.hop(way, k, half).start()

    def arrive(self):
        for way in range(2):
            self.hop(way, self.reach - 1, way).wait_recv()

    def back(self, way, k, half):
        sem = self.back_sems[way]
        return remote(
            self.slots[way].at[k, half], self.slots[way + 2].at[k, half], sem.at[0, k, half],
            sem.at[1, k, half], self.towards[way],
        )

    def begin_back(self):
        for way in range(2):
            self.slots[way + 2][0, 1 - way] = jnp.zeros(self.slots[0].shape[2:], bf16)
            self.slots[way][0, way] = self.part[self.source(way, self.reach), way]
            self.back(way, 0, way).start()

    def nearer(self, k):
        for half in range(2):
            for way in range(2):
                owner = self.source(1 - way, self.reach - k)
                piece = self.part[owner, half].astype(f32)
                if half == way:
                    self.back(way, k - 1, half).wait_recv()
                else:

                    @pl.when(k > 1)
                    def _(way=way, half=half):
                        self.back(way, k - 1, half).wait_recv()

                before = self.slots[way + 2][k - 1, half].astype(f32)
                self.slots[way][k, half] = (piece + before).astype(bf16)
                self.back(way, k, half).start()

    def swap_back(self):
        return remote(
            self.total.at[1 - self.core], self.pair_in, self.pair_sems.at[0, 1], self.pair_sems.at[1, 1],
            self.partner,
        )

    def sum_up(self):
        for half in range(2):
            value = self.part[self.dp, half].astype(f32)
            for way in range(2):
                if self.reach > 1 or half == way:
                    self.back(way, self.reach - 1, half).wait_recv()
                    value = value + self.slots[way + 2][self.reach - 1, half].astype(f32)
            self.total[half] = value.astype(bf16)
        self.swap_back().start()

    def end(self):
        self.out[self.core] = self.total[self.core]
        self.swap_back().wait_recv()
        self.out[1 - self.core] = self.pair_in[...]
        self.swap().wait_send()
        self.swap_back().wait_send()

    def finish(self, k):
        for half in range(2):
            for way in range(2):
                if half == way:
                    self.hop(way, k, half, self.first(half)).wait_send()
                    self.back(way, k, half).wait_send()
                else:

                    @pl.when(k < self.reach - 1)
                    def _(way=way, half=half):
                        self.hop(way, k, half, self.first(half)).wait_send()

                    @pl.when(k > 0)
                    def _(way=way, half=half):
                        self.back(way, k, half).wait_send()


def go_round(rounds):
    reach = rounds[0].reach

    def steps(from_step, step):
        def body(k, unused):
            step(k)
            return unused

        lax.fori_loop(from_step, reach, body, 0)

    for one in rounds:
        one.begin()
    for one in rounds:
        one.begin_other()
    for one in rounds:
        one.work([one.dp])

    def further(k):
        for one in rounds:
            one.further(k)
        for one in rounds:
            one.work([one.source(0, k), one.source(1, k)])

    steps(1, further)
    for one in rounds:
        one.arrive()
        one.work([one.source(0, reach)])
        one.begin_back()

    def nearer(k):
        for one in rounds:
            one.nearer(k)

    steps(1, nearer)
    for one in rounds:
        one.sum_up()
    for one in rounds:
        one.end()

    def finish(k):
        for one in rounds:
            one.finish(k)

    steps(0, finish)


def rows_of(held, sources):
    pieces = [held[s].reshape(-1, held.shape[-1]) for s in sources]
    return pieces[0] if len(pieces) == 1 else jnp.concatenate(pieces, 0)


def put_rows(ref, sources, value):
    size = value.shape[0] // len(sources)
    for i, s in enumerate(sources):
        ref[s] = value[i * size : (i + 1) * size].reshape(ref.shape[1:]).astype(ref.dtype)


def block_at(section, index, count):
    index = lax.rem(index + 2 * count, 2 * count)
    return section, lax.div(index, 2), lax.rem(index, 2)


def experts_kernel(count, ahead, behind, cross, *refs):
    refs = list(refs)

    def take(number):
        taken = refs[:number]
        del refs[:number]
        return taken

    if ahead:
        own, resid, table, gate = take(4)
    if behind:
        below = take(1)[0] if cross else None
        above, table_back, gate_back, arrived_hbm = take(4)
    up_hbm, down_hbm = take(2)
    if ahead:
        out, result = take(2)
        next_rows, next_halo = take(2) if cross else (None, None)
        (arrived_out,) = take(1)
    if behind:
        upstream_out, out_back, given_out, hidden_out, slope_out = take(5)
    up, down, load_sems = take(3)
    section = lax.axis_index("section")
    dp, core, place, right, left, partner = here(count)
    block = 2 * dp + core
    across, before, after = (block_at(1 - section, block + by, count) for by in (0, -1, 1))
    greet([right, left, partner] + [across] * cross + [before] * (cross and ahead))
    loads = [
        pltpu.make_async_copy(up_hbm, up, load_sems.at[0]),
        pltpu.make_async_copy(down_hbm, down, load_sems.at[1]),
    ]
    rounds = []
    if ahead:
        held, part = take(2)
        landed, landed_halo, cross_sems = take(3) if cross else (None, None, None)
        scratch = take(12)
        (save_sem,) = take(1)

        def work(sources):
            pre = mm(rows_of(held, sources), up[...], ((1,), (0,)))
            mask = own_expert(pre.shape[0], held.shape[2], pre.shape[1])
            hidden = jnp.where(mask, gelu_parts(pre)[0], 0.0).astype(bf16)
            put_rows(part, sources, mm(hidden, down[...], ((1,), (0,))))

        rounds.append(Round(count, own, held, work, part, out, scratch))
    if behind:
        own_back, held_back, arrived, hidden_all, slope_all, part_back = take(6)
        landed_back, cross_back = take(2) if cross else (None, None)
        scratch_back = take(12)
        (back_sems,) = take(1)
        loads.append(pltpu.make_async_copy(arrived_hbm, arrived, back_sems.at[0]))

        def work_back(sources):
            pre = mm(rows_of(arrived, sources), up[...], ((1,), (0,)))
            mask = own_expert(pre.shape[0], held_back.shape[2], pre.shape[1])
            act, slope = gelu_parts(pre)
            put_rows(hidden_all, sources, jnp.where(mask, act, 0.0))
            d_hidden = mm(rows_of(held_back, sources), down[...], ((1,), (1,)))
            d_pre = jnp.where(mask, d_hidden * slope, 0.0).astype(bf16)
            put_rows(slope_all, sources, d_pre)
            put_rows(part_back, sources, mm(d_pre, up[...], ((1,), (1,))))

        rounds.append(Round(count, own_back, held_back, work_back, part_back, out_back, scratch_back))
    if behind:
        if cross:
            crossing = remote(below, landed_back, cross_back.at[0], cross_back.at[1], across)
            crossing.start()
    for load in loads:
        load.start()
    if behind:
        upstream = above[...].astype(f32)
        if cross:
            crossing.wait_recv()
            upstream = jnp.where(section == 1, upstream, landed_back[...].astype(f32))
        upstream_out[...] = upstream.astype(bf16)
        slots_grad = mm(table_back[...], (upstream * gate_back[...]).astype(bf16), ((1,), (0,)))
        own_back[...] = slots_grad.astype(bf16).reshape(own_back.shape)
    waiting = list(loads)
    for one in rounds:

        def work_first(sources, work=one.work):
            while waiting:
                waiting.pop().wait()
            work(sources)

        one.work = work_first
    go_round(rounds)
    saves = []
    if ahead:
        saves.append(pltpu.make_async_copy(held, arrived_out, save_sem))
    if behind:
        for n, (src, dst) in enumerate(
            ((held_back, given_out), (hidden_all, hidden_out), (slope_all, slope_out))
        ):
            saves.append(pltpu.make_async_copy(src, dst, back_sems.at[1 + n]))
    for save in saves:
        save.start()
    if ahead:
        returned = out[...].reshape(-1, out.shape[2])
        combined = mm(table[...], returned, ((1,), (0,))) * gate[...]
        result[...] = (resid[...] + combined).astype(bf16)
    if ahead and cross:
        length, halo = result.shape[0], next_halo.shape[0]
        copies = [
            remote(result, landed, cross_sems.at[0, 0], cross_sems.at[1, 0], across),
            remote(
                result.at[length - halo : length], landed_halo, cross_sems.at[0, 1], cross_sems.at[1, 1], after
            ),
        ]
        for copy in copies:
            copy.start()
        for copy in copies:
            copy.wait_recv()
        next_rows[...] = landed[...]
        next_halo[...] = jnp.where(block > 0, landed_halo[...].astype(f32), 0.0).astype(bf16)
        for copy in copies:
            copy.wait_send()
    if behind and cross:
        crossing.wait_send()
    for save in saves:
        save.wait()


def experts(up, down, ahead, behind, cross):
    count = lax.axis_size("dp")
    reach = count // 2
    width = (ahead[1] if ahead else behind[-4]).shape[1]
    length = (ahead[1] if ahead else behind[-4]).shape[0]
    rows = (2, EXPERTS * CAP // 2, width)
    gathered = (count,) + rows
    units = (count, 2 * rows[1], up.shape[1])
    around = (
        [pltpu.VMEM((reach,) + rows, bf16)] * 4
        + [pltpu.VMEM(rows, bf16), pltpu.VMEM(rows[1:], bf16), dma((2, 2))]
        + [dma((2, reach, 2))] * 4
        + [dma(())]
    )
    in_specs, out_specs, shapes, scratch = [], [], [], []
    if ahead:
        landing = [(length, width), (HALO, width)] if cross else []
        in_specs += [in_vmem] * 4
        out_specs += [in_vmem] * (2 + len(landing)) + [anywhere]
        shapes += [rows, (length, width)] + landing + [gathered]
        scratch += [pltpu.VMEM(gathered, bf16)] * 2 + [pltpu.VMEM(shape, bf16) for shape in landing]
        scratch += [dma((2, 2))] * cross + around + [dma(())]
    if behind:
        in_specs += [in_vmem] * (len(behind) - 1) + [anywhere]
        out_specs += [in_vmem] * 2 + [anywhere] * 3
        shapes += [(length, width), rows, gathered, units, units]
        scratch += [pltpu.VMEM(rows, bf16)] + [pltpu.VMEM(gathered, bf16)] * 2
        scratch += [pltpu.VMEM(units, bf16)] * 2 + [pltpu.VMEM(gathered, bf16)]
        scratch += [pltpu.VMEM((length, width), bf16), dma((2,))] if cross else []
        scratch += around + [dma((4,))]
    number = 7 if ahead and behind else 1 if ahead else 2
    number += 0 if cross or number == 7 else 7
    return pl.pallas_call(
        functools.partial(experts_kernel, count, bool(ahead), bool(behind), cross),
        in_specs=in_specs + [anywhere] * 2,
        out_specs=out_specs,
        out_shape=[shape_of(*shape, dtype=bf16) for shape in shapes],
        scratch_shapes=[pltpu.VMEM(up.shape, bf16), pltpu.VMEM(down.shape, bf16), dma((2,))] + scratch,
        compiler_params=comm_params(number, {2: 40, 7: 46}.get(number, 60) if count <= 8 else 60),
        name="experts_both" if number == 7 else "experts_forward" if ahead else "experts_backward",
    )(*(ahead or ()), *(behind or ()), up, down)


def grid_here(count):
    section, dp, core = (lax.axis_index(name) for name in ("section", "dp", "expert"))
    a, b = lax.div(dp, 2), lax.rem(dp, 2)
    line = count // 2

    def at(place):
        return section, 2 * lax.rem(place + line, line) + b, core

    return a, b, core, at(a + 1), at(a - 1), (section, 2 * a + 1 - b, core), (section, dp, 1 - core)


def weights_gather_kernel(count, parts, tokens, wide_up, wide_down, *refs):
    own, refs = refs[:parts], refs[parts:]
    (halos, up_out, low_down), out, refs = refs[:3], refs[3 : parts + 3], refs[parts + 3 :]
    buffer_up, buffer_down, rounded_up, rounded_down, load_sems, up_sems = refs[:6]
    after_sems, before_sems, side_sems, pair_sems, local_sems, halo_sems = refs[6:]
    a, b, core, after, before, beside, partner = grid_here(count)
    line = count // 2
    section, block = lax.axis_index("section"), 2 * (2 * a + b) + core
    greet(dp_peers(count) + [partner, block_at(section, block - 1, count)])
    micro, length = tokens.shape[:2]
    ends = [
        remote(
            tokens.at[m, length - HALO : length], halos.at[m], halo_sems.at[0, m], halo_sems.at[1, m],
            block_at(section, block + 1, count),
        )
        for m in range(micro)
    ]
    for copy in ends:
        copy.start()

    def slot(p, place, which):
        return out[p].at[core, 2 * place + which]

    def source(p, place, k):
        return own[p] if isinstance(k, int) and k == 0 else slot(p, place, b)

    def along(way, k, p):
        place = a - k if way == 0 else a + k
        sems = after_sems if way == 0 else before_sems
        return remote(
            source(p, place, k), slot(p, place, b), sems.at[0, k, p], sems.at[1, k, p],
            after if way == 0 else before,
        )

    def aside(place, k, p):
        return remote(
            source(p, place, k), slot(p, place, b), side_sems.at[0, place, p], side_sems.at[1, place, p],
            beside,
        )

    def across(place, which, k, p):
        src = source(p, place, k) if which is b else slot(p, place, which)
        number = 2 * place + which
        return remote(
            src, slot(p, place, which), pair_sems.at[0, number, p], pair_sems.at[1, number, p], partner
        )

    def has(way, k):
        return a - k >= 0 if way == 0 else a + k < line

    def goes(way):
        return a + 1 < line if way == 0 else a >= 1

    for p in range(parts):
        aside(a, 0, p).start()
        for way in range(2):

            @pl.when(goes(way))
            def _(way=way, p=p):
                along(way, 0, p).start()

    keeps = [
        pltpu.make_async_copy(own[p], slot(p, a, b), local_sems.at[p]) for p in range(parts)
    ]
    for p in range(parts):
        across(a, b, 0, p).start()
        keeps[p].start()
    loads = [
        pltpu.make_async_copy(wide_up, buffer_up, load_sems.at[0]),
        pltpu.make_async_copy(wide_down, buffer_down, load_sems.at[1]),
    ]
    save = pltpu.make_async_copy(rounded_down, low_down, load_sems.at[2])
    for load in loads:
        load.start()
    loads[0].wait()
    each, depth, hidden = wide_up.shape
    cut = hidden // count
    for piece in range(count):
        for e in range(each):
            rounded_up[piece, :, e * cut : (e + 1) * cut] = buffer_up[
                e, :, piece * cut : (piece + 1) * cut
            ].astype(bf16)
    start, end = exchange(count, rounded_up, up_out, up_sems, load_sems.at[3])
    start(0)
    start(1)
    loads[1].wait()

    def rounding(e, unused):
        rounded_down[e] = buffer_down[e].astype(bf16)
        return unused

    lax.fori_loop(0, each, rounding, 0)
    save.start()

    def came_aside(place, p):
        aside(place, None, p).wait_recv()
        across(place, 1 - b, None, p).start()

    def arrivals(k, unused):
        for p in range(parts):
            for way in range(2):

                @pl.when(has(way, k))
                def _(way=way, p=p):
                    place = a - k if way == 0 else a + k
                    along(way, k - 1, p).wait_recv()

                    @pl.when(goes(way))
                    def _():
                        along(way, k, p).start()

                    aside(place, None, p).start()
                    across(place, b, None, p).start()

        for p in range(parts):

            @pl.when(k == 1)
            def _(p=p):
                came_aside(a, p)

            for way in range(2):

                @pl.when((k > 1) & has(way, k - 1))
                def _(way=way, p=p):
                    came_aside(a - k + 1 if way == 0 else a + k - 1, p)

        return unused

    lax.fori_loop(1, line, arrivals, 0)
    for p in range(parts):
        if line == 1:
            came_aside(a, p)
        for way in range(2):

            @pl.when((line > 1) & has(way, line - 1))
            def _(way=way, p=p):
                came_aside(a - line + 1 if way == 0 else a + line - 1, p)

    for p in range(parts):
        keeps[p].wait()

    def finish(place, unused):
        for p in range(parts):
            for which in range(2):
                copy = across(place, which, None, p)
                copy.wait_recv()
                copy.wait_send()
            aside(place, None, p).wait_send()
        return unused

    lax.fori_loop(0, line, finish, 0)

    def sent(k, unused):
        for p in range(parts):
            for way in range(2):

                @pl.when(has(way, k) & goes(way))
                def _(way=way, p=p):
                    along(way, k, p).wait_send()

        return unused

    lax.fori_loop(0, line, sent, 0)
    save.wait()
    end()
    for copy in ends:
        copy.wait()


def weights_gather(tokens, up, down, own):
    count = lax.axis_size("dp")
    reach = count // 2
    parts = len(own)
    pieces = (count, up.shape[1], up.shape[0] * up.shape[2] // count)
    return pl.pallas_call(
        functools.partial(weights_gather_kernel, count, parts),
        in_specs=[anywhere] * (parts + 3),
        out_specs=[anywhere] * (parts + 3),
        out_shape=[shape_of(tokens.shape[0], HALO, tokens.shape[2], dtype=bf16)]
        + [shape_of(*pieces, dtype=bf16), shape_of(*down.shape, dtype=bf16)]
        + [shape_of(2, count, *part.shape, dtype=part.dtype) for part in own],
        scratch_shapes=[
            pltpu.VMEM(up.shape, f32),
            pltpu.VMEM(down.shape, f32),
            pltpu.VMEM(pieces, bf16),
            pltpu.VMEM(down.shape, bf16),
            dma((4,)),
            dma((2, count - 1)),
            dma((2, reach, parts)),
            dma((2, reach, parts)),
            dma((2, reach, parts)),
            dma((2, count, parts)),
            dma((parts,)),
            dma((2, tokens.shape[0])),
        ],
        compiler_params=comm_params(3),
        name="weights_gather",
    )(tokens, up, down, *own)


def grads_reduce_kernel(count, micro, vec, pieces, *refs):
    refs = list(refs)

    def take(number):
        taken = refs[:number]
        del refs[:number]
        return taken

    given = [take(8) for _ in range(micro)]
    (up_out,), out = take(1), take(4)
    wholes, halves, (vecs, landed) = take(4), take(5), take(2)
    part, sides, ins = take(4), take(4), (take(4), take(4))
    whole_sems, half_sems, vec_sems, after_sems, before_sems, side_sems, piece_sems, local_sem = refs
    a, b, core, after, before, beside, partner = grid_here(count)
    line = count // 2
    parts = len(part)
    half = halves[0].shape[1]
    length = given[0][0].shape[0]
    greet_all(count)

    def lanes(side, begin):
        return pl.ds(pl.multiple_of(begin + side * half, LANES), half)

    def moves_of(i, n, which):
        place, there = pl.ds(i * length, length), pl.ds((micro + i) * length, length)
        if n < 4:
            src, dst = given[i][n], wholes[n]
            if which == 0:
                return pltpu.make_async_copy(src, dst.at[place], whole_sems.at[2, i, n])
            return remote(src, dst.at[there], whole_sems.at[0, i, n], whole_sems.at[1, i, n], partner)
        n -= 4
        src, begin = (given[i][4], n * 2 * half) if n < 2 else (given[i][3 + n], 0)
        dst = halves[n]
        if which == 0:
            return pltpu.make_async_copy(
                src.at[:, lanes(core, begin)], dst.at[place], half_sems.at[2, i, n]
            )
        return remote(
            src.at[:, lanes(1 - core, begin)], dst.at[there], half_sems.at[0, i, n], half_sems.at[1, i, n],
            partner,
        )

    order = (0, 4, 5, 1, 6, 2, 7, 3, 8)
    for n in order:
        for i in range(micro):
            for which in range(2):
                moves_of(i, n, which).start()
    vec_copies = (
        pltpu.make_async_copy(vec.at[core], vecs.at[0], vec_sems.at[2]),
        remote(vec.at[1 - core], vecs.at[1], vec_sems.at[0], vec_sems.at[1], partner),
    )
    for copy in vec_copies:
        copy.start()
    start, end = exchange(count, pieces, landed, piece_sems, local_sem)
    start(0)

    def ready(n):
        for i in range(micro):
            moves_of(i, n, 0).wait()
            moves_of(i, n, 1).wait_recv()

    def aside(place, p):
        return remote(
            part[p].at[2 * place + 1 - b], sides[p].at[place], side_sems.at[0, place, p],
            side_sems.at[1, place, p], beside,
        )

    def along(way, place, p):
        sems = after_sems if way == 0 else before_sems
        return remote(
            part[p].at[2 * place + b], ins[way][p].at[place], sems.at[0, place, p], sems.at[1, place, p],
            after if way == 0 else before,
        )

    def far(way, k):
        return line - 1 - k if way == 0 else k

    def put(p, value):
        share = part[p].shape[1]
        for index in range(count):
            part[p][index] = value[index * share : (index + 1) * share].astype(bf16)

        def starts(k, unused):
            for way in range(2):

                @pl.when((way == 0) | (far(0, k) != far(1, k)))
                def _(way=way):
                    aside(far(way, k), p).start()

            return unused

        lax.fori_loop(0, (line + 1) // 2, starts, 0)

    def both_lines(place, p):
        aside(place, p).wait_recv()
        return part[p][2 * place + b].astype(f32) + sides[p][place].astype(f32)

    def passing(k, p):
        for way in range(2):
            place = far(way, k)

            @pl.when(place > a if way == 0 else place < a)
            def _(way=way, place=place):
                index = 2 * place + b
                part[p][index] = both_lines(place, p).astype(bf16)

                @pl.when(a > 0 if way == 0 else a < line - 1)
                def _():
                    along(way, place, p).wait_recv()
                    value = part[p][index].astype(f32) + ins[way][p][place].astype(f32)
                    part[p][index] = value.astype(bf16)

                along(way, place, p).start()

    over = ((0,), (0,))
    ready(0)
    ready(4)
    put(0, mm(halves[0][...], wholes[0][...], over))
    ready(5)
    put(1, mm(halves[1][...], wholes[0][...], over))
    ready(1)
    ready(6)
    put(2, mm(halves[2][...], wholes[1][...], over))
    start(1)
    for n in (2, 7, 3, 8):
        ready(n)
    vec_copies[0].wait()
    vec_copies[1].wait_recv()
    put(
        3,
        jnp.concatenate(
            [
                mm(halves[3][...], wholes[2][...], over),
                mm(halves[4][...], wholes[3][...], over),
            ],
            1,
        )
        + vecs[0].astype(f32)
        + vecs[1].astype(f32),
    )
    for p in range(parts):

        def passing_on(k, unused, p=p):
            passing(k, p)
            return unused

        lax.fori_loop(0, line - 1, passing_on, 0)
    for p in range(parts):
        out[p][...] = both_lines(a, p)
        for way in range(2):

            @pl.when(a > 0 if way == 0 else a < line - 1)
            def _(way=way, p=p):
                along(way, a, p).wait_recv()
                out[p][...] = out[p][...] + ins[way][p][a].astype(f32)

    def finish(place, unused):
        for p in range(parts):
            aside(place, p).wait_send()
            for way in range(2):

                @pl.when(place > a if way == 0 else place < a)
                def _(way=way, p=p):
                    along(way, place, p).wait_send()

        return unused

    lax.fori_loop(0, line, finish, 0)
    for n in order:
        for i in range(micro):
            moves_of(i, n, 1).wait_send()
    vec_copies[1].wait_send()
    end()
    each, depth, hidden = up_out.shape
    cut = hidden // count
    for piece in range(count):
        for e in range(each):
            up_out[e, :, piece * cut : (piece + 1) * cut] = landed[
                piece, :, e * cut : (e + 1) * cut
            ]


def grads_reduce(vec, pieces, given):
    count = lax.axis_size("dp")
    line = count // 2
    micro = len(given)
    length, model = given[0][0].shape
    half, lanes = vec.shape[1:]
    share = half // count
    each = EXPERTS // 2
    rows = 2 * micro * length
    shares = [(share, model)] * 3 + [(share, lanes)]
    wholes = [value.shape[1] for value in given[0][:4]]
    return pl.pallas_call(
        functools.partial(grads_reduce_kernel, count, micro),
        in_specs=[anywhere] * (2 + 8 * micro),
        out_specs=[in_vmem] * 5,
        out_shape=[shape_of(each, pieces.shape[1], count * pieces.shape[2] // each, dtype=bf16)]
        + [shape_of(*shape) for shape in shares],
        scratch_shapes=[pltpu.VMEM((rows, width), bf16) for width in wholes]
        + [pltpu.VMEM((rows, half), bf16)] * 5
        + [pltpu.VMEM((2, half, lanes), bf16), pltpu.VMEM(pieces.shape, bf16)]
        + [pltpu.VMEM((count,) + shape, bf16) for shape in shares]
        + [pltpu.VMEM((line,) + shape, bf16) for shape in shares] * 3
        + [dma((3, micro, 4)), dma((3, micro, 5)), dma((3,))]
        + [dma((2, line, 4))] * 3
        + [dma((2, count - 1)), dma(())],
        compiler_params=comm_params(4, 60),
        name="grads_reduce",
    )(vec, pieces, *[value for one in given for value in one])


def join(
    count, forward, state_ref, total_ref, rates, out_ref, other_state, other_total, mine, mine_total, states,
    totals, back, back_in, pair_sems, sems,
):
    section, dp, core = (lax.axis_index(name) for name in ("section", "dp", "expert"))
    partner = (section, dp, 1 - core)
    swap = [
        remote(state_ref.at[1 - core], other_state, pair_sems.at[0, 0], pair_sems.at[1, 0], partner),
        remote(total_ref.at[1 - core], other_total, pair_sems.at[0, 1], pair_sems.at[1, 1], partner),
    ]
    for copy in swap:
        copy.start()
    own_state, own_total = state_ref[core], total_ref[core]
    for copy in swap:
        copy.wait_recv()
    leads = core == (0 if forward else 1)
    first_state = jnp.where(leads, own_state, other_state[...])
    first_total = jnp.where(leads, own_total, other_total[...])
    second_state = jnp.where(leads, other_state[...], own_state)
    second_total = jnp.where(leads, other_total[...], own_total)
    mine[...] = (jnp.exp2(rates * second_total) * first_state + second_state).astype(bf16)
    mine_total[...] = first_total + second_total
    copies = []
    for d, peer in enumerate(dp_peers(count)):
        for n, (src, dst) in enumerate(((mine, states), (mine_total, totals))):
            copy = remote(src, dst.at[dp], sems.at[0, d, n], sems.at[1, d, n], peer)
            copy.start()
            copies.append(copy)
    states[dp] = mine[...]
    totals[dp] = mine_total[...]
    for copy in copies:
        copy.wait_recv()

    entering = jnp.zeros_like(own_state)
    for k in range(count):
        source = k if forward else count - 1 - k
        reached = (source < dp) if forward else (source > dp)
        fresh = jnp.exp2(rates * totals[source]) * entering + states[source].astype(f32)
        entering = jnp.where(reached, fresh, entering)
    after = jnp.exp2(rates * first_total) * entering + first_state
    back[...] = jnp.where(leads, after, entering)
    swap_back = remote(back, back_in, pair_sems.at[0, 2], pair_sems.at[1, 2], partner)
    swap_back.start()
    out_ref[core] = jnp.where(leads, entering, after)
    swap_back.wait_recv()
    out_ref[1 - core] = back_in[...]
    for copy in swap + copies + [swap_back]:
        copy.wait_send()


def join_scratch(count, states, half):
    one, sums = pltpu.VMEM((states, half), f32), pltpu.VMEM((1, half), f32)
    return [
        pltpu.VMEM((2, states, half), f32),
        pltpu.VMEM((2, 1, half), f32),
        pltpu.VMEM((2, states, half), f32),
        one,
        sums,
        pltpu.VMEM((states, half), bf16),
        sums,
        pltpu.VMEM((count, states, half), bf16),
        pltpu.VMEM((count, 1, half), f32),
        one,
        one,
        dma((2, 3)),
        dma((2, count - 1, 2)),
    ]


def own_lanes(a_ref, half):
    return a_ref[:, lanes_at(lax.axis_index("expert"), half)]


def greet_all(count):
    section, dp, core = (lax.axis_index(name) for name in ("section", "dp", "expert"))
    greet(dp_peers(count) + [(section, dp, 1 - core)])


def exchange(count, pieces_ref, out_ref, sems, local_sem):
    dp = lax.axis_index("dp")
    keep = pltpu.make_async_copy(pieces_ref.at[dp], out_ref.at[dp], local_sem)
    keep.start()
    copies = []
    for by, peer in enumerate(dp_peers(count)):
        copies.append(
            remote(pieces_ref.at[peer[1]], out_ref.at[dp], sems.at[0, by], sems.at[1, by], peer)
        )

    def start(beside):
        for copy in copies[1 - beside :: 2]:
            copy.start()

    def end():
        keep.wait()
        for copy in copies:
            copy.wait()

    return start, end


def mixer_forward_kernel(
    count, step_ref, drive_ref, bb_ref, cb_ref, a_ref, y_ref, starts_ref, state, total, entering, *rest
):
    half = state.shape[2]
    width = block_width(half, 384)
    scan_final(step_ref, drive_ref, bb_ref, a_ref, state, total, width)
    greet_all(count)
    join(count, True, state, total, own_lanes(a_ref, half), entering, *rest)
    scan_outputs(step_ref, drive_ref, bb_ref, cb_ref, a_ref, entering, y_ref, starts_ref, width)


def mixer_forward(step, drive, in_map, out_map, rates):
    count = lax.axis_size("dp")
    (length, width), states = step.shape, rates.shape[0]
    return pl.pallas_call(
        functools.partial(mixer_forward_kernel, count),
        in_specs=[in_vmem] * 5,
        out_specs=[in_vmem] * 2,
        out_shape=[shape_of(length, width), shape_of(length // CHUNK, states, width)],
        scratch_shapes=join_scratch(count, states, width // 2),
        compiler_params=comm_params(5),
        name="mixer_forward",
    )(step, drive, in_map, out_map, rates)


def mixer_backward_kernel(
    count, step_ref, drive_ref, dy_ref, bb_ref, cb_ref, a_ref, starts_ref, through_ref, flow_ref, db_ref, dc_ref,
    da_ref, state, total, inflow, *rest,
):
    half = state.shape[2]
    width = block_width(half, 384)
    scan_leak(step_ref, dy_ref, cb_ref, a_ref, state, total, width)
    greet_all(count)
    join(count, False, state, total, own_lanes(a_ref, half), inflow, *rest)
    scan_back(
        step_ref, drive_ref, dy_ref, bb_ref, cb_ref, a_ref, starts_ref, inflow, through_ref, flow_ref, db_ref,
        dc_ref, da_ref, width,
    )


def mixer_backward(step, drive, dy, in_map, out_map, rates, starts):
    count = lax.axis_size("dp")
    (length, width), states = step.shape, rates.shape[0]
    wide, maps = shape_of(length, width), shape_of(*in_map.shape)
    return pl.pallas_call(
        functools.partial(mixer_backward_kernel, count),
        in_specs=[in_vmem] * 7,
        out_specs=[in_vmem] * 5,
        out_shape=[wide, wide, maps, maps, shape_of(states, width)],
        scratch_shapes=join_scratch(count, states, width // 2),
        compiler_params=comm_params(6),
        name="mixer_backward",
    )(step, drive, dy, in_map, out_map, rates, starts)


def dot(a, b, dims, dtype=f32):
    return lax.dot_general(a, b, (dims, ((), ())), preferred_element_type=f32).astype(dtype)


def nn(a, b, dtype=f32):
    return dot(a, b, ((1,), (0,)), dtype)


def nt(a, b, dtype=f32):
    return dot(a, b, ((1,), (1,)), dtype)


def tn(a, b, dtype=f32):
    return dot(a, b, ((0,), (0,)), dtype)


def normalize(values, gain):
    return values * lax.rsqrt(jnp.mean(values * values, axis=-1, keepdims=True) + epsilon) * gain


def sums(value):
    return jnp.sum(value, 0)


def normalize_back(values, gain, upstream):
    scale = lax.rsqrt(jnp.mean(values * values, axis=-1, keepdims=True) + epsilon)
    unit = values * scale
    inner = upstream * gain
    d_values = scale * (inner - unit * jnp.mean(inner * unit, axis=-1, keepdims=True))
    return d_values, sums(upstream * unit)


def from_behind(shard, axis, by):
    count = 1
    for name in (axis,) if isinstance(axis, str) else axis:
        count *= lax.axis_size(name)
    pairs = [(i, i + by) for i in range(count) if 0 <= i + by < count]
    return lax.ppermute(shard, axis, pairs)


def swap_pair(value):
    return lax.ppermute(value, "expert", [(0, 1), (1, 0)])


def spread(values):
    return jnp.broadcast_to(values[:, :, None], values.shape + (LANES,))


def routing(resid, moe_gain, router, chosen, placed, dropped):
    normed = normalize(resid, moe_gain)
    probs = jax.nn.softmax(jnp.dot(normed, router, precision=highest), axis=-1)
    keep = (1 - dropped).astype(f32)
    pick = (chosen[:, None] == jnp.arange(EXPERTS)[None]).astype(f32)
    gate = jnp.sum(probs * pick, -1) * keep
    flat = chosen * CAP + placed
    table = ((flat[:, None] == jnp.arange(EXPERTS * CAP)[None]) & (dropped[:, None] == 0)).astype(
        bf16
    )
    return normed, probs, pick, keep, gate, table


def by_core(buffer):
    return buffer.reshape(2, -1, buffer.shape[1])


def mixed(xz, weights):
    width = weights["w_out"].shape[0]
    taps = weights["conv_w"].shape[0]
    length = xz.shape[0] - HALO
    padded = xz[HALO - taps + 1 :, :width]
    summed = weights["conv_b"]
    for tap in range(taps):
        summed = summed + weights["conv_w"][tap : tap + 1] * padded[tap : tap + length]
    return padded, summed, xz[HALO:, width:]


def selective(projected, weights):
    rank = weights["rank"]
    states = weights["rates"].shape[0]
    dt_low = jnp.where(jnp.arange(projected.shape[1])[None] < rank, projected, 0.0).astype(bf16)
    dt_raw = nn(dt_low, weights["dt_proj"]) + weights["dt_bias"]
    in_map = projected[:, rank : rank + states]
    out_map = projected[:, rank + states : rank + 2 * states]
    return dt_low, dt_raw, jax.nn.softplus(dt_raw), spread(in_map), spread(out_map)


def forward(rows, halo, chosen, placed, dropped, weights):
    inputs = jnp.concatenate([halo, rows], 0).astype(f32)
    normed = normalize(inputs, weights["norm_gain"]).astype(bf16)
    xz = nt(normed, weights["w_in"])
    padded, summed, gate_in = mixed(xz, weights)
    signal = jax.nn.silu(summed).astype(bf16)
    projected = nn(signal, weights["x_proj"])
    dt_low, dt_raw, step, in_map, out_map = selective(projected, weights)
    wide = signal.astype(f32)
    drive = step * wide
    rates = weights["rates"] * LOG2E
    scanned, starts = mixer_forward(step, drive, in_map, out_map, rates)
    gated = ((scanned + weights["skip"] * wide) * jax.nn.silu(gate_in)).astype(bf16)
    resid = rows.astype(f32) + nn(gated, weights["w_out"])
    normed_moe, probs, pick, keep, gate, table = routing(
        resid, weights["moe_gain"], weights["router"], chosen, placed, dropped
    )
    buffer = tn(table, normed_moe.astype(bf16), bf16)
    ahead = (by_core(buffer), resid, table, gate[:, None])
    kept = dict(
        rows=rows, halo=halo, xz=xz, projected=projected, scanned=scanned, starts=starts, resid=resid,
    )
    return ahead, kept


def backward_routing(kept, chosen, placed, dropped, weights):
    return routing(
        kept["resid"], weights["moe_gain"], weights["router"], chosen, placed, dropped
    )


def backward_experts(routed, returned, upstream, d_sent, weights):
    normed_moe, probs, pick, keep, gate, table = routed
    d_sent = d_sent.reshape(-1, d_sent.shape[2])
    returned = returned.reshape(d_sent.shape)
    upstream = upstream.astype(f32)
    d_gate = jnp.sum(upstream * nn(table, returned), -1)
    d_choice = d_gate[:, None] * pick * keep[:, None]
    d_logits = probs * (d_choice - jnp.sum(probs * d_choice, -1, keepdims=True))
    d_normed = nn(table, d_sent) + jnp.dot(d_logits, weights["router"].T, precision=highest)
    return upstream, d_normed, d_logits


def backward_mixer(upstream, kept, d_normed, d_logits, weights):
    resid = kept["resid"]
    normed_moe = normalize(resid, weights["moe_gain"])
    grad_router = lax.dot_general(
        normed_moe, d_logits, (((0,), (0,)), ((), ())), precision=highest
    )
    d_norm, grad_moe = normalize_back(resid, weights["moe_gain"], d_normed)
    d_resid = upstream + d_norm

    inputs = kept["rows"].astype(f32)
    normed = normalize(inputs, weights["norm_gain"]).astype(bf16)
    xz = kept["xz"]
    padded, summed, gate_in = mixed(xz, weights)
    signal_act, signal_back = jax.vjp(jax.nn.silu, summed)
    signal = signal_act.astype(bf16)
    wide = signal.astype(f32)
    dt_low, dt_raw, step, in_map, out_map = selective(kept["projected"], weights)
    drive = step * wide
    rates = weights["rates"] * LOG2E
    skip = weights["skip"]
    total_out = kept["scanned"] + skip * wide
    gate_act, gate_back = jax.vjp(jax.nn.silu, gate_in)
    gated = (total_out * gate_act).astype(bf16)
    d_mixer = d_resid.astype(bf16)
    d_gated = nt(d_mixer, weights["w_out"])
    d_total = d_gated * gate_act
    d_gate_in = gate_back(d_gated * total_out)[0]
    grad_skip = sums(d_total * wide)
    through, flow, d_in_map, d_out_map, d_rates = mixer_backward(
        step, drive, d_total, in_map, out_map, rates, kept["starts"]
    )
    d_step = flow / LOG2E + through * wide
    d_signal = step * through + d_total * skip
    d_raw = d_step * jax.nn.sigmoid(dt_raw)
    grad_dt_bias = sums(d_raw)
    d_raw_low = d_raw.astype(bf16)
    d_low = nt(d_raw_low, weights["dt_proj"])
    rank, states = weights["rank"], weights["rates"].shape[0]
    d_maps = jnp.concatenate([jnp.sum(d_in_map, -1), jnp.sum(d_out_map, -1)], 1)
    d_maps = jnp.pad(d_maps, ((0, 0), (rank, d_low.shape[1] - rank - 2 * states)))
    d_projected = (d_low + d_maps).astype(bf16)
    d_signal = d_signal + nt(d_projected, weights["x_proj"])
    d_summed = signal_back(d_signal)[0]
    taps = weights["conv_w"].shape[0]
    length = d_summed.shape[0]
    ahead = from_behind(d_summed[:8], ("dp", "expert"), -1)
    extended = jnp.concatenate([d_summed, ahead], 0)
    d_conv_in = jnp.zeros_like(d_summed)
    for tap in range(taps):
        begin = taps - 1 - tap
        d_conv_in = d_conv_in + weights["conv_w"][tap : tap + 1] * extended[begin : begin + length]
    grad_conv = [
        sums(d_summed * padded[tap : tap + length]) for tap in range(taps)
    ]
    d_xz = jnp.concatenate([d_conv_in, d_gate_in], 1).astype(bf16)
    d_normed_in = nn(d_xz, weights["w_in"])
    d_inputs, grad_norm = normalize_back(inputs, weights["norm_gain"], d_normed_in)
    result = (d_resid + d_inputs).astype(bf16)
    given = (
        normed,
        d_mixer,
        d_projected,
        dt_low,
        d_xz,
        gated,
        signal,
        d_raw_low,
    )
    vectors = (
        grad_conv + [sums(d_summed), grad_dt_bias, grad_skip], d_rates * weights["rates"],
        [grad_norm, grad_moe], grad_router,
    )
    return result, given, vectors


def gather_weights(
    tokens, norm_gain, w_in, conv_w, conv_b, x_proj, dt_proj, dt_bias, a_log, skip, w_out, moe_gain, router,
    w_up, w_down,
):
    count = lax.axis_size("dp")
    share = x_proj.shape[1]
    model = w_out.shape[2]
    low_in = jnp.transpose(w_in[0].astype(bf16), (1, 2, 0))
    pieces = [
        x_proj[0], dt_proj[0].T, conv_w[0].T, conv_b[0][:, None], dt_bias[0][:, None],
        skip[0][:, None], a_log[0].T, norm_gain[0][:, None], moe_gain[0][:, None], router[0],
    ]
    sizes = [piece.shape[1] for piece in pieces]
    lead = -(-sizes[0] // LANES) * LANES
    begins = [0] + [lead + sum(sizes[1:n]) for n in range(1, len(sizes))]
    places = list(zip(begins, sizes, strict=True))
    pieces.insert(1, jnp.zeros((share, lead - sizes[0]), f32))
    pad = (-sum(sizes[1:])) % LANES
    small = jnp.concatenate(pieces + [jnp.zeros((share, pad), f32)], 1).astype(bf16)
    halos, up, low_down, in_x, in_z, out, small = weights_gather(
        tokens, w_up[0], w_down[0], [low_in[0], low_in[1], w_out[0].astype(bf16), small]
    )
    width = 2 * count * share
    w_in_all = jnp.concatenate([in_x.reshape(width, model), in_z.reshape(width, model)], 0)
    table = small.reshape(width, -1)
    rows = table.astype(f32).T
    found = [rows[begin : begin + size] for begin, size in places]
    unused, dt_proj, conv_w, conv_b, dt_bias, a_skip, a_log, norm_gain, moe_gain, router = found
    weights = dict(
        rank=sizes[1],
        w_in=w_in_all,
        w_out=out.reshape(width, model),
        x_proj=table[:, :lead],
        dt_proj=jnp.pad(dt_proj, ((0, lead - sizes[1]), (0, 0))).astype(bf16),
        conv_w=conv_w,
        conv_b=conv_b,
        dt_bias=dt_bias,
        skip=a_skip,
        rates=-jnp.exp(a_log),
        norm_gain=norm_gain[:, :model],
        moe_gain=moe_gain[:, :model],
        router=router[:, :model].T,
        w_up=up.reshape(-1, up.shape[2]),
        w_down=low_down.reshape(-1, model),
    )
    return weights, places, halos


def mixer_grads(given, vectors, places, up, count):
    channel, d_rates, feature, grad_router = vectors
    feature = jnp.concatenate([piece[None] for piece in feature] + [grad_router.T], 0)
    rows = jnp.concatenate(
        [piece[None] for piece in channel] + [d_rates, jnp.concatenate([feature, feature], 1)], 0
    )
    begin = places[2][0]
    lanes = -(-sum(places[-1]) // LANES) * LANES
    vec = jnp.pad(rows.T.astype(bf16), ((0, 0), (begin, lanes - begin - rows.shape[0])))
    vec = vec.reshape(2, -1, lanes)
    up, grad_x, grad_z, grad_out, small = grads_reduce(vec, up, given)
    found = [small[:, begin : begin + size] for begin, size in places]
    x_proj, dt_proj, conv_w, conv_b, dt_bias, skip, a_log, norm_gain, moe_gain, router = found
    return (
        norm_gain[:, 0],
        jnp.transpose(jnp.stack([grad_x, grad_z], 0), (2, 0, 1)),
        conv_w.T,
        conv_b[:, 0],
        x_proj,
        dt_proj.T,
        dt_bias[:, 0],
        a_log.T,
        skip[:, 0],
        grad_out,
        moe_gain[:, 0],
        router,
        up.astype(f32),
    )


def rows_flat(value):
    return value.reshape(-1, value.shape[-1])


def down_grad(first, second):
    hidden, d_produced = (
        jnp.concatenate([rows_flat(a), rows_flat(b)], 0)
        for a, b in zip(first, second, strict=True)
    )
    return tn(hidden, d_produced).reshape(EXPERTS // 2, -1, d_produced.shape[1])


def up_pieces(first, second, count):
    arrived, d_pre = (
        jnp.concatenate([rows_flat(a), rows_flat(b)], 0)
        for a, b in zip(first, second, strict=True)
    )
    return tn(arrived, d_pre, bf16).reshape(count, arrived.shape[1] // count, -1)


def shards(
    tokens, cotangent, routes, slots, drops, norm_gain, w_in, conv_w, conv_b, x_proj, dt_proj, dt_bias,
    a_log, skip, w_out, moe_gain, router, w_up, w_down,
):
    count = lax.axis_size("dp")
    section = lax.axis_index("section")
    top = section == 1
    weights, places, halos = gather_weights(
        tokens, norm_gain, w_in, conv_w, conv_b, x_proj, dt_proj, dt_bias, a_log, skip, w_out, moe_gain,
        router, w_up, w_down,
    )
    micro = tokens.shape[0]
    blocks = ("dp", "expert")
    steps = micro + 1

    def pick(which):
        return [lax.dynamic_index_in_dim(v[0], which, 0, False) for v in (routes, slots, drops)]

    begins = (lax.axis_index("dp") == 0) & (lax.axis_index("expert") == 0)
    halos = jnp.where(begins, jnp.zeros_like(halos), halos)
    incoming, incoming_halo = jnp.zeros_like(tokens[0]), jnp.zeros_like(halos[0])
    results, bank, grads, found, last = [], [], [], [], []
    below = None

    def micro_of(step, first):
        return jnp.clip(step - first, 0, micro - 1)

    def back_parts(step):
        if step == 1:
            kept = jax.tree.map(lambda a, b: jnp.where(top, a, b), bank[2], bank[0])
        else:
            kept = bank[1]
        routed = backward_routing(kept, *pick(micro_of(step, 1 - section)), weights)
        above = cotangent[step] if step < micro else jnp.zeros_like(cotangent[0])
        above = jnp.where(top, above, jnp.zeros_like(above))
        crossing = () if below is None else (below,)
        return kept, routed, crossing + (above, routed[5].T, routed[4][:, None], kept["arrived"])

    for step in range(2 * steps - 1):
        ahead = behind = None
        if step < steps:
            fresh = min(step, micro - 1)
            rows = jnp.where(top, incoming, tokens[fresh])
            halo = jnp.where(top, incoming_halo, halos[fresh])
            ahead, fresh_kept = forward(rows, halo, *pick(micro_of(step, section)), weights)
        if step >= steps - 1:
            kept, routed, behind = back_parts(step - steps + 1)
        cross = (ahead is None) != (behind is None)
        if cross or count <= 8:
            done = experts(weights["w_up"], weights["w_down"], ahead, behind, cross)
        else:
            done = experts(weights["w_up"], weights["w_down"], ahead, None, False)
            done = [*done, *experts(weights["w_up"], weights["w_down"], None, behind, False)]
        if ahead is not None:
            fresh_kept["returned"], result = done[:2]
            if cross:
                incoming, incoming_halo = done[2:4]
            number = 5 if cross else 3
            fresh_kept["arrived"] = done[number - 1]
            results.append(result)
            bank.append(fresh_kept)
            done = done[number:]
        if behind is not None:
            upstream, d_sent, d_produced, hidden, d_pre = done
            last.append((hidden, d_produced, kept["arrived"], d_pre))
            upstream, d_normed, d_logits = backward_experts(
                routed, kept["returned"], upstream, d_sent, weights
            )
            if len(last) == steps:
                one = jax.tree.map(lambda a, b: jnp.where(top, a, b), last[0], last[2])
                moving = up_pieces(one[2:], last[1][2:], count)
            below, *pieces = backward_mixer(upstream, kept, d_normed, d_logits, weights)
            grads.append(below)
            found.append(pieces)
    outputs = jnp.stack(
        [jnp.where(top, results[m + 1], results[m]) for m in range(micro)], 0
    )
    backs = jnp.stack([jnp.where(top, grads[m], grads[m + 1]) for m in range(micro)], 0)

    def valid_one(place):
        return jax.tree.map(lambda a, b: jnp.where(top, a, b), found[0][place], found[2][place])

    vectors = jax.tree.map(lambda a, b: a + b, valid_one(1), found[1][1])
    mixer = mixer_grads([valid_one(0), found[1][0]], vectors, places, moving, count)
    down = down_grad(one[:2], last[1][:2])
    return (outputs[None], backs[None]) + tuple(v[None] for v in mixer) + (down[None],)


def solution(mesh):
    both = ("dp", "expert")
    weights = (
        P("section", "dp"),
        P("section", None, None, both),
        P("section", None, both),
        P("section", both),
        P("section", both, None),
        P("section", None, both),
        P("section", both),
        P("section", None, both),
        P("section", both),
        P("section", both, None),
        P("section", "dp"),
        P("section", "dp", None),
        P("section", "expert", "dp", None),
        P("section", "expert", "dp", None),
    )
    return jax.shard_map(
        shards,
        mesh=mesh,
        in_specs=(P(None, both, None),) * 2 + (P("section", None, both),) * 3 + weights,
        out_specs=(P("section", None, both, None),) * 2 + weights,
        check_vma=False,
    )
```
